32 devices in a mesh: group: 2 (over y), dp: 4 (over z), tensor: 2 (over x), seq: 2 (over core).
Axes of the slice: x: 2, y: 2, z: 4, core: 2. Of those that a mesh axis runs over, the one named last changes fastest.
Arguments:
- queries: bfloat16 [8, 1024, 4096], P(('group', 'dp'), 'seq', 'tensor'), parts along dimension 0, may hold values from -6 to 6
- keys: bfloat16 [8, 1024, 2048], P(('group', 'dp'), 'seq', 'tensor'), parts along dimension 0, may hold values from -6 to 6
- out_grad: bfloat16 [8, 1024, 4096], P(('group', 'dp'), 'seq', 'tensor'), parts along dimension 0, may hold values from -1.2 to 1.2
- value_weight: bfloat16 [4608, 2048], P('dp', 'tensor'), may hold values from -0.09375 to 0.09375
- tenant_of: int32 [8], P('group'), parts along dimension 0, may hold values from 0 to 3
- owner_of: int32 [8], P('group'), parts along dimension 0, may hold values from 0 to 3, each once
- counts: int32 [8], P('group'), parts along dimension 0, may hold values from 1 to 16
- noise: float32 [8, 64, 4608], P(('group', 'dp'), 'seq'), parts along dimension 0, may hold values from -6 to 6
Outputs:
- tenant_update: float32 [8, 64, 4608], P(('group', 'dp'), 'seq'), parts along dimension 0
The draws below stay inside these ranges and needn't reach their ends.
There are 2 independent parts, one for each index of `group`. The reference program is written for one: setup_inputs(seed, part) draws one part's arguments, and reference() takes and returns one part's arrays. A program takes and returns all parts, laid end to end along the dimension named above; an argument that names none is the same for every part. Nothing has to cross between parts.
All inputs are finite; a program needn't handle non-finite values.
Results may differ from the reference program's by a relative error of at most 0.0035.
Values may be sent and summed in bfloat16 or wider, within the bound.
No kernel may reach another device: no remote copies, remote signals or barrier semaphores. Data moves between devices by JAX's collectives and lax.ppermute only.
A program may use at most 64 MiB of HBM per device.

```python
import math
import jax
import jax.numpy as jnp
import numpy as np
from jax import lax

D = 4608
HEADS = 32
KV_HEADS = 16
HEAD_DIM = 128
SEQ_LEN = 1024
PROMPT = 64
QD = 4096
KVD = 2048
EXAMPLES = 4
TENANTS = 4


def draw_out_grad(key, part):
    key = jax.random.fold_in(key, 7)
    scale_key = jax.random.fold_in(key, 0)
    value_key = jax.random.fold_in(key, 1)
    pick_key = jax.random.fold_in(key, 3)
    scales = jnp.exp(jax.random.uniform(scale_key, (EXAMPLES,), jnp.float32, math.log(0.0003), math.log(0.2)))
    picked = jax.random.permutation(pick_key, EXAMPLES)
    scales = scales.at[picked[0]].set(0.0005).at[picked[1]].set(0.2)
    scales = scales.reshape(EXAMPLES, 1, 1)
    base = jnp.clip(jax.random.normal(value_key, (EXAMPLES, SEQ_LEN, QD), jnp.float32), -6.0, 6.0)
    return (base * scales).astype(jnp.bfloat16)


def draw_counts(key, part):
    key = jax.random.fold_in(key, 11)
    power_key, place_key = jax.random.split(key)
    values = jnp.left_shift(jnp.ones((TENANTS,), jnp.int32), jax.random.randint(power_key, (TENANTS,), 0, 5))
    where_top = jax.random.randint(place_key, (), 0, TENANTS)
    return values.at[where_top].set(16).astype(jnp.int32)


def set_ends(entries, key, low, high):
    dims = entries.shape
    place = [jax.random.randint(jax.random.fold_in(key, axis), (), 0, dims[axis]) for axis in range(len(dims))]
    entries = entries.at[tuple(place)].set(low)
    longest = dims.index(max(dims))
    place[longest] = (place[longest] + 1) % dims[longest]
    return entries.at[tuple(place)].set(high)


def block_scale(stream_key, extent, shards, least, high):
    level, own = 1.0, jax.random.fold_in(stream_key, 6)
    for dim, parts in shards:
        heights = jnp.exp(jax.random.uniform(jax.random.fold_in(own, dim), (parts,), jnp.float32, least / len(shards), high / len(shards)))
        level = level * jnp.repeat(heights, extent[dim] // parts).reshape([-1 if axis == dim else 1 for axis in range(len(extent))])
    return level


def rank_bounds(number_of, skew):
    portions = [(1 << 20) // math.isqrt(rank ** skew) + 1 for rank in range(1, number_of + 1)]
    scale = 1 + sum(portions) // (1 << 30)
    return np.cumsum(np.array([max(1, weight // scale) for weight in portions]))


def skewed_ids(rng, extent, amount, slope):
    grid = rank_bounds(amount, slope)
    lot = jax.random.randint(jax.random.fold_in(rng, 1), extent, 0, int(grid[amount - 1]))
    rank = jnp.searchsorted(jnp.asarray(grid, jnp.int32), lot, side="right")
    return jax.random.permutation(jax.random.fold_in(rng, 2), amount)[rank].astype(jnp.int32)


def scatter_about(key, shape, width, most, cuts=(), kind=jnp.bfloat16):
    drawn = jax.random.normal(key, shape, jnp.float32) * width
    if len(cuts) > 0:
        drawn = block_scale(key, shape, cuts, -0.22, 0.18) * drawn
    return jnp.clip(drawn, min=-most, max=most).astype(kind)


def setup_inputs(seed: int = 0, part: int = 0) -> dict:
    key_list = jax.random.split(jax.random.key(seed), 9)
    part_keys = jax.random.split(jax.random.fold_in(key_list[8], part), 9)
    return {
        "queries": scatter_about(part_keys[0], (EXAMPLES, SEQ_LEN, QD), 1.0, 6.0, ((0, 4), (1, 2), (2, 2))),
        "keys": scatter_about(part_keys[1], (EXAMPLES, SEQ_LEN, KVD), 1.0, 6.0, ((0, 4), (1, 2), (2, 2))),
        "out_grad": draw_out_grad(jax.random.fold_in(jax.random.fold_in(key_list[8], part), 71), part),
        "value_weight": scatter_about(key_list[3], (D, KVD), D ** -0.5, 0.09375, ((0, 4), (1, 2))),
        "tenant_of": set_ends(skewed_ids(part_keys[4], (EXAMPLES,), TENANTS, 2), jax.random.fold_in(part_keys[4], 3), 0, TENANTS - 1).astype(jnp.int32),
        "owner_of": jax.random.permutation(part_keys[5], TENANTS).astype(jnp.int32),
        "counts": draw_counts(jax.random.fold_in(jax.random.fold_in(key_list[8], part), 71), part),
        "noise": scatter_about(part_keys[7], (TENANTS, PROMPT, D), 0.5, 6.0, ((0, 4), (1, 2)), jnp.float32),
    }


softcap = 50.0
query_scale = 144.0 ** (-0.5)

def capped(raw):
    return softcap * jnp.tanh(raw * query_scale / softcap)

def reference(queries, keys, out_grad, value_weight, tenant_of, owner_of, counts, noise):
    group_size = HEADS // KV_HEADS
    position = jnp.arange(SEQ_LEN)
    causal = position[None, :] <= position[:, None]

    def one_example(item):
        query_rows, key_rows, grad_rows = item
        query_all = query_rows.astype(jnp.float32).reshape(SEQ_LEN, KV_HEADS, group_size, HEAD_DIM)
        key_all = key_rows.astype(jnp.float32).reshape(SEQ_LEN, KV_HEADS, HEAD_DIM)
        grad_all = grad_rows.astype(jnp.float32).reshape(SEQ_LEN, KV_HEADS, group_size, HEAD_DIM)

        def one_head(head):
            query_head = query_all[:, head]
            key_head = key_all[:, head]
            grad_head = grad_all[:, head]
            raw = jnp.einsum('qgc,kc->gqk', query_head, key_head)
            weights = jnp.where(causal[None], jnp.exp(capped(raw)), 0.0)
            total = lax.optimization_barrier(jnp.sum(weights, axis=-1))
            prob = (weights[:, :, :PROMPT] / total[:, :, None]).astype(jnp.bfloat16)
            prob = lax.optimization_barrier(prob).astype(jnp.float32)
            return jnp.einsum('gqp,qgc->pc', prob, grad_head)
        value_grad = lax.map(one_head, jnp.arange(KV_HEADS))
        value_grad = jnp.transpose(value_grad, (1, 0, 2)).reshape(PROMPT, KVD).astype(jnp.bfloat16)
        return jnp.dot(value_grad, value_weight.T, preferred_element_type=jnp.float32)
    grads = lax.map(one_example, (queries, keys, out_grad))
    norms = jnp.sqrt(lax.optimization_barrier(jnp.sum(grads * grads, axis=(1, 2))))
    clipped = grads / jnp.maximum(1.0, norms)[:, None, None]
    slots = jnp.arange(TENANTS)
    owner_hit = owner_of[None, :] == slots[:, None]
    owner_ex = lax.optimization_barrier(jnp.sum(jnp.where(tenant_of[:, None] == slots[None, :], owner_of[None, :], 0), axis=1))
    select = (owner_ex[:, None] == slots[None, :]).astype(jnp.float32)
    tenant_sum = jnp.einsum('eo,epd->opd', select, clipped, precision=lax.Precision.HIGHEST)
    count_at = lax.optimization_barrier(jnp.sum(jnp.where(owner_hit, counts[None, :], 0), axis=1)).astype(jnp.float32)
    return (math.sqrt(PROMPT * D) * tenant_sum + noise) / count_at[:, None, None]
```

```python
import functools
import math

import jax
import jax.numpy as jnp
from jax import lax
from jax.experimental import pallas as pl
from jax.experimental.pallas import tpu as pltpu
from jax.sharding import PartitionSpec as P

D = 4608
HEAD_DIM = 128
PROMPT = 64
LANES = 128

softcap = 50.0
query_scale = 144.0 ** (-0.5)
TANH_SCALE = query_scale / softcap
EXP2_SCALE = softcap * math.log2(math.e)

CONTRACT_LAST = (((1,), (1,)), ((), ()))


def xor_pairs(size, step):
    return [(i, i ^ step) for i in range(size)]


def head_value_grad(q_halves, k_halves, g_halves, out, prob):
    block = LANES
    rows = q_halves[0].shape[0]
    group = q_halves[0].shape[1] // HEAD_DIM
    key_pos = lax.broadcasted_iota(jnp.int32, (block, block), 0)
    query_pos = lax.broadcasted_iota(jnp.int32, (block, block), 1)
    keep = jnp.concatenate([key_pos <= query_pos] * group, axis=1)

    def query_block(q_ref, parts, start, column):
        q_block = jnp.concatenate(
            [q_ref[start : start + block, g * HEAD_DIM : (g + 1) * HEAD_DIM] for g in range(group)],
            axis=0,
        )
        total, prompt = None, None
        for k_ref, count, diagonal in parts:
            raw = lax.dot_general(
                k_ref[:count, :], q_block, CONTRACT_LAST, preferred_element_type=jnp.float32
            )
            for low in range(0, count, block):
                e = jnp.exp2(jnp.tanh(raw[low : low + block] * TANH_SCALE) * EXP2_SCALE)
                if diagonal and low == count - block:
                    e = jnp.where(keep, e, 0.0)
                if prompt is None:
                    prompt = e[:PROMPT]
                part = jnp.sum(e.reshape(block // 8, 8, group * block), axis=0)
                total = part if total is None else total + part
        total = jnp.sum(total, axis=0, keepdims=True)
        scaled = (prompt / total).astype(jnp.bfloat16)
        for g in range(group):
            prob[g, :, column : column + block] = scaled[:, g * block : (g + 1) * block]

    for start in range(0, rows, block):
        query_block(q_halves[0], [(k_halves[0], start + block, True)], start, start)
    for start in range(0, rows, block):
        parts = [(k_halves[0], rows, False), (k_halves[1], start + block, True)]
        query_block(q_halves[1], parts, start, rows + start)
    value = None
    for g in range(group):
        for half in range(2):
            term = jnp.dot(
                prob[g, :, half * rows : (half + 1) * rows],
                g_halves[half][:, g * HEAD_DIM : (g + 1) * HEAD_DIM],
                preferred_element_type=jnp.float32,
            )
            value = term if value is None else value + term
    value = value.astype(jnp.bfloat16)
    out[0] = value[: PROMPT // 2]
    out[1] = value[PROMPT // 2 :]


def attention_kernel(seq_ref, q_own, q_far, k_own, k_far, g_own, g_far, out, prob):
    @pl.when(seq_ref[0] == 0)
    def _():
        head_value_grad((q_own, q_far), (k_own, k_far), (g_own, g_far), out, prob)

    @pl.when(seq_ref[0] == 1)
    def _():
        head_value_grad((q_far, q_own), (k_far, k_own), (g_far, g_own), out, prob)


def prompt_value_grad(seq_index, q_own, q_far, k_own, k_far, g_own, g_far):
    rows = q_own.shape[0]
    heads = k_far.shape[1] // HEAD_DIM
    group = q_own.shape[1] // k_own.shape[1]
    width = group * HEAD_DIM
    own = lambda h, seq: (0, seq[0] * heads + h)
    far = lambda h, seq: (0, h)
    return pl.pallas_call(
        attention_kernel,
        grid_spec=pltpu.PrefetchScalarGridSpec(
            num_scalar_prefetch=1,
            grid=(heads,),
            in_specs=[
                pl.BlockSpec((rows, width), own),
                pl.BlockSpec((rows, width), far),
                pl.BlockSpec((rows, HEAD_DIM), own),
                pl.BlockSpec((rows, HEAD_DIM), far),
                pl.BlockSpec((rows, width), own),
                pl.BlockSpec((rows, width), far),
            ],
            out_specs=pl.BlockSpec((2, PROMPT // 2, HEAD_DIM), lambda h, seq: (0, 0, h)),
            scratch_shapes=[pltpu.VMEM((group, PROMPT, 2 * rows), jnp.bfloat16)],
        ),
        out_shape=jax.ShapeDtypeStruct((2, PROMPT // 2, heads * HEAD_DIM), jnp.bfloat16),
        compiler_params=pltpu.CompilerParams(vmem_limit_bytes=32 * 1024 * 1024),
        cost_estimate=pl.CostEstimate(
            flops=heads * group * 9 * rows * rows * HEAD_DIM,
            bytes_accessed=10 * rows * heads * width,
            transcendentals=heads * group * 4 * rows * rows,
        ),
    )(seq_index.reshape(1), q_own, q_far, k_own, k_far, g_own, g_far)


def grad_kernel(place, *refs, examples, columns):
    near, far = refs[:examples], refs[examples : 2 * examples]
    weight, weight_far_0, weight_far_1, grad, squares = refs[2 * examples :]
    width = grad.shape[-1]
    depth = weight.shape[1] // 2
    rows = grad.shape[1]
    start = pl.multiple_of(place[2] * (columns - width), 16)
    total = None
    for half in range(2):
        offset = pl.multiple_of((place[1] ^ half) * depth, LANES)
        own = jnp.concatenate([ref[half] for ref in near], axis=0)
        other = jnp.concatenate([ref[half] for ref in far], axis=0)
        weight_far = (weight_far_0, weight_far_1)[half]
        term = lax.dot_general(
            own,
            weight[pl.ds(start, width), pl.ds(offset, depth)],
            CONTRACT_LAST,
            preferred_element_type=jnp.float32,
        ) + lax.dot_general(
            other, weight_far[...], CONTRACT_LAST, preferred_element_type=jnp.float32
        )
        total = term if total is None else total + term
    column = lax.broadcasted_iota(jnp.int32, (1, width), 1) + place[2] * (columns - width)
    split = columns // 2
    low = place[2] * split
    counted = (column >= low) & (column < low + split)
    squares[...] = jnp.zeros_like(squares)
    for step in range(examples):
        part = total[step * rows : (step + 1) * rows]
        grad[step] = part
        sums = jnp.sum(jnp.where(counted, part * part, 0.0), axis=0, keepdims=True)
        folded = sums[:, :LANES]
        for at in range(LANES, width, LANES):
            folded = folded + sums[:, at : at + LANES]
        squares[pl.ds(place[0] ^ step, 1), :] = folded


def share_kernel(place, select, norms, near, far, *outs):
    examples, rows, width = near.shape
    rest = far.shape[2]
    outs, scales = outs[:examples], outs[examples]
    devices = norms.shape[0] // 8
    norm_sq = jnp.sum(norms[...].reshape(devices, 8, LANES), axis=0)
    norm_sq = jnp.sum(norm_sq, axis=1, keepdims=True)
    scales[...] = jnp.broadcast_to(1.0 / jnp.maximum(1.0, jnp.sqrt(norm_sq)), scales.shape)
    scale = [scales[pl.ds(place[0] ^ step, 1), :] for step in range(examples)]
    near_at = pl.multiple_of(place[2] * rest, LANES)
    far_at = pl.multiple_of((1 - place[2]) * width, LANES)
    for k in range(examples):
        factor = [scale[step] * select[k * examples + step] for step in range(examples)]
        for ref, base, extent in ((near, near_at, width), (far, far_at, rest)):
            for at in range(0, extent, LANES):
                total = None
                for step in range(examples):
                    term = ref[step, :, at : at + LANES] * factor[step]
                    total = term if total is None else total + term
                to = pl.multiple_of(base + at, LANES)
                outs[k][:, pl.ds(to, LANES)] = total.astype(jnp.bfloat16)


def update_kernel(place, count, *refs, examples):
    shares, noise, out = refs[:examples], refs[examples], refs[examples + 1]
    columns = shares[0].shape[1]
    for step in range(examples):
        at = pl.ds(pl.multiple_of((place[0] ^ step) * columns, LANES), columns)
        share = shares[step][...].astype(jnp.float32)
        out[0, :, at] = (math.sqrt(PROMPT * D) * share + noise[0, :, at]) / count[0]


VMEM = pl.BlockSpec(memory_space=pltpu.VMEM)
SMEM = pl.BlockSpec(memory_space=pltpu.SMEM)


def tail_by_permutes(value_grad, weight, weight_far, tenant_of, owner_of, counts, noise, sizes):
    dp = sizes["dp"]
    columns = weight.shape[0]
    rows = PROMPT // 2
    width = weight_far[0].shape[0]
    rest = columns - width
    dp_index, seq_index, tensor_index = (lax.axis_index(a) for a in ("dp", "seq", "tensor"))
    place = jnp.stack([dp_index, seq_index, tensor_index]).astype(jnp.int32)

    order = jnp.arange(dp) ^ dp_index
    owner_ex = jnp.sum(
        jnp.where(tenant_of[:, None] == jnp.arange(dp)[None, :], owner_of[None, :], 0), axis=1
    )
    select = (owner_ex[order][None, :] == order[:, None]).astype(jnp.float32).reshape(-1)
    my_count = jnp.sum(jnp.where(owner_of == dp_index, counts, 0)).astype(jnp.float32).reshape(1)

    near = [value_grad] + [
        lax.ppermute(value_grad, "dp", xor_pairs(dp, step)) for step in range(1, dp)
    ]
    far = [lax.ppermute(block, "tensor", xor_pairs(2, 1)) for block in near]
    grad, squares = pl.pallas_call(
        functools.partial(grad_kernel, examples=dp, columns=columns),
        in_specs=[SMEM] + [VMEM] * (2 * dp + 3),
        out_specs=[VMEM, VMEM],
        out_shape=[
            jax.ShapeDtypeStruct((dp, rows, width), jnp.float32),
            jax.ShapeDtypeStruct((8, LANES), jnp.float32),
        ],
        compiler_params=pltpu.CompilerParams(vmem_limit_bytes=32 * 1024 * 1024),
    )(place, *near, *far, weight, *weight_far)
    sent = lax.dynamic_slice_in_dim(grad, tensor_index * (width - rest), rest, axis=2)
    grad_far = lax.ppermute(sent, "tensor", xor_pairs(2, 1))
    devices = dp * sizes["tensor"] * sizes["seq"]
    norms = lax.all_to_all(
        jnp.broadcast_to(squares[None], (devices, 8, LANES)).reshape(devices * 8, LANES),
        ("dp", "tensor", "seq"),
        split_axis=0,
        concat_axis=0,
        tiled=True,
    )
    shares = pl.pallas_call(
        share_kernel,
        in_specs=[SMEM, SMEM] + [VMEM] * 3,
        out_specs=[VMEM] * dp,
        out_shape=[jax.ShapeDtypeStruct((rows, columns), jnp.bfloat16)] * dp,
        scratch_shapes=[pltpu.VMEM((8, LANES), jnp.float32)],
    )(place, select, norms, grad, grad_far)
    arrived = [shares[0]] + [
        lax.ppermute(shares[step], "dp", xor_pairs(dp, step)) for step in range(1, dp)
    ]
    return pl.pallas_call(
        functools.partial(update_kernel, examples=dp),
        in_specs=[SMEM, SMEM] + [VMEM] * (dp + 1),
        out_specs=VMEM,
        out_shape=jax.ShapeDtypeStruct(noise.shape, jnp.float32),
    )(place, my_count, *arrived, noise)


def tail_by_collectives(value_grad, weight, tenant_of, owner_of, counts, noise):
    rows = PROMPT // 2
    seq_index, dp_index = lax.axis_index("seq"), lax.axis_index("dp")
    halves = jnp.where(seq_index == 0, value_grad, value_grad[::-1])
    mine = jnp.concatenate([halves[0], halves[1]], axis=1)
    whole = lax.all_gather(mine, "tensor", axis=1, tiled=True)
    whole = lax.all_gather(whole, "dp", axis=0, tiled=True)
    part = lax.all_to_all(weight, "tensor", split_axis=0, concat_axis=1, tiled=True)
    grad = lax.dot_general(whole, part, CONTRACT_LAST, preferred_element_type=jnp.float32)
    grad = grad.reshape(-1, rows, part.shape[0])
    norm_sq = lax.psum(jnp.sum(grad * grad, axis=(1, 2)), ("dp", "tensor", "seq"))
    clipped = grad / jnp.maximum(1.0, jnp.sqrt(norm_sq))[:, None, None]
    slots = jnp.arange(owner_of.shape[0])
    owner_ex = jnp.sum(
        jnp.where(tenant_of[:, None] == slots[None, :], owner_of[None, :], 0), axis=1
    )
    select = (owner_ex[None, :] == slots[:, None]).astype(jnp.float32)
    sums = jnp.einsum("oe,erc->orc", select, clipped, precision=lax.Precision.HIGHEST)
    sums = lax.all_gather(sums, "tensor", axis=2, tiled=True)
    sums = lax.all_to_all(sums, "dp", split_axis=0, concat_axis=2, tiled=True)
    my_count = jnp.sum(jnp.where(owner_of == dp_index, counts, 0)).astype(jnp.float32)
    return (math.sqrt(PROMPT * D) * sums + noise) / my_count


def body(sizes, queries, keys, out_grad, value_weight, tenant_of, owner_of, counts, noise):
    swap = xor_pairs(2, 1)
    seq_index = lax.axis_index("seq").astype(jnp.int32)
    tensor_index = lax.axis_index("tensor")
    q, k, g = queries[0], keys[0], out_grad[0]

    def from_sibling(x):
        half = x.shape[1] // 2
        sent = lax.dynamic_slice_in_dim(x, (1 - seq_index) * half, half, axis=1)
        return lax.ppermute(sent, "seq", swap)

    k_far, q_far, g_far = from_sibling(k), from_sibling(q), from_sibling(g)

    columns = value_weight.shape[0]
    dp = sizes["dp"]
    permutes = sizes["tensor"] == 2 and columns % LANES == 0 and dp in (1, 2, 4, 8)
    if permutes:
        width = -(-columns // (2 * LANES)) * LANES
        depth = value_weight.shape[1] // 2
        sent = lax.dynamic_slice(
            value_weight,
            ((1 - tensor_index) * (columns - width), seq_index * depth),
            (width, depth),
        )
        weight_far = lax.ppermute(sent, "tensor", swap)
        weight_far = (weight_far, lax.ppermute(weight_far, "seq", swap))

    halves = prompt_value_grad(seq_index, q, q_far, k, k_far, g, g_far)
    mine = lax.dynamic_index_in_dim(halves, seq_index, 0, keepdims=False)
    theirs = lax.dynamic_index_in_dim(halves, 1 - seq_index, 0, keepdims=False)
    value_grad = jnp.stack([mine, lax.ppermute(theirs, "seq", swap)])
    if permutes:
        return tail_by_permutes(
            value_grad, value_weight, weight_far, tenant_of, owner_of, counts, noise, sizes
        )
    return tail_by_collectives(value_grad, value_weight, tenant_of, owner_of, counts, noise)


def solution(mesh):
    return jax.shard_map(
        functools.partial(body, dict(mesh.shape)),
        mesh=mesh,
        in_specs=(
            P(("group", "dp"), "seq", "tensor"),
            P(("group", "dp"), "seq", "tensor"),
            P(("group", "dp"), "seq", "tensor"),
            P("dp", "tensor"),
            P("group"),
            P("group"),
            P("group"),
            P(("group", "dp"), "seq", None),
        ),
        out_specs=P(("group", "dp"), "seq", None),
        check_vma=False,
    )
```

```python
import functools
import math

import jax
import jax.numpy as jnp
from jax import lax
from jax.experimental import pallas as pl
from jax.experimental.pallas import tpu as pltpu
from jax.sharding import PartitionSpec as P

D = 4608
HEAD_DIM = 128
PROMPT = 64
LANES = 128

softcap = 50.0
query_scale = 144.0 ** (-0.5)
TANH_SCALE = query_scale / softcap
EXP2_SCALE = softcap * math.log2(math.e)

CONTRACT_LAST = (((1,), (1,)), ((), ()))
VMEM = pl.BlockSpec(memory_space=pltpu.VMEM)
SMEM = pl.BlockSpec(memory_space=pltpu.SMEM)
HBM = pl.BlockSpec(memory_space=pltpu.HBM)
ANY = pl.BlockSpec(memory_space=pl.ANY)


def xor_pairs(size, step):
    return [(i, i ^ step) for i in range(size)]


def head_value_grad(q, k, g, prob):
    block = LANES
    rows = q.shape[1]
    group = q.shape[2] // HEAD_DIM
    key_pos = lax.broadcasted_iota(jnp.int32, (block, block), 0)
    query_pos = lax.broadcasted_iota(jnp.int32, (block, block), 1)
    keep = jnp.concatenate([key_pos <= query_pos] * group, axis=1)

    def query_block(half, parts, start, column):
        q_block = jnp.concatenate(
            [
                q[half, start : start + block, i * HEAD_DIM : (i + 1) * HEAD_DIM]
                for i in range(group)
            ],
            axis=0,
        )
        total, prompt = None, None
        for key_half, count, diagonal in parts:
            raw = lax.dot_general(
                k[key_half, :count, :], q_block, CONTRACT_LAST, preferred_element_type=jnp.float32
            )
            for low in range(0, count, block):
                e = jnp.exp2(jnp.tanh(raw[low : low + block] * TANH_SCALE) * EXP2_SCALE)
                if diagonal and low == count - block:
                    e = jnp.where(keep, e, 0.0)
                if prompt is None:
                    prompt = e[:PROMPT]
                part = jnp.sum(e.reshape(block // 8, 8, group * block), axis=0)
                total = part if total is None else total + part
        total = jnp.sum(total, axis=0, keepdims=True)
        scaled = (prompt / total).astype(jnp.bfloat16)
        for i in range(group):
            prob[i, :, column : column + block] = scaled[:, i * block : (i + 1) * block]

    for start in range(0, rows, block):
        query_block(0, [(0, start + block, True)], start, start)
    for start in range(0, rows, block):
        query_block(1, [(0, rows, False), (1, start + block, True)], start, rows + start)
    value = None
    for i in range(group):
        for half in range(2):
            term = jnp.dot(
                prob[i, :, half * rows : (half + 1) * rows],
                g[half, :, i * HEAD_DIM : (i + 1) * HEAD_DIM],
                preferred_element_type=jnp.float32,
            )
            value = term if value is None else value + term
    return value.astype(jnp.bfloat16)


def attention_kernel(place, q, k, g, q_far, k_far, g_far, out, q_all, k_all, g_all, prob, done):
    heads = q_all.shape[0]
    seq = place[1]

    def copies(h):
        pairs = []
        for own, far, buffer in ((q, q_far, q_all), (k, k_far, k_all), (g, g_far, g_all)):
            width = buffer.shape[-1]
            at = pl.multiple_of((seq * heads + h) * width, LANES)
            pairs.append((own.at[:, pl.ds(at, width)], buffer.at[h, seq]))
            at = pl.multiple_of(h * width, LANES)
            pairs.append((far.at[:, pl.ds(at, width)], buffer.at[h, 1 - seq]))
        return [
            pltpu.make_async_copy(source, target, done.at[h, i])
            for i, (source, target) in enumerate(pairs)
        ]

    for h in range(heads):
        for copy in copies(h):
            copy.start()

    def step(h, carry):
        for copy in copies(h):
            copy.wait()
        value = head_value_grad(q_all.at[h], k_all.at[h], g_all.at[h], prob)
        at = pl.ds(pl.multiple_of(h * HEAD_DIM, LANES), HEAD_DIM)
        out[0, :, at] = value[: PROMPT // 2]
        out[1, :, at] = value[PROMPT // 2 :]
        return carry

    lax.fori_loop(0, heads, step, 0)


def prompt_value_grad(place, q, k, g, q_far, k_far, g_far):
    rows = q.shape[0]
    heads = k_far.shape[1] // HEAD_DIM
    group = q.shape[1] // k.shape[1]
    width = group * HEAD_DIM
    return pl.pallas_call(
        attention_kernel,
        in_specs=[SMEM] + [HBM] * 3 + [ANY] * 3,
        out_specs=VMEM,
        out_shape=jax.ShapeDtypeStruct((2, PROMPT // 2, heads * HEAD_DIM), jnp.bfloat16),
        scratch_shapes=[
            pltpu.VMEM((heads, 2, rows, width), jnp.bfloat16),
            pltpu.VMEM((heads, 2, rows, HEAD_DIM), jnp.bfloat16),
            pltpu.VMEM((heads, 2, rows, width), jnp.bfloat16),
            pltpu.VMEM((group, PROMPT, 2 * rows), jnp.bfloat16),
            pltpu.SemaphoreType.DMA((heads, 6)),
        ],
        compiler_params=pltpu.CompilerParams(vmem_limit_bytes=56 * 1024 * 1024),
        cost_estimate=pl.CostEstimate(
            flops=heads * group * 9 * rows * rows * HEAD_DIM,
            bytes_accessed=10 * rows * heads * width,
            transcendentals=heads * group * 4 * rows * rows,
        ),
    )(place, q, k, g, q_far, k_far, g_far)


def sibling_kernel(place, *refs, starts):
    count = len(starts)
    sources, targets, buffers = refs[:count], refs[count : 2 * count], refs[2 * count : 3 * count]
    done_in, done_out = refs[3 * count :]
    loads, stores = [], []
    for i, start in enumerate(starts):
        rows, width = targets[i].shape
        row, column = start(place)
        row = row if isinstance(row, int) else pl.multiple_of(row, 16)
        window = sources[i].at[pl.ds(row, rows), pl.ds(pl.multiple_of(column, LANES), width)]
        loads.append(pltpu.make_async_copy(window, buffers[i], done_in.at[i]))
        stores.append(pltpu.make_async_copy(buffers[i], targets[i], done_out.at[i]))
    for load in loads:
        load.start()
    for load, store in zip(loads, stores):
        load.wait()
        store.start()
    for store in stores:
        store.wait()


def cut(place, arrays, starts, shapes):
    return pl.pallas_call(
        functools.partial(sibling_kernel, starts=starts),
        in_specs=[SMEM] + [HBM] * len(arrays),
        out_specs=[ANY] * len(arrays),
        out_shape=[jax.ShapeDtypeStruct(shape, jnp.bfloat16) for shape in shapes],
        scratch_shapes=[pltpu.VMEM(shape, jnp.bfloat16) for shape in shapes]
        + [pltpu.SemaphoreType.DMA((len(arrays),))] * 2,
        compiler_params=pltpu.CompilerParams(vmem_limit_bytes=60 * 1024 * 1024),
    )(place, *arrays)


def grad_kernel(place, *refs, examples, columns):
    near, far = refs[:examples], refs[examples : 2 * examples]
    weight, weight_far_0, weight_far_1, grad, squares = refs[2 * examples :]
    width = grad.shape[-1]
    depth = weight.shape[1] // 2
    rows = grad.shape[1]
    start = pl.multiple_of(place[2] * (columns - width), 16)
    total = None
    for half in range(2):
        offset = pl.multiple_of((place[1] ^ half) * depth, LANES)
        own = jnp.concatenate([ref[half] for ref in near], axis=0)
        other = jnp.concatenate([ref[half] for ref in far], axis=0)
        weight_far = (weight_far_0, weight_far_1)[half]
        term = lax.dot_general(
            own,
            weight[pl.ds(start, width), pl.ds(offset, depth)],
            CONTRACT_LAST,
            preferred_element_type=jnp.float32,
        ) + lax.dot_general(
            other, weight_far[...], CONTRACT_LAST, preferred_element_type=jnp.float32
        )
        total = term if total is None else total + term
    column = lax.broadcasted_iota(jnp.int32, (1, width), 1) + place[2] * (columns - width)
    split = columns // 2
    low = place[2] * split
    counted = (column >= low) & (column < low + split)
    example = lax.broadcasted_iota(jnp.int32, (8, LANES), 0)
    by_example = jnp.zeros((8, LANES), jnp.float32)
    for step in range(examples):
        part = total[step * rows : (step + 1) * rows]
        grad[step] = part
        sums = jnp.sum(jnp.where(counted, part * part, 0.0), axis=0, keepdims=True)
        folded = sums[:, :LANES]
        for at in range(LANES, width, LANES):
            folded = folded + sums[:, at : at + LANES]
        by_example = jnp.where(example == (place[0] ^ step), folded, by_example)
    for device in range(squares.shape[0]):
        squares[device] = by_example


def share_kernel(place, tenant_of, owner_of, norms, near, far, *outs):
    examples, rows, width = near.shape
    rest = far.shape[2]
    outs, scales = outs[:examples], outs[examples]
    norm_sq = jnp.sum(jnp.sum(norms[...], axis=0), axis=1, keepdims=True)
    scales[...] = jnp.broadcast_to(1.0 / jnp.maximum(1.0, jnp.sqrt(norm_sq)), scales.shape)
    scale = [scales[pl.ds(place[0] ^ step, 1), :] for step in range(examples)]
    owner = [owner_of[tenant_of[place[0] ^ step]] for step in range(examples)]
    near_at = pl.multiple_of(place[2] * rest, LANES)
    far_at = pl.multiple_of((1 - place[2]) * width, LANES)
    for k in range(examples):
        factor = [
            scale[step] * (owner[step] == (place[0] ^ k)).astype(jnp.float32)
            for step in range(examples)
        ]
        for ref, base, extent in ((near, near_at, width), (far, far_at, rest)):
            for at in range(0, extent, LANES):
                total = None
                for step in range(examples):
                    term = ref[step, :, at : at + LANES] * factor[step]
                    total = term if total is None else total + term
                to = pl.multiple_of(base + at, LANES)
                outs[k][:, pl.ds(to, LANES)] = total.astype(jnp.bfloat16)


def update_kernel(place, owner_of, counts, *refs, examples):
    shares, noise, out = refs[:examples], refs[examples], refs[examples + 1]
    columns = shares[0].shape[1]
    count = 0
    for slot in range(owner_of.shape[0]):
        count = count + jnp.where(owner_of[slot] == place[0], counts[slot], 0)
    count = count.astype(jnp.float32)
    for step in range(examples):
        at = pl.ds(pl.multiple_of((place[0] ^ step) * columns, LANES), columns)
        share = shares[step][...].astype(jnp.float32)
        out[0, :, at] = (math.sqrt(PROMPT * D) * share + noise[0, :, at]) / count


def tail_by_permutes(
    place, value_grad, weight, weight_far, tenant_of, owner_of, counts, noise, sizes
):
    dp = sizes["dp"]
    columns = weight.shape[0]
    rows = PROMPT // 2
    width = weight_far[0].shape[0]
    rest = columns - width
    near = [value_grad] + [
        lax.ppermute(value_grad, "dp", xor_pairs(dp, step)) for step in range(1, dp)
    ]
    far = [lax.ppermute(block, "tensor", xor_pairs(2, 1)) for block in near]
    devices = dp * sizes["tensor"] * sizes["seq"]
    grad, squares = pl.pallas_call(
        functools.partial(grad_kernel, examples=dp, columns=columns),
        in_specs=[SMEM] + [VMEM] * (2 * dp + 3),
        out_specs=[VMEM, VMEM],
        out_shape=[
            jax.ShapeDtypeStruct((dp, rows, width), jnp.float32),
            jax.ShapeDtypeStruct((devices, 8, LANES), jnp.float32),
        ],
        compiler_params=pltpu.CompilerParams(vmem_limit_bytes=24 * 1024 * 1024),
    )(place, *near, *far, weight, *weight_far)
    sent = lax.dynamic_slice_in_dim(grad, place[2] * (width - rest), rest, axis=2)
    grad_far = lax.ppermute(sent, "tensor", xor_pairs(2, 1))
    norms = lax.all_to_all(
        squares, ("dp", "tensor", "seq"), split_axis=0, concat_axis=0, tiled=True
    )
    shares = pl.pallas_call(
        share_kernel,
        in_specs=[SMEM] * 3 + [VMEM] * 3,
        out_specs=[VMEM] * dp,
        out_shape=[jax.ShapeDtypeStruct((rows, columns), jnp.bfloat16)] * dp,
        scratch_shapes=[pltpu.VMEM((8, LANES), jnp.float32)],
        compiler_params=pltpu.CompilerParams(vmem_limit_bytes=16 * 1024 * 1024),
    )(place, tenant_of, owner_of, norms, grad, grad_far)
    arrived = [shares[0]] + [
        lax.ppermute(shares[step], "dp", xor_pairs(dp, step)) for step in range(1, dp)
    ]
    return pl.pallas_call(
        functools.partial(update_kernel, examples=dp),
        in_specs=[SMEM] * 3 + [VMEM] * (dp + 1),
        out_specs=VMEM,
        out_shape=jax.ShapeDtypeStruct(noise.shape, jnp.float32),
        compiler_params=pltpu.CompilerParams(vmem_limit_bytes=16 * 1024 * 1024),
    )(place, owner_of, counts, *arrived, noise)


def tail_by_collectives(value_grad, weight, tenant_of, owner_of, counts, noise):
    rows = PROMPT // 2
    seq_index, dp_index = lax.axis_index("seq"), lax.axis_index("dp")
    halves = jnp.where(seq_index == 0, value_grad, value_grad[::-1])
    mine = jnp.concatenate([halves[0], halves[1]], axis=1)
    whole = lax.all_gather(mine, "tensor", axis=1, tiled=True)
    whole = lax.all_gather(whole, "dp", axis=0, tiled=True)
    part = lax.all_to_all(weight, "tensor", split_axis=0, concat_axis=1, tiled=True)
    grad = lax.dot_general(whole, part, CONTRACT_LAST, preferred_element_type=jnp.float32)
    grad = grad.reshape(-1, rows, part.shape[0])
    norm_sq = lax.psum(jnp.sum(grad * grad, axis=(1, 2)), ("dp", "tensor", "seq"))
    clipped = grad / jnp.maximum(1.0, jnp.sqrt(norm_sq))[:, None, None]
    slots = jnp.arange(owner_of.shape[0])
    owner_ex = jnp.sum(
        jnp.where(tenant_of[:, None] == slots[None, :], owner_of[None, :], 0), axis=1
    )
    select = (owner_ex[None, :] == slots[:, None]).astype(jnp.float32)
    sums = jnp.einsum("oe,erc->orc", select, clipped, precision=lax.Precision.HIGHEST)
    sums = lax.all_gather(sums, "tensor", axis=2, tiled=True)
    sums = lax.all_to_all(sums, "dp", split_axis=0, concat_axis=2, tiled=True)
    my_count = jnp.sum(jnp.where(owner_of == dp_index, counts, 0)).astype(jnp.float32)
    return (math.sqrt(PROMPT * D) * sums + noise) / my_count


def body(sizes, queries, keys, out_grad, value_weight, tenant_of, owner_of, counts, noise):
    swap = xor_pairs(2, 1)
    place = jnp.stack([lax.axis_index(a) for a in ("dp", "seq", "tensor")]).astype(jnp.int32)
    seq_index = place[1]
    q, k, g = queries[0], keys[0], out_grad[0]

    def other_half(array):
        half = array.shape[1] // 2
        return (lambda at: (0, (1 - at[1]) * half)), (array.shape[0], half)

    arrays, windows = [k, q, g], [other_half(x) for x in (k, q, g)]
    columns = value_weight.shape[0]
    dp = sizes["dp"]
    permutes = sizes["tensor"] == 2 and columns % LANES == 0 and dp in (1, 2, 4, 8)
    if permutes:
        width = -(-columns // (2 * LANES)) * LANES
        depth = value_weight.shape[1] // 2
        arrays.append(value_weight)
        windows.append(
            (lambda at: ((1 - at[2]) * (columns - width), at[1] * depth), (width, depth))
        )
    starts, shapes = zip(*windows)
    sent = cut(place, arrays, starts, shapes)
    k_far, q_far, g_far = (lax.ppermute(x, "seq", swap) for x in sent[:3])
    if permutes:
        weight_far = lax.ppermute(sent[3], "tensor", swap)

    halves = prompt_value_grad(place, q, k, g, q_far, k_far, g_far)
    mine = lax.dynamic_index_in_dim(halves, seq_index, 0, keepdims=False)
    theirs = lax.dynamic_index_in_dim(halves, 1 - seq_index, 0, keepdims=False)
    value_grad = jnp.stack([mine, lax.ppermute(theirs, "seq", swap)])
    if permutes:
        weight_far, value_grad = lax.optimization_barrier((weight_far, value_grad))
        weight_far = (weight_far, lax.ppermute(weight_far, "seq", swap))
        return tail_by_permutes(
            place, value_grad, value_weight, weight_far, tenant_of, owner_of, counts, noise, sizes
        )
    return tail_by_collectives(value_grad, value_weight, tenant_of, owner_of, counts, noise)


def solution(mesh):
    return jax.shard_map(
        functools.partial(body, dict(mesh.shape)),
        mesh=mesh,
        in_specs=(
            P(("group", "dp"), "seq", "tensor"),
            P(("group", "dp"), "seq", "tensor"),
            P(("group", "dp"), "seq", "tensor"),
            P("dp", "tensor"),
            P("group"),
            P("group"),
            P("group"),
            P(("group", "dp"), "seq", None),
        ),
        out_specs=P(("group", "dp"), "seq", None),
        check_vma=False,
    )
```

```python
import functools
import math

import jax
import jax.numpy as jnp
from jax import lax
from jax.experimental import pallas as pl
from jax.experimental.pallas import tpu as pltpu
from jax.sharding import PartitionSpec as P

D = 4608
HEAD_DIM = 128
PROMPT = 64
LANES = 128

softcap = 50.0
query_scale = 144.0 ** (-0.5)
TANH_SCALE = query_scale / softcap
EXP2_SCALE = softcap * math.log2(math.e)

PARTIAL_TYPE = jnp.float32


def GROUPS(dp):
    return [[step] for step in range(dp)]


CONTRACT_LAST = (((1,), (1,)), ((), ()))
VMEM = pl.BlockSpec(memory_space=pltpu.VMEM)
SMEM = pl.BlockSpec(memory_space=pltpu.SMEM)
HBM = pl.BlockSpec(memory_space=pltpu.HBM)
ANY = pl.BlockSpec(memory_space=pl.ANY)


def xor_pairs(size, step):
    return [(i, i ^ step) for i in range(size)]


def head_value_grad(q, k, g, prob):
    block = LANES
    rows = q.shape[1]
    group = q.shape[2] // HEAD_DIM
    key_pos = lax.broadcasted_iota(jnp.int32, (block, block), 0)
    query_pos = lax.broadcasted_iota(jnp.int32, (block, block), 1)
    keep = jnp.concatenate([key_pos <= query_pos] * group, axis=1)

    def query_block(half, parts, start, column):
        q_block = jnp.concatenate(
            [
                q[half, start : start + block, i * HEAD_DIM : (i + 1) * HEAD_DIM]
                for i in range(group)
            ],
            axis=0,
        )
        total, prompt = None, None
        for key_half, count, diagonal in parts:
            raw = lax.dot_general(
                k[key_half, :count, :], q_block, CONTRACT_LAST, preferred_element_type=jnp.float32
            )
            for low in range(0, count, block):
                e = jnp.exp2(jnp.tanh(raw[low : low + block] * TANH_SCALE) * EXP2_SCALE)
                if diagonal and low == count - block:
                    e = jnp.where(keep, e, 0.0)
                if prompt is None:
                    prompt = e[:PROMPT]
                part = jnp.sum(e.reshape(block // 8, 8, group * block), axis=0)
                total = part if total is None else total + part
        total = jnp.sum(total, axis=0, keepdims=True)
        scaled = (prompt / total).astype(jnp.bfloat16)
        for i in range(group):
            prob[i, :, column : column + block] = scaled[:, i * block : (i + 1) * block]

    for start in range(0, rows, block):
        query_block(0, [(0, start + block, True)], start, start)
    for start in range(0, rows, block):
        query_block(1, [(0, rows, False), (1, start + block, True)], start, rows + start)
    value = None
    for i in range(group):
        for half in range(2):
            term = jnp.dot(
                prob[i, :, half * rows : (half + 1) * rows],
                g[half, :, i * HEAD_DIM : (i + 1) * HEAD_DIM],
                preferred_element_type=jnp.float32,
            )
            value = term if value is None else value + term
    return value.astype(jnp.bfloat16)


def attention_kernel(place, q, k, g, q_far, k_far, g_far, mine, theirs, q_all, k_all, g_all, prob, done):
    heads = q_all.shape[0]
    seq = place[1]

    def copies(h):
        pairs = []
        for own, far, buffer in ((q, q_far, q_all), (k, k_far, k_all), (g, g_far, g_all)):
            width = buffer.shape[-1]
            at = pl.multiple_of((seq * heads + h) * width, LANES)
            pairs.append((own.at[:, pl.ds(at, width)], buffer.at[h, seq]))
            at = pl.multiple_of(h * width, LANES)
            pairs.append((far.at[:, pl.ds(at, width)], buffer.at[h, 1 - seq]))
        return [
            pltpu.make_async_copy(source, target, done.at[h, i])
            for i, (source, target) in enumerate(pairs)
        ]

    for h in range(heads):
        for copy in copies(h):
            copy.start()

    def step(h, carry):
        for copy in copies(h):
            copy.wait()
        value = head_value_grad(q_all.at[h], k_all.at[h], g_all.at[h], prob)
        at = pl.ds(pl.multiple_of(h * HEAD_DIM, LANES), HEAD_DIM)
        low, high = value[: PROMPT // 2], value[PROMPT // 2 :]
        mine[:, at] = jnp.where(seq == 0, low, high)
        theirs[:, at] = jnp.where(seq == 0, high, low)
        return carry

    lax.fori_loop(0, heads, step, 0)


def prompt_value_grad(place, q, k, g, q_far, k_far, g_far):
    rows = q.shape[0]
    heads = k_far.shape[1] // HEAD_DIM
    group = q.shape[1] // k.shape[1]
    width = group * HEAD_DIM
    return pl.pallas_call(
        attention_kernel,
        in_specs=[SMEM] + [HBM] * 3 + [ANY] * 3,
        out_specs=[VMEM] * 2,
        out_shape=[jax.ShapeDtypeStruct((PROMPT // 2, heads * HEAD_DIM), jnp.bfloat16)] * 2,
        scratch_shapes=[
            pltpu.VMEM((heads, 2, rows, width), jnp.bfloat16),
            pltpu.VMEM((heads, 2, rows, HEAD_DIM), jnp.bfloat16),
            pltpu.VMEM((heads, 2, rows, width), jnp.bfloat16),
            pltpu.VMEM((group, PROMPT, 2 * rows), jnp.bfloat16),
            pltpu.SemaphoreType.DMA((heads, 6)),
        ],
        compiler_params=pltpu.CompilerParams(vmem_limit_bytes=24 * 1024 * 1024),
        cost_estimate=pl.CostEstimate(
            flops=heads * group * 9 * rows * rows * HEAD_DIM,
            bytes_accessed=10 * rows * heads * width,
            transcendentals=heads * group * 4 * rows * rows,
        ),
    )(place, q, k, g, q_far, k_far, g_far)


def sibling_kernel(place, *refs, starts):
    count = len(starts)
    sources, targets, done = refs[:count], refs[count : 2 * count], refs[2 * count]
    copies = []
    for i, start in enumerate(starts):
        rows, width = targets[i].shape
        row, column = start(place)
        window = sources[i].at[pl.ds(row, rows), pl.ds(pl.multiple_of(column, LANES), width)]
        copies.append(pltpu.make_async_copy(window, targets[i], done.at[i]))
    for copy in copies:
        copy.start()
    for copy in copies:
        copy.wait()


def cut(place, arrays, starts, shapes):
    return pl.pallas_call(
        functools.partial(sibling_kernel, starts=starts),
        in_specs=[SMEM] + [HBM] * len(arrays),
        out_specs=[VMEM] * len(arrays),
        out_shape=[jax.ShapeDtypeStruct(shape, jnp.bfloat16) for shape in shapes],
        scratch_shapes=[pltpu.SemaphoreType.DMA((len(arrays),))],
        compiler_params=pltpu.CompilerParams(vmem_limit_bytes=16 * 1024 * 1024),
    )(place, *arrays)


def partial_kernel(*refs):
    blocks, weight, out = refs[:-2], refs[-2], refs[-1]
    rows = blocks[0].shape[0]
    total = lax.dot_general(
        jnp.concatenate([block[...] for block in blocks], axis=0),
        weight[...],
        CONTRACT_LAST,
        preferred_element_type=jnp.float32,
    )
    for i in range(len(blocks)):
        out[i] = total[i * rows : (i + 1) * rows].astype(out.dtype)


def combine_kernel(place, near, far, grad, squares, *, steps):
    example = lax.broadcasted_iota(jnp.int32, squares.shape, 0)
    by_example = jnp.zeros(squares.shape, jnp.float32)
    for i, step in enumerate(steps):
        folded = None
        for at in range(0, near.shape[2], LANES):
            part = near[i, :, at : at + LANES].astype(jnp.float32)
            part = part + far[i, :, at : at + LANES].astype(jnp.float32)
            grad[i, :, at : at + LANES] = part
            folded = part * part if folded is None else folded + part * part
        folded = jnp.sum(folded, axis=0, keepdims=True)
        by_example = jnp.where(example == (place[0] ^ step), folded, by_example)
    squares[...] = by_example


def share_kernel(place, tenant_of, owner_of, *refs, groups):
    examples = sum(len(steps) for steps in groups)
    norms, grads = refs[:examples], refs[examples : examples + len(groups)]
    outs, scales = refs[examples + len(groups) : -1], refs[-1]
    norm_sq = norms[0][...]
    for other in norms[1:]:
        norm_sq = norm_sq + other[...]
    norm_sq = jnp.sum(norm_sq, axis=1, keepdims=True)
    scales[...] = jnp.broadcast_to(1.0 / jnp.maximum(1.0, jnp.sqrt(norm_sq)), scales.shape)
    scale = [scales[pl.ds(place[0] ^ step, 1), :] for step in range(examples)]
    owner = [owner_of[tenant_of[place[0] ^ step]] for step in range(examples)]
    for k in range(examples):
        factor = [
            scale[step] * (owner[step] == (place[0] ^ k)).astype(jnp.float32)
            for step in range(examples)
        ]
        for at in range(0, outs[k].shape[1], LANES):
            total = None
            for ref, steps in zip(grads, groups):
                for i, step in enumerate(steps):
                    term = ref[i, :, at : at + LANES] * factor[step]
                    total = term if total is None else total + term
            outs[k][:, at : at + LANES] = total.astype(jnp.bfloat16)


def update_kernel(place, owner_of, counts, *refs, examples):
    shares, noise, out = refs[:examples], refs[examples], refs[examples + 1]
    columns = shares[0].shape[1]
    count = 0
    for slot in range(owner_of.shape[0]):
        count = count + jnp.where(owner_of[slot] == place[0], counts[slot], 0)
    count = count.astype(jnp.float32)
    for step in range(examples):
        at = pl.ds(pl.multiple_of((place[0] ^ step) * columns, LANES), columns)
        share = shares[step][...].astype(jnp.float32)
        out[0, :, at] = (math.sqrt(PROMPT * D) * share + noise[0, :, at]) / count


def to_dp(array, dp):
    return [array] + [lax.ppermute(array, "dp", xor_pairs(dp, step)) for step in range(1, dp)]


def tail_by_permutes(place, value_grad, weight, tenant_of, owner_of, counts, noise, sizes):
    dp = sizes["dp"]
    columns = weight.shape[0]
    rows = PROMPT // 2
    swap = xor_pairs(2, 1)
    small = pltpu.CompilerParams(vmem_limit_bytes=16 * 1024 * 1024)
    blocks = to_dp(value_grad, dp)
    groups = GROUPS(dp)
    grads, squares = [], None
    for steps in groups:
        shape = (len(steps), rows, columns)
        near = pl.pallas_call(
            partial_kernel,
            in_specs=[VMEM] * (len(steps) + 1),
            out_specs=VMEM,
            out_shape=jax.ShapeDtypeStruct(shape, PARTIAL_TYPE),
            compiler_params=small,
            cost_estimate=pl.CostEstimate(
                flops=2 * len(steps) * rows * weight.size,
                bytes_accessed=2 * weight.size,
                transcendentals=0,
            ),
        )(*[blocks[step] for step in steps], weight)
        far = lax.ppermute(near, "tensor", swap)
        grad, square = pl.pallas_call(
            functools.partial(combine_kernel, steps=steps),
            in_specs=[SMEM] + [VMEM] * 2,
            out_specs=[VMEM] * 2,
            out_shape=[
                jax.ShapeDtypeStruct(shape, jnp.float32),
                jax.ShapeDtypeStruct((8, LANES), jnp.float32),
            ],
            compiler_params=small,
        )(place, near, far)
        grads.append(grad)
        squares = square if squares is None else squares + square
    norms = to_dp(squares + lax.ppermute(squares, "seq", swap), dp)
    shares = pl.pallas_call(
        functools.partial(share_kernel, groups=groups),
        in_specs=[SMEM] * 3 + [VMEM] * (dp + len(groups)),
        out_specs=[VMEM] * dp,
        out_shape=[jax.ShapeDtypeStruct((rows, columns), jnp.bfloat16)] * dp,
        scratch_shapes=[pltpu.VMEM((8, LANES), jnp.float32)],
        compiler_params=small,
    )(place, tenant_of, owner_of, *norms, *grads)
    arrived = [shares[0]] + [
        lax.ppermute(shares[step], "dp", xor_pairs(dp, step)) for step in range(1, dp)
    ]
    return pl.pallas_call(
        functools.partial(update_kernel, examples=dp),
        in_specs=[SMEM] * 3 + [VMEM] * (dp + 1),
        out_specs=VMEM,
        out_shape=jax.ShapeDtypeStruct(noise.shape, jnp.float32),
        compiler_params=small,
    )(place, owner_of, counts, *arrived, noise)


def tail_by_collectives(value_grad, weight, tenant_of, owner_of, counts, noise):
    rows = PROMPT // 2
    dp_index = lax.axis_index("dp")
    whole = lax.all_gather(value_grad, "tensor", axis=1, tiled=True)
    whole = lax.all_gather(whole, "dp", axis=0, tiled=True)
    part = lax.all_to_all(weight, "tensor", split_axis=0, concat_axis=1, tiled=True)
    grad = lax.dot_general(whole, part, CONTRACT_LAST, preferred_element_type=jnp.float32)
    grad = grad.reshape(-1, rows, part.shape[0])
    norm_sq = lax.psum(jnp.sum(grad * grad, axis=(1, 2)), ("dp", "tensor", "seq"))
    clipped = grad / jnp.maximum(1.0, jnp.sqrt(norm_sq))[:, None, None]
    slots = jnp.arange(owner_of.shape[0])
    owner_ex = jnp.sum(
        jnp.where(tenant_of[:, None] == slots[None, :], owner_of[None, :], 0), axis=1
    )
    select = (owner_ex[None, :] == slots[:, None]).astype(jnp.float32)
    sums = jnp.einsum("oe,erc->orc", select, clipped, precision=lax.Precision.HIGHEST)
    sums = lax.all_gather(sums, "tensor", axis=2, tiled=True)
    sums = lax.all_to_all(sums, "dp", split_axis=0, concat_axis=2, tiled=True)
    my_count = jnp.sum(jnp.where(owner_of == dp_index, counts, 0)).astype(jnp.float32)
    return (math.sqrt(PROMPT * D) * sums + noise) / my_count


def body(sizes, queries, keys, out_grad, value_weight, tenant_of, owner_of, counts, noise):
    swap = xor_pairs(2, 1)
    place = jnp.stack([lax.axis_index(a) for a in ("dp", "seq", "tensor")]).astype(jnp.int32)
    seq_index = place[1]
    q, k, g = (
        pltpu.with_memory_space_constraint(x[0], pltpu.HBM) for x in (queries, keys, out_grad)
    )

    def other_half(array):
        half = array.shape[1] // 2
        return (lambda at: (0, (1 - at[1]) * half)), (array.shape[0], half)

    starts, shapes = zip(*[other_half(x) for x in (k, q, g)])
    k_far, q_far, g_far = (
        lax.ppermute(x, "seq", swap) for x in cut(place, (k, q, g), starts, shapes)
    )
    mine, theirs = prompt_value_grad(place, q, k, g, q_far, k_far, g_far)
    other = lax.ppermute(theirs, "seq", swap)
    first = seq_index == 0
    value_grad = jnp.concatenate(
        [jnp.where(first, mine, other), jnp.where(first, other, mine)], axis=1
    )
    aligned = value_weight.shape[0] % LANES == 0 and sizes["dp"] in (1, 2, 4, 8)
    if sizes["tensor"] == 2 and aligned:
        return tail_by_permutes(
            place, value_grad, value_weight, tenant_of, owner_of, counts, noise, sizes
        )
    return tail_by_collectives(value_grad, value_weight, tenant_of, owner_of, counts, noise)


def solution(mesh):
    return jax.shard_map(
        functools.partial(body, dict(mesh.shape)),
        mesh=mesh,
        in_specs=(
            P(("group", "dp"), "seq", "tensor"),
            P(("group", "dp"), "seq", "tensor"),
            P(("group", "dp"), "seq", "tensor"),
            P("dp", "tensor"),
            P("group"),
            P("group"),
            P("group"),
            P(("group", "dp"), "seq", None),
        ),
        out_specs=P(("group", "dp"), "seq", None),
        check_vma=False,
    )
```

```python
import functools
import math

import jax
import jax.numpy as jnp
from jax import lax
from jax.experimental import pallas as pl
from jax.experimental.pallas import tpu as pltpu
from jax.sharding import PartitionSpec as P

D = 4608
HEAD_DIM = 128
PROMPT = 64
LANES = 128

softcap = 50.0
query_scale = 144.0 ** (-0.5)
TANH_SCALE = query_scale / softcap
EXP2_SCALE = softcap * math.log2(math.e)

PARTIAL_TYPE = jnp.bfloat16


def GROUPS(dp):
    return [[step] for step in range(dp)]


CONTRACT_LAST = (((1,), (1,)), ((), ()))
VMEM = pl.BlockSpec(memory_space=pltpu.VMEM)
SMEM = pl.BlockSpec(memory_space=pltpu.SMEM)
HBM = pl.BlockSpec(memory_space=pltpu.HBM)
ANY = pl.BlockSpec(memory_space=pl.ANY)


def xor_pairs(size, step):
    return [(i, i ^ step) for i in range(size)]


def add_scores(query, keys, count, diagonal, total):
    block = LANES
    lanes = query.shape[0]
    raw = lax.dot_general(
        keys[:count, :], query, CONTRACT_LAST, preferred_element_type=jnp.float32
    )
    prompt = None
    for low in range(0, count, block):
        e = jnp.exp2(jnp.tanh(raw[low : low + block] * TANH_SCALE) * EXP2_SCALE)
        if diagonal and low == count - block:
            key_pos = lax.broadcasted_iota(jnp.int32, (block, block), 0)
            query_pos = lax.broadcasted_iota(jnp.int32, (block, block), 1)
            keep = jnp.concatenate([key_pos <= query_pos] * (lanes // block), axis=1)
            e = jnp.where(keep, e, 0.0)
        if prompt is None:
            prompt = e[:PROMPT]
        part = jnp.sum(e.reshape(block // 8, 8, lanes), axis=0)
        total = part if total is None else total + part
    return total, prompt


def query_block(queries):
    return jnp.concatenate(
        [
            queries[:, at : at + HEAD_DIM] for at in range(0, queries.shape[1], HEAD_DIM)
        ],
        axis=0,
    )


def triangle_kernel(place, q, k, g, totals, prompts, q_own, k_own, g_own, done):
    heads, rows, width = q_own.shape
    skipped = place[1] * heads
    lanes = width // HEAD_DIM * LANES

    def load(source, target, h, i):
        extent = target.shape[2]
        columns = pl.ds(pl.multiple_of((skipped + h) * extent, LANES), extent)
        return pltpu.make_async_copy(source.at[:, columns], target.at[h], done.at[h, i])

    for h in range(heads):
        load(k, k_own, h, 0).start()
        load(q, q_own, h, 1).start()
    for h in range(heads):
        load(g, g_own, h, 2).start()

    def step(h, carry):
        load(k, k_own, h, 0).wait()
        load(q, q_own, h, 1).wait()
        for i, start in enumerate(range(0, rows, LANES)):
            total, prompt = add_scores(
                query_block(q_own[h, start : start + LANES, :]),
                k_own.at[h],
                start + LANES,
                True,
                None,
            )
            at = slice(i * lanes, (i + 1) * lanes)
            totals[h, :, at] = total
            prompts[h, :, at] = prompt
        return carry

    lax.fori_loop(0, heads, step, 0)
    for h in range(heads):
        load(g, g_own, h, 2).wait()


def own_triangle(place, q, k, g):
    rows = q.shape[0]
    heads = k.shape[1] // (2 * HEAD_DIM)
    width = q.shape[1] // (2 * heads)
    lanes = width // HEAD_DIM * rows
    return pl.pallas_call(
        triangle_kernel,
        in_specs=[SMEM, HBM, HBM, HBM],
        out_specs=[VMEM] * 5,
        out_shape=[
            jax.ShapeDtypeStruct((heads, 8, lanes), jnp.float32),
            jax.ShapeDtypeStruct((heads, PROMPT, lanes), jnp.float32),
            jax.ShapeDtypeStruct((heads, rows, width), jnp.bfloat16),
            jax.ShapeDtypeStruct((heads, rows, HEAD_DIM), jnp.bfloat16),
            jax.ShapeDtypeStruct((heads, rows, width), jnp.bfloat16),
        ],
        scratch_shapes=[pltpu.SemaphoreType.DMA((heads, 3))],
        compiler_params=pltpu.CompilerParams(vmem_limit_bytes=16 * 1024 * 1024),
        cost_estimate=pl.CostEstimate(
            flops=2 * heads * lanes * rows * HEAD_DIM,
            bytes_accessed=6 * heads * rows * width,
            transcendentals=heads * lanes * rows,
        ),
    )(place, q, k, g)


def attention_kernel(
    place, totals, prompts, q_own, k_own, g_own, q_far, k_far, g_far, mine, theirs, k_first, prob
):
    heads, rows, width = q_own.shape
    group = width // HEAD_DIM
    lanes = group * LANES
    first = place[1] == 0

    def step(h, carry):
        at_q = pl.ds(pl.multiple_of(h * width, LANES), width)
        at_k = pl.ds(pl.multiple_of(h * HEAD_DIM, LANES), HEAD_DIM)
        k_first[...] = jnp.where(first, k_own[h], k_far[:, at_k])
        for i, start in enumerate(range(0, rows, LANES)):
            at = slice(i * lanes, (i + 1) * lanes)
            q_block = q_far[start : start + LANES, at_q]
            far, far_prompt = add_scores(
                query_block(q_block), k_far.at[:, at_k], start + LANES, True, None
            )
            q_block = jnp.where(first, q_block, q_own[h, start : start + LANES, :])
            square, late_prompt = add_scores(query_block(q_block), k_first, rows, False, None)
            own, own_prompt = totals[h, :, at], prompts[h, :, at]
            early = jnp.where(first, own, far)
            late = square + jnp.where(first, far, own)
            early_prompt = jnp.where(first, own_prompt, far_prompt)
            early = early_prompt / jnp.sum(early, axis=0, keepdims=True)
            late = late_prompt / jnp.sum(late, axis=0, keepdims=True)
            for slot, scaled in enumerate((jnp.where(first, early, late), jnp.where(first, late, early))):
                scaled = scaled.astype(jnp.bfloat16)
                column = slot * rows + start
                for j in range(group):
                    prob[j, :, column : column + LANES] = scaled[:, j * LANES : (j + 1) * LANES]
        value = None
        for j in range(group):
            at_g = pl.ds(pl.multiple_of(h * width + j * HEAD_DIM, LANES), HEAD_DIM)
            for slot, g in enumerate(
                (g_own[h, :, j * HEAD_DIM : (j + 1) * HEAD_DIM], g_far[:, at_g])
            ):
                term = jnp.dot(
                    prob[j, :, slot * rows : (slot + 1) * rows],
                    g,
                    preferred_element_type=jnp.float32,
                )
                value = term if value is None else value + term
        value = value.astype(jnp.bfloat16)
        low, high = value[: PROMPT // 2], value[PROMPT // 2 :]
        mine[:, at_k] = jnp.where(first, low, high)
        theirs[:, at_k] = jnp.where(first, high, low)
        return carry

    lax.fori_loop(0, heads, step, 0)


def prompt_value_grad(place, totals, prompts, q_own, k_own, g_own, q_far, k_far, g_far):
    heads, rows, width = q_own.shape
    group = width // HEAD_DIM
    return pl.pallas_call(
        attention_kernel,
        in_specs=[SMEM] + [VMEM] * 8,
        out_specs=[VMEM] * 2,
        out_shape=[jax.ShapeDtypeStruct((PROMPT // 2, heads * HEAD_DIM), jnp.bfloat16)] * 2,
        scratch_shapes=[
            pltpu.VMEM((rows, HEAD_DIM), jnp.bfloat16),
            pltpu.VMEM((group, PROMPT, 2 * rows), jnp.bfloat16),
        ],
        compiler_params=pltpu.CompilerParams(vmem_limit_bytes=16 * 1024 * 1024),
        cost_estimate=pl.CostEstimate(
            flops=heads * group * 7 * rows * rows * HEAD_DIM,
            bytes_accessed=10 * rows * heads * width,
            transcendentals=heads * group * 3 * rows * rows,
        ),
    )(place, totals, prompts, q_own, k_own, g_own, q_far, k_far, g_far)


def sibling_kernel(place, *refs, starts):
    count = len(starts)
    sources, targets, done = refs[:count], refs[count : 2 * count], refs[2 * count]
    copies = []
    for i, start in enumerate(starts):
        rows, width = targets[i].shape
        row, column = start(place)
        window = sources[i].at[pl.ds(row, rows), pl.ds(pl.multiple_of(column, LANES), width)]
        copies.append(pltpu.make_async_copy(window, targets[i], done.at[i]))
    for copy in copies:
        copy.start()
    for copy in copies:
        copy.wait()


def cut(place, arrays, starts, shapes):
    return pl.pallas_call(
        functools.partial(sibling_kernel, starts=starts),
        in_specs=[SMEM] + [HBM] * len(arrays),
        out_specs=[VMEM] * len(arrays),
        out_shape=[jax.ShapeDtypeStruct(shape, jnp.bfloat16) for shape in shapes],
        scratch_shapes=[pltpu.SemaphoreType.DMA((len(arrays),))],
        compiler_params=pltpu.CompilerParams(vmem_limit_bytes=16 * 1024 * 1024),
    )(place, *arrays)


def partial_kernel(*refs):
    blocks, weight, out = refs[:-2], refs[-2], refs[-1]
    rows = blocks[0].shape[0]
    total = lax.dot_general(
        jnp.concatenate([block[...] for block in blocks], axis=0),
        weight[...],
        CONTRACT_LAST,
        preferred_element_type=jnp.float32,
    )
    for i in range(len(blocks)):
        out[i] = total[i * rows : (i + 1) * rows].astype(out.dtype)


def combine_kernel(place, near, far, grad, squares, *, steps):
    example = lax.broadcasted_iota(jnp.int32, squares.shape, 0)
    by_example = jnp.zeros(squares.shape, jnp.float32)
    for i, step in enumerate(steps):
        folded = None
        for at in range(0, near.shape[2], LANES):
            part = near[i, :, at : at + LANES].astype(jnp.float32)
            part = part + far[i, :, at : at + LANES].astype(jnp.float32)
            grad[i, :, at : at + LANES] = part
            folded = part * part if folded is None else folded + part * part
        folded = jnp.sum(folded, axis=0, keepdims=True)
        by_example = jnp.where(example == (place[0] ^ step), folded, by_example)
    squares[...] = by_example


def share_kernel(place, tenant_of, owner_of, *refs, groups):
    examples = sum(len(steps) for steps in groups)
    norms, grads = refs[:examples], refs[examples : examples + len(groups)]
    outs, scales = refs[examples + len(groups) : -1], refs[-1]
    norm_sq = norms[0][...]
    for other in norms[1:]:
        norm_sq = norm_sq + other[...]
    norm_sq = jnp.sum(norm_sq, axis=1, keepdims=True)
    scales[...] = jnp.broadcast_to(1.0 / jnp.maximum(1.0, jnp.sqrt(norm_sq)), scales.shape)
    scale = [scales[pl.ds(place[0] ^ step, 1), :] for step in range(examples)]
    owner = [owner_of[tenant_of[place[0] ^ step]] for step in range(examples)]
    for k in range(examples):
        factor = [
            scale[step] * (owner[step] == (place[0] ^ k)).astype(jnp.float32)
            for step in range(examples)
        ]
        for at in range(0, outs[k].shape[1], LANES):
            total = None
            for ref, steps in zip(grads, groups):
                for i, step in enumerate(steps):
                    term = ref[i, :, at : at + LANES] * factor[step]
                    total = term if total is None else total + term
            outs[k][:, at : at + LANES] = total.astype(jnp.bfloat16)


def update_kernel(place, owner_of, counts, *refs, examples):
    shares, noise, out = refs[:examples], refs[examples], refs[examples + 1]
    columns = shares[0].shape[1]
    count = 0
    for slot in range(owner_of.shape[0]):
        count = count + jnp.where(owner_of[slot] == place[0], counts[slot], 0)
    count = count.astype(jnp.float32)
    for step in range(examples):
        at = pl.ds(pl.multiple_of((place[0] ^ step) * columns, LANES), columns)
        share = shares[step][...].astype(jnp.float32)
        out[0, :, at] = (math.sqrt(PROMPT * D) * share + noise[0, :, at]) / count


def to_dp(array, dp):
    return [array] + [lax.ppermute(array, "dp", xor_pairs(dp, step)) for step in range(1, dp)]


def tail_by_permutes(place, value_grad, weight, tenant_of, owner_of, counts, noise, sizes):
    dp = sizes["dp"]
    columns = weight.shape[0]
    rows = PROMPT // 2
    swap = xor_pairs(2, 1)
    small = pltpu.CompilerParams(vmem_limit_bytes=16 * 1024 * 1024)
    blocks = to_dp(value_grad, dp)
    groups = GROUPS(dp)
    grads, squares = [], None
    for steps in groups:
        shape = (len(steps), rows, columns)
        near = pl.pallas_call(
            partial_kernel,
            in_specs=[VMEM] * (len(steps) + 1),
            out_specs=VMEM,
            out_shape=jax.ShapeDtypeStruct(shape, PARTIAL_TYPE),
            compiler_params=small,
            cost_estimate=pl.CostEstimate(
                flops=2 * len(steps) * rows * weight.size,
                bytes_accessed=2 * weight.size,
                transcendentals=0,
            ),
        )(*[blocks[step] for step in steps], weight)
        far = lax.ppermute(near, "tensor", swap)
        grad, square = pl.pallas_call(
            functools.partial(combine_kernel, steps=steps),
            in_specs=[SMEM] + [VMEM] * 2,
            out_specs=[VMEM] * 2,
            out_shape=[
                jax.ShapeDtypeStruct(shape, jnp.float32),
                jax.ShapeDtypeStruct((8, LANES), jnp.float32),
            ],
            compiler_params=small,
        )(place, near, far)
        grads.append(grad)
        squares = square if squares is None else squares + square
    norms = to_dp(squares + lax.ppermute(squares, "seq", swap), dp)
    shares = pl.pallas_call(
        functools.partial(share_kernel, groups=groups),
        in_specs=[SMEM] * 3 + [VMEM] * (dp + len(groups)),
        out_specs=[VMEM] * dp,
        out_shape=[jax.ShapeDtypeStruct((rows, columns), jnp.bfloat16)] * dp,
        scratch_shapes=[pltpu.VMEM((8, LANES), jnp.float32)],
        compiler_params=small,
    )(place, tenant_of, owner_of, *norms, *grads)
    arrived = [shares[0]] + [
        lax.ppermute(shares[step], "dp", xor_pairs(dp, step)) for step in range(1, dp)
    ]
    return pl.pallas_call(
        functools.partial(update_kernel, examples=dp),
        in_specs=[SMEM] * 3 + [VMEM] * (dp + 1),
        out_specs=VMEM,
        out_shape=jax.ShapeDtypeStruct(noise.shape, jnp.float32),
        compiler_params=small,
    )(place, owner_of, counts, *arrived, noise)


def tail_by_collectives(value_grad, weight, tenant_of, owner_of, counts, noise):
    rows = PROMPT // 2
    dp_index = lax.axis_index("dp")
    whole = lax.all_gather(value_grad, "tensor", axis=1, tiled=True)
    whole = lax.all_gather(whole, "dp", axis=0, tiled=True)
    part = lax.all_to_all(weight, "tensor", split_axis=0, concat_axis=1, tiled=True)
    grad = lax.dot_general(whole, part, CONTRACT_LAST, preferred_element_type=jnp.float32)
    grad = grad.reshape(-1, rows, part.shape[0])
    norm_sq = lax.psum(jnp.sum(grad * grad, axis=(1, 2)), ("dp", "tensor", "seq"))
    clipped = grad / jnp.maximum(1.0, jnp.sqrt(norm_sq))[:, None, None]
    slots = jnp.arange(owner_of.shape[0])
    owner_ex = jnp.sum(
        jnp.where(tenant_of[:, None] == slots[None, :], owner_of[None, :], 0), axis=1
    )
    select = (owner_ex[None, :] == slots[:, None]).astype(jnp.float32)
    sums = jnp.einsum("oe,erc->orc", select, clipped, precision=lax.Precision.HIGHEST)
    sums = lax.all_gather(sums, "tensor", axis=2, tiled=True)
    sums = lax.all_to_all(sums, "dp", split_axis=0, concat_axis=2, tiled=True)
    my_count = jnp.sum(jnp.where(owner_of == dp_index, counts, 0)).astype(jnp.float32)
    return (math.sqrt(PROMPT * D) * sums + noise) / my_count


def body(sizes, queries, keys, out_grad, value_weight, tenant_of, owner_of, counts, noise):
    swap = xor_pairs(2, 1)
    place = jnp.stack([lax.axis_index(a) for a in ("dp", "seq", "tensor")]).astype(jnp.int32)
    seq_index = place[1]
    q, k, g = (
        pltpu.with_memory_space_constraint(x[0], pltpu.HBM) for x in (queries, keys, out_grad)
    )

    def other_half(array):
        half = array.shape[1] // 2
        return (lambda at: (0, (1 - at[1]) * half)), (array.shape[0], half)

    starts, shapes = zip(*[other_half(x) for x in (k, q, g)])
    k_far, q_far, g_far = (
        lax.ppermute(x, "seq", swap) for x in cut(place, (k, q, g), starts, shapes)
    )
    own = own_triangle(place, q, k, g)
    mine, theirs = prompt_value_grad(place, *own, q_far, k_far, g_far)
    other = lax.ppermute(theirs, "seq", swap)
    first = seq_index == 0
    value_grad = jnp.concatenate(
        [jnp.where(first, mine, other), jnp.where(first, other, mine)], axis=1
    )
    aligned = value_weight.shape[0] % LANES == 0 and sizes["dp"] in (1, 2, 4, 8)
    if sizes["tensor"] == 2 and aligned:
        return tail_by_permutes(
            place, value_grad, value_weight, tenant_of, owner_of, counts, noise, sizes
        )
    return tail_by_collectives(value_grad, value_weight, tenant_of, owner_of, counts, noise)


def solution(mesh):
    return jax.shard_map(
        functools.partial(body, dict(mesh.shape)),
        mesh=mesh,
        in_specs=(
            P(("group", "dp"), "seq", "tensor"),
            P(("group", "dp"), "seq", "tensor"),
            P(("group", "dp"), "seq", "tensor"),
            P("dp", "tensor"),
            P("group"),
            P("group"),
            P("group"),
            P(("group", "dp"), "seq", None),
        ),
        out_specs=P(("group", "dp"), "seq", None),
        check_vma=False,
    )
```

```python
import functools
import math

import jax
import jax.numpy as jnp
from jax import lax
from jax.experimental import pallas as pl
from jax.experimental.pallas import tpu as pltpu
from jax.sharding import PartitionSpec as P

D = 4608
HEAD_DIM = 128
PROMPT = 64
LANES = 128

softcap = 50.0
query_scale = 144.0 ** (-0.5)
TANH_SCALE = query_scale / softcap
EXP2_SCALE = softcap * math.log2(math.e)

PARTIAL_TYPE = jnp.bfloat16


def GROUPS(dp):
    return [[step] for step in range(dp)]


CONTRACT_LAST = (((1,), (1,)), ((), ()))
VMEM = pl.BlockSpec(memory_space=pltpu.VMEM)
SMEM = pl.BlockSpec(memory_space=pltpu.SMEM)
HBM = pl.BlockSpec(memory_space=pltpu.HBM)
ANY = pl.BlockSpec(memory_space=pl.ANY)


def xor_pairs(size, step):
    return [(i, i ^ step) for i in range(size)]


def add_scores(query, keys, count, diagonal, total):
    block = LANES
    lanes = query.shape[0]
    raw = lax.dot_general(
        keys[:count, :], query, CONTRACT_LAST, preferred_element_type=jnp.float32
    )
    prompt = None
    for low in range(0, count, block):
        e = jnp.exp2(jnp.tanh(raw[low : low + block] * TANH_SCALE) * EXP2_SCALE)
        if diagonal and low == count - block:
            key_pos = lax.broadcasted_iota(jnp.int32, (block, block), 0)
            query_pos = lax.broadcasted_iota(jnp.int32, (block, block), 1)
            keep = jnp.concatenate([key_pos <= query_pos] * (lanes // block), axis=1)
            e = jnp.where(keep, e, 0.0)
        if prompt is None:
            prompt = e[:PROMPT]
        part = jnp.sum(e.reshape(block // 8, 8, lanes), axis=0)
        total = part if total is None else total + part
    return total, prompt


def query_block(queries):
    return jnp.concatenate(
        [
            queries[:, at : at + HEAD_DIM] for at in range(0, queries.shape[1], HEAD_DIM)
        ],
        axis=0,
    )


def triangle_kernel(q, k, g, totals, prompts, q_own, k_own, g_own, done):
    heads, rows, width = q_own.shape
    skipped = lax.axis_index("seq") * heads
    lanes = width // HEAD_DIM * LANES

    def load(source, target, h, i):
        extent = target.shape[2]
        columns = pl.ds(pl.multiple_of((skipped + h) * extent, LANES), extent)
        return pltpu.make_async_copy(source.at[:, columns], target.at[h], done.at[h, i])

    for h in range(heads):
        load(k, k_own, h, 0).start()
        load(q, q_own, h, 1).start()
    for h in range(heads):
        load(g, g_own, h, 2).start()

    def step(h, carry):
        load(k, k_own, h, 0).wait()
        load(q, q_own, h, 1).wait()
        for i, start in enumerate(range(0, rows, LANES)):
            total, prompt = add_scores(
                query_block(q_own[h, start : start + LANES, :]),
                k_own.at[h],
                start + LANES,
                True,
                None,
            )
            at = slice(i * lanes, (i + 1) * lanes)
            totals[h, :, at] = total
            prompts[h, :, at] = prompt
        return carry

    lax.fori_loop(0, heads, step, 0)
    for h in range(heads):
        load(g, g_own, h, 2).wait()


def own_triangle(q, k, g):
    rows = q.shape[0]
    heads = k.shape[1] // (2 * HEAD_DIM)
    width = q.shape[1] // (2 * heads)
    lanes = width // HEAD_DIM * rows
    return pl.pallas_call(
        triangle_kernel,
        in_specs=[HBM, HBM, HBM],
        out_specs=[VMEM] * 5,
        out_shape=[
            jax.ShapeDtypeStruct((heads, 8, lanes), jnp.float32),
            jax.ShapeDtypeStruct((heads, PROMPT, lanes), jnp.float32),
            jax.ShapeDtypeStruct((heads, rows, width), jnp.bfloat16),
            jax.ShapeDtypeStruct((heads, rows, HEAD_DIM), jnp.bfloat16),
            jax.ShapeDtypeStruct((heads, rows, width), jnp.bfloat16),
        ],
        scratch_shapes=[pltpu.SemaphoreType.DMA((heads, 3))],
        compiler_params=pltpu.CompilerParams(vmem_limit_bytes=16 * 1024 * 1024),
        cost_estimate=pl.CostEstimate(
            flops=2 * heads * lanes * rows * HEAD_DIM,
            bytes_accessed=6 * heads * rows * width,
            transcendentals=heads * lanes * rows,
        ),
    )(q, k, g)


def attention_kernel(
    totals, prompts, q_own, k_own, g_own, q_far, k_far, g_far, mine, theirs, k_first, prob
):
    heads, rows, width = q_own.shape
    group = width // HEAD_DIM
    lanes = group * LANES
    first = lax.axis_index("seq") == 0

    def step(h, carry):
        at_q = pl.ds(pl.multiple_of(h * width, LANES), width)
        at_k = pl.ds(pl.multiple_of(h * HEAD_DIM, LANES), HEAD_DIM)
        k_first[...] = jnp.where(first, k_own[h], k_far[:, at_k])
        for i, start in enumerate(range(0, rows, LANES)):
            at = slice(i * lanes, (i + 1) * lanes)
            q_block = q_far[start : start + LANES, at_q]
            far, far_prompt = add_scores(
                query_block(q_block), k_far.at[:, at_k], start + LANES, True, None
            )
            q_block = jnp.where(first, q_block, q_own[h, start : start + LANES, :])
            square, late_prompt = add_scores(query_block(q_block), k_first, rows, False, None)
            own, own_prompt = totals[h, :, at], prompts[h, :, at]
            early = jnp.where(first, own, far)
            late = square + jnp.where(first, far, own)
            early_prompt = jnp.where(first, own_prompt, far_prompt)
            early = early_prompt / jnp.sum(early, axis=0, keepdims=True)
            late = late_prompt / jnp.sum(late, axis=0, keepdims=True)
            for slot, scaled in enumerate((jnp.where(first, early, late), jnp.where(first, late, early))):
                scaled = scaled.astype(jnp.bfloat16)
                column = slot * rows + start
                for j in range(group):
                    prob[j, :, column : column + LANES] = scaled[:, j * LANES : (j + 1) * LANES]
        value = None
        for j in range(group):
            at_g = pl.ds(pl.multiple_of(h * width + j * HEAD_DIM, LANES), HEAD_DIM)
            for slot, g in enumerate(
                (g_own[h, :, j * HEAD_DIM : (j + 1) * HEAD_DIM], g_far[:, at_g])
            ):
                term = jnp.dot(
                    prob[j, :, slot * rows : (slot + 1) * rows],
                    g,
                    preferred_element_type=jnp.float32,
                )
                value = term if value is None else value + term
        value = value.astype(jnp.bfloat16)
        low, high = value[: PROMPT // 2], value[PROMPT // 2 :]
        mine[:, at_k] = jnp.where(first, low, high)
        theirs[:, at_k] = jnp.where(first, high, low)
        return carry

    lax.fori_loop(0, heads, step, 0)


def prompt_value_grad(totals, prompts, q_own, k_own, g_own, q_far, k_far, g_far):
    heads, rows, width = q_own.shape
    group = width // HEAD_DIM
    return pl.pallas_call(
        attention_kernel,
        in_specs=[VMEM] * 8,
        out_specs=[VMEM] * 2,
        out_shape=[jax.ShapeDtypeStruct((PROMPT // 2, heads * HEAD_DIM), jnp.bfloat16)] * 2,
        scratch_shapes=[
            pltpu.VMEM((rows, HEAD_DIM), jnp.bfloat16),
            pltpu.VMEM((group, PROMPT, 2 * rows), jnp.bfloat16),
        ],
        compiler_params=pltpu.CompilerParams(vmem_limit_bytes=16 * 1024 * 1024),
        cost_estimate=pl.CostEstimate(
            flops=heads * group * 7 * rows * rows * HEAD_DIM,
            bytes_accessed=10 * rows * heads * width,
            transcendentals=heads * group * 3 * rows * rows,
        ),
    )(totals, prompts, q_own, k_own, g_own, q_far, k_far, g_far)


def sibling_kernel(*refs, starts):
    count = len(starts)
    sources, targets, done = refs[:count], refs[count : 2 * count], refs[2 * count]
    copies = []
    for i, start in enumerate(starts):
        rows, width = targets[i].shape
        row, column = start(lax.axis_index("seq"))
        window = sources[i].at[pl.ds(row, rows), pl.ds(pl.multiple_of(column, LANES), width)]
        copies.append(pltpu.make_async_copy(window, targets[i], done.at[i]))
    for copy in copies:
        copy.start()
    for copy in copies:
        copy.wait()


def cut(arrays, starts, shapes):
    return pl.pallas_call(
        functools.partial(sibling_kernel, starts=starts),
        in_specs=[HBM] * len(arrays),
        out_specs=[VMEM] * len(arrays),
        out_shape=[jax.ShapeDtypeStruct(shape, jnp.bfloat16) for shape in shapes],
        scratch_shapes=[pltpu.SemaphoreType.DMA((len(arrays),))],
        compiler_params=pltpu.CompilerParams(vmem_limit_bytes=16 * 1024 * 1024),
    )(*arrays)


def partial_kernel(*refs):
    blocks, weight, out = refs[:-2], refs[-2], refs[-1]
    rows = blocks[0].shape[0]
    total = lax.dot_general(
        jnp.concatenate([block[...] for block in blocks], axis=0),
        weight[...],
        CONTRACT_LAST,
        preferred_element_type=jnp.float32,
    )
    for i in range(len(blocks)):
        out[i] = total[i * rows : (i + 1) * rows].astype(out.dtype)


def combine_kernel(near, far, grad, squares, *, steps):
    example = lax.broadcasted_iota(jnp.int32, squares.shape, 0)
    by_example = jnp.zeros(squares.shape, jnp.float32)
    for i, step in enumerate(steps):
        folded = None
        for at in range(0, near.shape[2], LANES):
            part = near[i, :, at : at + LANES].astype(jnp.float32)
            part = part + far[i, :, at : at + LANES].astype(jnp.float32)
            grad[i, :, at : at + LANES] = part
            folded = part * part if folded is None else folded + part * part
        folded = jnp.sum(folded, axis=0, keepdims=True)
        by_example = jnp.where(example == (lax.axis_index("dp") ^ step), folded, by_example)
    squares[...] = by_example


def select_kernel(tenant_of, owner_of, counts, select, count, *, examples):
    dp_index = lax.axis_index("dp")
    for step in range(examples):
        owner = owner_of[tenant_of[dp_index ^ step]]
        for k in range(examples):
            hit = jnp.where(owner == (dp_index ^ k), 1.0, 0.0)
            row = k * examples + step
            select[row : row + 1, :] = jnp.full((1, LANES), hit, jnp.float32)
    total = 0
    for slot in range(examples):
        total = total + jnp.where(owner_of[slot] == dp_index, counts[slot], 0)
    count[...] = jnp.full((1, LANES), total.astype(jnp.float32), jnp.float32)


def share_kernel(select, *refs, groups):
    examples = sum(len(steps) for steps in groups)
    norms, grads = refs[:examples], refs[examples : examples + len(groups)]
    outs, scales = refs[examples + len(groups) : -1], refs[-1]
    norm_sq = norms[0][...]
    for other in norms[1:]:
        norm_sq = norm_sq + other[...]
    norm_sq = jnp.sum(norm_sq, axis=1, keepdims=True)
    scales[...] = jnp.broadcast_to(1.0 / jnp.maximum(1.0, jnp.sqrt(norm_sq)), scales.shape)
    dp_index = lax.axis_index("dp")
    scale = [scales[pl.ds(dp_index ^ step, 1), :] for step in range(examples)]
    for k in range(examples):
        factor = [
            scale[step] * select[k * examples + step : k * examples + step + 1, :]
            for step in range(examples)
        ]
        for at in range(0, outs[k].shape[1], LANES):
            total = None
            for ref, steps in zip(grads, groups):
                for i, step in enumerate(steps):
                    term = ref[i, :, at : at + LANES] * factor[step]
                    total = term if total is None else total + term
            outs[k][:, at : at + LANES] = total.astype(jnp.bfloat16)


def update_kernel(count, *refs, examples):
    shares, noise, out = refs[:examples], refs[examples], refs[examples + 1]
    stage, done = refs[examples + 2 :]
    columns = shares[0].shape[1]
    dp_index = lax.axis_index("dp")
    copies = []
    for step in range(examples):
        base = pl.multiple_of((dp_index ^ step) * columns, LANES)
        for at in range(0, columns, LANES):
            share = shares[step][:, at : at + LANES].astype(jnp.float32)
            added = noise[0, :, pl.ds(pl.multiple_of(base + at, LANES), LANES)]
            stage[step, :, at : at + LANES] = (math.sqrt(PROMPT * D) * share + added) / count[...]
        copy = pltpu.make_async_copy(
            stage.at[step], out.at[0, :, pl.ds(base, columns)], done.at[step]
        )
        copy.start()
        copies.append(copy)
    for copy in copies:
        copy.wait()


def to_dp(array, dp):
    return [array] + [lax.ppermute(array, "dp", xor_pairs(dp, step)) for step in range(1, dp)]


def tail_by_permutes(value_grad, weight, tenant_of, owner_of, counts, noise, sizes):
    dp = sizes["dp"]
    columns = weight.shape[0]
    rows = PROMPT // 2
    swap = xor_pairs(2, 1)
    small = pltpu.CompilerParams(vmem_limit_bytes=16 * 1024 * 1024)
    blocks = to_dp(value_grad, dp)
    groups = GROUPS(dp)
    tenant_of, blocks[-1] = lax.optimization_barrier((tenant_of, blocks[-1]))
    select, count = pl.pallas_call(
        functools.partial(select_kernel, examples=dp),
        in_specs=[SMEM] * 3,
        out_specs=[VMEM] * 2,
        out_shape=[
            jax.ShapeDtypeStruct((dp * dp, LANES), jnp.float32),
            jax.ShapeDtypeStruct((1, LANES), jnp.float32),
        ],
        compiler_params=small,
    )(tenant_of, owner_of, counts)
    grads, squares = [], None
    for steps in groups:
        shape = (len(steps), rows, columns)
        near = pl.pallas_call(
            partial_kernel,
            in_specs=[VMEM] * (len(steps) + 1),
            out_specs=VMEM,
            out_shape=jax.ShapeDtypeStruct(shape, PARTIAL_TYPE),
            compiler_params=small,
            cost_estimate=pl.CostEstimate(
                flops=2 * len(steps) * rows * weight.size,
                bytes_accessed=2 * weight.size,
                transcendentals=0,
            ),
        )(*[blocks[step] for step in steps], weight)
        far = lax.ppermute(near, "tensor", swap)
        grad, square = pl.pallas_call(
            functools.partial(combine_kernel, steps=steps),
            in_specs=[VMEM] * 2,
            out_specs=[VMEM] * 2,
            out_shape=[
                jax.ShapeDtypeStruct(shape, jnp.float32),
                jax.ShapeDtypeStruct((8, LANES), jnp.float32),
            ],
            compiler_params=small,
        )(near, far)
        grads.append(grad)
        squares = square if squares is None else squares + square
    norms = to_dp(squares + lax.ppermute(squares, "seq", swap), dp)
    shares = pl.pallas_call(
        functools.partial(share_kernel, groups=groups),
        in_specs=[VMEM] * (1 + dp + len(groups)),
        out_specs=[VMEM] * dp,
        out_shape=[jax.ShapeDtypeStruct((rows, columns), jnp.bfloat16)] * dp,
        scratch_shapes=[pltpu.VMEM((8, LANES), jnp.float32)],
        compiler_params=small,
    )(select, *norms, *grads)
    arrived = [shares[0]] + [
        lax.ppermute(shares[step], "dp", xor_pairs(dp, step)) for step in range(1, dp)
    ]
    return pl.pallas_call(
        functools.partial(update_kernel, examples=dp),
        in_specs=[VMEM] * (dp + 2),
        out_specs=ANY,
        out_shape=jax.ShapeDtypeStruct(noise.shape, jnp.float32),
        scratch_shapes=[
            pltpu.VMEM((dp, rows, columns), jnp.float32),
            pltpu.SemaphoreType.DMA((dp,)),
        ],
        compiler_params=small,
    )(count, *arrived, noise)


def tail_by_collectives(value_grad, weight, tenant_of, owner_of, counts, noise):
    rows = PROMPT // 2
    dp_index = lax.axis_index("dp")
    whole = lax.all_gather(value_grad, "tensor", axis=1, tiled=True)
    whole = lax.all_gather(whole, "dp", axis=0, tiled=True)
    part = lax.all_to_all(weight, "tensor", split_axis=0, concat_axis=1, tiled=True)
    grad = lax.dot_general(whole, part, CONTRACT_LAST, preferred_element_type=jnp.float32)
    grad = grad.reshape(-1, rows, part.shape[0])
    norm_sq = lax.psum(jnp.sum(grad * grad, axis=(1, 2)), ("dp", "tensor", "seq"))
    clipped = grad / jnp.maximum(1.0, jnp.sqrt(norm_sq))[:, None, None]
    slots = jnp.arange(owner_of.shape[0])
    owner_ex = jnp.sum(
        jnp.where(tenant_of[:, None] == slots[None, :], owner_of[None, :], 0), axis=1
    )
    select = (owner_ex[None, :] == slots[:, None]).astype(jnp.float32)
    sums = jnp.einsum("oe,erc->orc", select, clipped, precision=lax.Precision.HIGHEST)
    sums = lax.all_gather(sums, "tensor", axis=2, tiled=True)
    sums = lax.all_to_all(sums, "dp", split_axis=0, concat_axis=2, tiled=True)
    my_count = jnp.sum(jnp.where(owner_of == dp_index, counts, 0)).astype(jnp.float32)
    return (math.sqrt(PROMPT * D) * sums + noise) / my_count


def body(sizes, queries, keys, out_grad, value_weight, tenant_of, owner_of, counts, noise):
    swap = xor_pairs(2, 1)
    seq_index = lax.axis_index("seq")
    q, k, g = (
        pltpu.with_memory_space_constraint(x[0], pltpu.HBM) for x in (queries, keys, out_grad)
    )

    def other_half(array):
        half = array.shape[1] // 2
        return (lambda seq: (0, (1 - seq) * half)), (array.shape[0], half)

    starts, shapes = zip(*[other_half(x) for x in (k, q, g)])
    k_far, q_far, g_far = (
        lax.ppermute(x, "seq", swap) for x in cut((k, q, g), starts, shapes)
    )
    aligned = value_weight.shape[0] % LANES == 0 and sizes["dp"] in (1, 2, 4, 8)
    permutes = sizes["tensor"] == 2 and aligned
    own = own_triangle(q, k, g)
    mine, theirs = prompt_value_grad(*own, q_far, k_far, g_far)
    other = lax.ppermute(theirs, "seq", swap)
    first = seq_index == 0
    value_grad = jnp.concatenate(
        [jnp.where(first, mine, other), jnp.where(first, other, mine)], axis=1
    )
    if permutes:
        return tail_by_permutes(
            value_grad, value_weight, tenant_of, owner_of, counts, noise, sizes
        )
    return tail_by_collectives(value_grad, value_weight, tenant_of, owner_of, counts, noise)


def solution(mesh):
    return jax.shard_map(
        functools.partial(body, dict(mesh.shape)),
        mesh=mesh,
        in_specs=(
            P(("group", "dp"), "seq", "tensor"),
            P(("group", "dp"), "seq", "tensor"),
            P(("group", "dp"), "seq", "tensor"),
            P("dp", "tensor"),
            P("group"),
            P("group"),
            P("group"),
            P(("group", "dp"), "seq", None),
        ),
        out_specs=P(("group", "dp"), "seq", None),
        check_vma=False,
    )
```

```python
import functools
import math

import jax
import jax.numpy as jnp
from jax import lax
from jax.experimental import pallas as pl
from jax.experimental.pallas import tpu as pltpu
from jax.sharding import PartitionSpec as P

D = 4608
HEAD_DIM = 128
PROMPT = 64
LANES = 128

softcap = 50.0
query_scale = 144.0 ** (-0.5)
TANH_SCALE = query_scale / softcap
EXP2_SCALE = softcap * math.log2(math.e)

PARTIAL_TYPE = jnp.bfloat16


def GROUPS(dp):
    return [[step] for step in range(dp)]


CONTRACT_LAST = (((1,), (1,)), ((), ()))
VMEM = pl.BlockSpec(memory_space=pltpu.VMEM)
SMEM = pl.BlockSpec(memory_space=pltpu.SMEM)
HBM = pl.BlockSpec(memory_space=pltpu.HBM)
ANY = pl.BlockSpec(memory_space=pl.ANY)


def xor_pairs(size, step):
    return [(i, i ^ step) for i in range(size)]


def add_scores(query, keys, count, diagonal, total):
    block = LANES
    lanes = query.shape[0]
    raw = lax.dot_general(
        keys[:count, :], query, CONTRACT_LAST, preferred_element_type=jnp.float32
    )
    prompt = None
    for low in range(0, count, block):
        e = jnp.exp2(jnp.tanh(raw[low : low + block] * TANH_SCALE) * EXP2_SCALE)
        if diagonal and low == count - block:
            key_pos = lax.broadcasted_iota(jnp.int32, (block, block), 0)
            query_pos = lax.broadcasted_iota(jnp.int32, (block, block), 1)
            keep = jnp.concatenate([key_pos <= query_pos] * (lanes // block), axis=1)
            e = jnp.where(keep, e, 0.0)
        if prompt is None:
            prompt = e[:PROMPT]
        part = jnp.sum(e.reshape(block // 8, 8, lanes), axis=0)
        total = part if total is None else total + part
    return total, prompt


def query_block(queries):
    return jnp.concatenate(
        [
            queries[:, at : at + HEAD_DIM] for at in range(0, queries.shape[1], HEAD_DIM)
        ],
        axis=0,
    )


def triangle_kernel(
    q, k, g, q_head, k_head, totals, prompts, q_own, k_own, g_own, g_sent, done
):
    heads, rows, width = q_own.shape
    seq = lax.axis_index("seq")
    lanes = width // HEAD_DIM * LANES

    def load(source, target, h, i):
        extent = target.shape[2]
        columns = pl.ds(pl.multiple_of((seq * heads + h) * extent, LANES), extent)
        return pltpu.make_async_copy(source.at[:, columns], target.at[h], done.at[h, i])

    for h in range(1, heads):
        load(k, k_own, h, 0).start()
        load(q, q_own, h, 1).start()
    half = g_sent.shape[1]
    sibling = pl.ds(pl.multiple_of((1 - seq) * half, LANES), half)
    send = pltpu.make_async_copy(g.at[:, sibling], g_sent, done.at[0, 3])
    send.start()
    for h in range(heads):
        load(g, g_own, h, 2).start()

    def triangle(h, queries, keys):
        for i, start in enumerate(range(0, rows, LANES)):
            total, prompt = add_scores(
                query_block(queries[start : start + LANES, :]), keys, start + LANES, True, None
            )
            at = slice(i * lanes, (i + 1) * lanes)
            totals[h, :, at] = total
            prompts[h, :, at] = prompt

    def step(h, carry):
        load(k, k_own, h, 0).wait()
        load(q, q_own, h, 1).wait()
        triangle(h, q_own.at[h], k_own.at[h])
        return carry

    q_own[0] = q_head[...]
    k_own[0] = k_head[...]
    triangle(0, q_head, k_head)
    lax.fori_loop(1, heads, step, 0)
    send.wait()
    for h in range(heads):
        load(g, g_own, h, 2).wait()


def own_triangle(q, k, g, q_head, k_head):
    rows = q.shape[0]
    heads = k.shape[1] // (2 * HEAD_DIM)
    width = q.shape[1] // (2 * heads)
    lanes = width // HEAD_DIM * rows
    return pl.pallas_call(
        triangle_kernel,
        in_specs=[HBM] * 3 + [VMEM] * 2,
        out_specs=[VMEM] * 6,
        out_shape=[
            jax.ShapeDtypeStruct((heads, 8, lanes), jnp.float32),
            jax.ShapeDtypeStruct((heads, PROMPT, lanes), jnp.float32),
            jax.ShapeDtypeStruct((heads, rows, width), jnp.bfloat16),
            jax.ShapeDtypeStruct((heads, rows, HEAD_DIM), jnp.bfloat16),
            jax.ShapeDtypeStruct((heads, rows, width), jnp.bfloat16),
            jax.ShapeDtypeStruct((rows, heads * width), jnp.bfloat16),
        ],
        scratch_shapes=[pltpu.SemaphoreType.DMA((heads, 4))],
        compiler_params=pltpu.CompilerParams(vmem_limit_bytes=16 * 1024 * 1024),
        cost_estimate=pl.CostEstimate(
            flops=2 * heads * lanes * rows * HEAD_DIM,
            bytes_accessed=6 * heads * rows * width,
            transcendentals=heads * lanes * rows,
        ),
    )(q, k, g, q_head, k_head)


def attention_kernel(totals, prompts, q_own, k_own, far, prob, k_first):
    heads, rows, width = q_own.shape
    group = width // HEAD_DIM
    lanes = group * LANES
    first = lax.axis_index("seq") == 0

    def step(h, carry):
        at_q = pl.ds(pl.multiple_of(h * width, LANES), width)
        at_k = pl.ds(pl.multiple_of(heads * width + h * HEAD_DIM, LANES), HEAD_DIM)
        k_far = far.at[:, at_k]
        k_first[...] = jnp.where(first, k_own[h], k_far[...])
        for i, start in enumerate(range(0, rows, LANES)):
            at = slice(i * lanes, (i + 1) * lanes)
            q_block = far[start : start + LANES, at_q]
            other, far_prompt = add_scores(query_block(q_block), k_far, start + LANES, True, None)
            q_block = jnp.where(first, q_block, q_own[h, start : start + LANES, :])
            square, late_prompt = add_scores(query_block(q_block), k_first, rows, False, None)
            own, own_prompt = totals[h, :, at], prompts[h, :, at]
            early = jnp.where(first, own, other)
            late = square + jnp.where(first, other, own)
            early_prompt = jnp.where(first, own_prompt, far_prompt)
            early = early_prompt / jnp.sum(early, axis=0, keepdims=True)
            late = late_prompt / jnp.sum(late, axis=0, keepdims=True)
            for slot, scaled in enumerate((jnp.where(first, early, late), jnp.where(first, late, early))):
                scaled = scaled.astype(jnp.bfloat16)
                column = slot * rows + start
                for j in range(group):
                    prob[h, j, :, column : column + LANES] = scaled[:, j * LANES : (j + 1) * LANES]
        return carry

    lax.fori_loop(0, heads, step, 0)


def value_kernel(prob, g_own, g_far, mine, theirs):
    heads, rows, width = g_own.shape
    group = width // HEAD_DIM
    first = lax.axis_index("seq") == 0

    def step(h):
        at_k = slice(h * HEAD_DIM, (h + 1) * HEAD_DIM)
        at_g = slice(h * width, (h + 1) * width)
        whole = None
        for slot, g in enumerate((g_own[h], g_far[:, at_g])):
            term = jnp.dot(
                jnp.concatenate(
                    [prob[h, j, :, slot * rows : (slot + 1) * rows] for j in range(group)], axis=0
                ),
                g,
                preferred_element_type=jnp.float32,
            )
            whole = term if whole is None else whole + term
        value = None
        for j in range(group):
            part = whole[j * PROMPT : (j + 1) * PROMPT, j * HEAD_DIM : (j + 1) * HEAD_DIM]
            value = part if value is None else value + part
        value = value.astype(jnp.bfloat16)
        low, high = value[: PROMPT // 2], value[PROMPT // 2 :]
        mine[:, at_k] = jnp.where(first, low, high)
        theirs[:, at_k] = jnp.where(first, high, low)

    for h in range(heads):
        step(h)


def prompt_value_grad(totals, prompts, q_own, k_own, g_own, far, g_far):
    heads, rows, width = q_own.shape
    group = width // HEAD_DIM
    prob = pl.pallas_call(
        attention_kernel,
        in_specs=[VMEM] * 5,
        out_specs=VMEM,
        out_shape=jax.ShapeDtypeStruct((heads, group, PROMPT, 2 * rows), jnp.bfloat16),
        scratch_shapes=[pltpu.VMEM((rows, HEAD_DIM), jnp.bfloat16)],
        compiler_params=pltpu.CompilerParams(vmem_limit_bytes=16 * 1024 * 1024),
        cost_estimate=pl.CostEstimate(
            flops=heads * group * 6 * rows * rows * HEAD_DIM,
            bytes_accessed=6 * rows * heads * width,
            transcendentals=heads * group * 3 * rows * rows,
        ),
    )(totals, prompts, q_own, k_own, far)
    return pl.pallas_call(
        value_kernel,
        in_specs=[VMEM] * 3,
        out_specs=[VMEM] * 2,
        out_shape=[jax.ShapeDtypeStruct((PROMPT // 2, heads * HEAD_DIM), jnp.bfloat16)] * 2,
        compiler_params=pltpu.CompilerParams(vmem_limit_bytes=16 * 1024 * 1024),
        cost_estimate=pl.CostEstimate(
            flops=4 * heads * group * PROMPT * rows * HEAD_DIM,
            bytes_accessed=6 * rows * heads * width,
            transcendentals=0,
        ),
    )(prob, g_own, g_far)


def sibling_kernel(q, k, out, q_head, k_head, done):
    seq = lax.axis_index("seq")
    copies, to = [], 0
    for i, source in enumerate((q, k)):
        half = source.shape[1] // 2
        columns = pl.ds(pl.multiple_of((1 - seq) * half, LANES), half)
        copies.append(
            pltpu.make_async_copy(
                source.at[:, columns], out.at[:, to : to + half], done.at[i]
            )
        )
        to += half
    for i, (source, target) in enumerate(((q, q_head), (k, k_head))):
        start = pl.multiple_of(seq * (source.shape[1] // 2), LANES)
        copies.append(
            pltpu.make_async_copy(
                source.at[:, pl.ds(start, target.shape[1])], target, done.at[2 + i]
            )
        )
    for copy in copies:
        copy.start()
    for copy in copies:
        copy.wait()


def for_sibling(q, k):
    rows = q.shape[0]
    width = q.shape[1] * HEAD_DIM // k.shape[1]
    return pl.pallas_call(
        sibling_kernel,
        in_specs=[HBM] * 2,
        out_specs=[VMEM] * 3,
        out_shape=[
            jax.ShapeDtypeStruct((rows, (q.shape[1] + k.shape[1]) // 2), jnp.bfloat16),
            jax.ShapeDtypeStruct((rows, width), jnp.bfloat16),
            jax.ShapeDtypeStruct((rows, HEAD_DIM), jnp.bfloat16),
        ],
        scratch_shapes=[pltpu.SemaphoreType.DMA((4,))],
        compiler_params=pltpu.CompilerParams(vmem_limit_bytes=16 * 1024 * 1024),
    )(q, k)


def partial_kernel(*refs):
    blocks, weight, out = refs[:-2], refs[-2], refs[-1]
    rows = blocks[0].shape[0]
    total = lax.dot_general(
        jnp.concatenate([block[...] for block in blocks], axis=0),
        weight[...],
        CONTRACT_LAST,
        preferred_element_type=jnp.float32,
    )
    for i in range(len(blocks)):
        out[i] = total[i * rows : (i + 1) * rows].astype(out.dtype)


def combine_kernel(near, far, grad, squares, *, steps):
    example = lax.broadcasted_iota(jnp.int32, squares.shape, 0)
    by_example = jnp.zeros(squares.shape, jnp.float32)
    for i, step in enumerate(steps):
        folded = None
        for at in range(0, near.shape[2], LANES):
            part = near[i, :, at : at + LANES].astype(jnp.float32)
            part = part + far[i, :, at : at + LANES].astype(jnp.float32)
            grad[i, :, at : at + LANES] = part
            folded = part * part if folded is None else folded + part * part
        folded = jnp.sum(folded, axis=0, keepdims=True)
        by_example = jnp.where(example == (lax.axis_index("dp") ^ step), folded, by_example)
    squares[...] = by_example


def select_kernel(tenant_of, owner_of, counts, select, count, *, examples):
    dp_index = lax.axis_index("dp")
    for step in range(examples):
        owner = owner_of[tenant_of[dp_index ^ step]]
        for k in range(examples):
            hit = jnp.where(owner == (dp_index ^ k), 1.0, 0.0)
            row = k * examples + step
            select[row : row + 1, :] = jnp.full((1, LANES), hit, jnp.float32)
    total = 0
    for slot in range(examples):
        total = total + jnp.where(owner_of[slot] == dp_index, counts[slot], 0)
    count[...] = jnp.full((1, LANES), total.astype(jnp.float32), jnp.float32)


def share_kernel(select, *refs, groups):
    examples = sum(len(steps) for steps in groups)
    norms, grads = refs[:examples], refs[examples : examples + len(groups)]
    outs, scales = refs[examples + len(groups) : -1], refs[-1]
    norm_sq = norms[0][...]
    for other in norms[1:]:
        norm_sq = norm_sq + other[...]
    norm_sq = jnp.sum(norm_sq, axis=1, keepdims=True)
    scales[...] = jnp.broadcast_to(1.0 / jnp.maximum(1.0, jnp.sqrt(norm_sq)), scales.shape)
    dp_index = lax.axis_index("dp")
    scale = [scales[pl.ds(dp_index ^ step, 1), :] for step in range(examples)]
    for k in range(examples):
        factor = [
            scale[step] * select[k * examples + step : k * examples + step + 1, :]
            for step in range(examples)
        ]
        for at in range(0, outs[k].shape[1], LANES):
            total = None
            for ref, steps in zip(grads, groups):
                for i, step in enumerate(steps):
                    term = ref[i, :, at : at + LANES] * factor[step]
                    total = term if total is None else total + term
            outs[k][:, at : at + LANES] = total.astype(jnp.bfloat16)


def update_kernel(count, *refs, examples):
    shares, noise, out = refs[:examples], refs[examples], refs[examples + 1]
    stage, done = refs[examples + 2 :]
    columns = shares[0].shape[1]
    dp_index = lax.axis_index("dp")
    copies = []
    for step in range(examples):
        base = pl.multiple_of((dp_index ^ step) * columns, LANES)
        for at in range(0, columns, LANES):
            share = shares[step][:, at : at + LANES].astype(jnp.float32)
            added = noise[0, :, pl.ds(pl.multiple_of(base + at, LANES), LANES)]
            stage[step, :, at : at + LANES] = (math.sqrt(PROMPT * D) * share + added) / count[...]
        copy = pltpu.make_async_copy(
            stage.at[step], out.at[0, :, pl.ds(base, columns)], done.at[step]
        )
        copy.start()
        copies.append(copy)
    for copy in copies:
        copy.wait()


def to_dp(array, dp):
    return [array] + [lax.ppermute(array, "dp", xor_pairs(dp, step)) for step in range(1, dp)]


def tail_by_permutes(value_grad, weight, tenant_of, owner_of, counts, noise, sizes):
    dp = sizes["dp"]
    columns = weight.shape[0]
    rows = PROMPT // 2
    swap = xor_pairs(2, 1)
    small = pltpu.CompilerParams(vmem_limit_bytes=16 * 1024 * 1024)
    blocks = to_dp(value_grad, dp)
    groups = GROUPS(dp)
    tenant_of, blocks[-1] = lax.optimization_barrier((tenant_of, blocks[-1]))
    select, count = pl.pallas_call(
        functools.partial(select_kernel, examples=dp),
        in_specs=[SMEM] * 3,
        out_specs=[VMEM] * 2,
        out_shape=[
            jax.ShapeDtypeStruct((dp * dp, LANES), jnp.float32),
            jax.ShapeDtypeStruct((1, LANES), jnp.float32),
        ],
        compiler_params=small,
    )(tenant_of, owner_of, counts)
    grads, squares = [], None
    for steps in groups:
        shape = (len(steps), rows, columns)
        near = pl.pallas_call(
            partial_kernel,
            in_specs=[VMEM] * (len(steps) + 1),
            out_specs=VMEM,
            out_shape=jax.ShapeDtypeStruct(shape, PARTIAL_TYPE),
            compiler_params=small,
            cost_estimate=pl.CostEstimate(
                flops=2 * len(steps) * rows * weight.size,
                bytes_accessed=2 * weight.size,
                transcendentals=0,
            ),
        )(*[blocks[step] for step in steps], weight)
        far = lax.ppermute(near, "tensor", swap)
        grad, square = pl.pallas_call(
            functools.partial(combine_kernel, steps=steps),
            in_specs=[VMEM] * 2,
            out_specs=[VMEM] * 2,
            out_shape=[
                jax.ShapeDtypeStruct(shape, jnp.float32),
                jax.ShapeDtypeStruct((8, LANES), jnp.float32),
            ],
            compiler_params=small,
        )(near, far)
        grads.append(grad)
        squares = square if squares is None else squares + square
    norms = to_dp(squares + lax.ppermute(squares, "seq", swap), dp)
    shares = pl.pallas_call(
        functools.partial(share_kernel, groups=groups),
        in_specs=[VMEM] * (1 + dp + len(groups)),
        out_specs=[VMEM] * dp,
        out_shape=[jax.ShapeDtypeStruct((rows, columns), jnp.bfloat16)] * dp,
        scratch_shapes=[pltpu.VMEM((8, LANES), jnp.float32)],
        compiler_params=small,
    )(select, *norms, *grads)
    arrived = [shares[0]] + [
        lax.ppermute(shares[step], "dp", xor_pairs(dp, step)) for step in range(1, dp)
    ]
    return pl.pallas_call(
        functools.partial(update_kernel, examples=dp),
        in_specs=[VMEM] * (dp + 2),
        out_specs=ANY,
        out_shape=jax.ShapeDtypeStruct(noise.shape, jnp.float32),
        scratch_shapes=[
            pltpu.VMEM((dp, rows, columns), jnp.float32),
            pltpu.SemaphoreType.DMA((dp,)),
        ],
        compiler_params=small,
    )(count, *arrived, noise)


def tail_by_collectives(value_grad, weight, tenant_of, owner_of, counts, noise):
    rows = PROMPT // 2
    dp_index = lax.axis_index("dp")
    whole = lax.all_gather(value_grad, "tensor", axis=1, tiled=True)
    whole = lax.all_gather(whole, "dp", axis=0, tiled=True)
    part = lax.all_to_all(weight, "tensor", split_axis=0, concat_axis=1, tiled=True)
    grad = lax.dot_general(whole, part, CONTRACT_LAST, preferred_element_type=jnp.float32)
    grad = grad.reshape(-1, rows, part.shape[0])
    norm_sq = lax.psum(jnp.sum(grad * grad, axis=(1, 2)), ("dp", "tensor", "seq"))
    clipped = grad / jnp.maximum(1.0, jnp.sqrt(norm_sq))[:, None, None]
    slots = jnp.arange(owner_of.shape[0])
    owner_ex = jnp.sum(
        jnp.where(tenant_of[:, None] == slots[None, :], owner_of[None, :], 0), axis=1
    )
    select = (owner_ex[None, :] == slots[:, None]).astype(jnp.float32)
    sums = jnp.einsum("oe,erc->orc", select, clipped, precision=lax.Precision.HIGHEST)
    sums = lax.all_gather(sums, "tensor", axis=2, tiled=True)
    sums = lax.all_to_all(sums, "dp", split_axis=0, concat_axis=2, tiled=True)
    my_count = jnp.sum(jnp.where(owner_of == dp_index, counts, 0)).astype(jnp.float32)
    return (math.sqrt(PROMPT * D) * sums + noise) / my_count


def body(sizes, queries, keys, out_grad, value_weight, tenant_of, owner_of, counts, noise):
    swap = xor_pairs(2, 1)
    seq_index = lax.axis_index("seq")
    q, k, g = (
        pltpu.with_memory_space_constraint(x[0], pltpu.HBM) for x in (queries, keys, out_grad)
    )

    sent, q_head, k_head = for_sibling(q, k)
    far = lax.ppermute(sent, "seq", swap)
    aligned = value_weight.shape[0] % LANES == 0 and sizes["dp"] in (1, 2, 4, 8)
    permutes = sizes["tensor"] == 2 and aligned
    *own, g_sent = own_triangle(q, k, g, q_head, k_head)
    g_far = lax.ppermute(g_sent, "seq", swap)
    mine, theirs = prompt_value_grad(*own, far, g_far)
    other = lax.ppermute(theirs, "seq", swap)
    first = seq_index == 0
    value_grad = jnp.concatenate(
        [jnp.where(first, mine, other), jnp.where(first, other, mine)], axis=1
    )
    if permutes:
        return tail_by_permutes(
            value_grad, value_weight, tenant_of, owner_of, counts, noise, sizes
        )
    return tail_by_collectives(value_grad, value_weight, tenant_of, owner_of, counts, noise)


def solution(mesh):
    return jax.shard_map(
        functools.partial(body, dict(mesh.shape)),
        mesh=mesh,
        in_specs=(
            P(("group", "dp"), "seq", "tensor"),
            P(("group", "dp"), "seq", "tensor"),
            P(("group", "dp"), "seq", "tensor"),
            P("dp", "tensor"),
            P("group"),
            P("group"),
            P("group"),
            P(("group", "dp"), "seq", None),
        ),
        out_specs=P(("group", "dp"), "seq", None),
        check_vma=False,
    )
```

```python
import functools
import math

import jax
import jax.numpy as jnp
from jax import lax
from jax.experimental import pallas as pl
from jax.experimental.pallas import tpu as pltpu
from jax.sharding import PartitionSpec as P

D = 4608
HEAD_DIM = 128
PROMPT = 64
LANES = 128

softcap = 50.0
query_scale = 144.0 ** (-0.5)
TANH_SCALE = query_scale / softcap
EXP2_SCALE = softcap * math.log2(math.e)

PARTIAL_TYPE = jnp.bfloat16


ARRIVAL = {"blocks": (3, 1, 2), "norms": (3, 2, 1), "shares": (1, 2, 3)}


def arrival(what, dp):
    return list(ARRIVAL[what]) if dp == 4 else list(range(1, dp))


CONTRACT_LAST = (((1,), (1,)), ((), ()))
VMEM = pl.BlockSpec(memory_space=pltpu.VMEM)
SMEM = pl.BlockSpec(memory_space=pltpu.SMEM)
HBM = pl.BlockSpec(memory_space=pltpu.HBM)
ANY = pl.BlockSpec(memory_space=pl.ANY)


def xor_pairs(size, step):
    return [(i, i ^ step) for i in range(size)]


def add_scores(query, keys, count, diagonal, total):
    block = LANES
    lanes = query.shape[0]
    raw = lax.dot_general(
        keys[:count, :], query, CONTRACT_LAST, preferred_element_type=jnp.float32
    )
    prompt = None
    for low in range(0, count, block):
        e = jnp.exp2(jnp.tanh(raw[low : low + block] * TANH_SCALE) * EXP2_SCALE)
        if diagonal and low == count - block:
            key_pos = lax.broadcasted_iota(jnp.int32, (block, block), 0)
            query_pos = lax.broadcasted_iota(jnp.int32, (block, block), 1)
            keep = jnp.concatenate([key_pos <= query_pos] * (lanes // block), axis=1)
            e = jnp.where(keep, e, 0.0)
        if prompt is None:
            prompt = e[:PROMPT]
        part = jnp.sum(e.reshape(block // 8, 8, lanes), axis=0)
        total = part if total is None else total + part
    return total, prompt


def query_block(queries):
    return jnp.concatenate(
        [
            queries[:, at : at + HEAD_DIM] for at in range(0, queries.shape[1], HEAD_DIM)
        ],
        axis=0,
    )


def triangle_kernel(q, k, g, q_head, k_head, totals, prompts, q_own, k_own, g_sent, done):
    heads, rows, width = q_own.shape
    seq = lax.axis_index("seq")
    lanes = width // HEAD_DIM * LANES

    def load(source, target, h, i):
        extent = target.shape[2]
        columns = pl.ds(pl.multiple_of((seq * heads + h) * extent, LANES), extent)
        return pltpu.make_async_copy(source.at[:, columns], target.at[h], done.at[h, i])

    for h in range(1, heads):
        load(k, k_own, h, 0).start()
        load(q, q_own, h, 1).start()
    half = g_sent.shape[1]
    sibling = pl.ds(pl.multiple_of((1 - seq) * half, LANES), half)
    send = pltpu.make_async_copy(g.at[:, sibling], g_sent, done.at[0, 0])
    send.start()

    def triangle(h, queries, keys):
        for i, start in enumerate(range(0, rows, LANES)):
            total, prompt = add_scores(
                query_block(queries[start : start + LANES, :]), keys, start + LANES, True, None
            )
            at = slice(i * lanes, (i + 1) * lanes)
            totals[h, :, at] = total
            prompts[h, :, at] = prompt

    def step(h, carry):
        load(k, k_own, h, 0).wait()
        load(q, q_own, h, 1).wait()
        triangle(h, q_own.at[h], k_own.at[h])
        return carry

    q_own[0] = q_head[...]
    k_own[0] = k_head[...]
    triangle(0, q_head, k_head)
    lax.fori_loop(1, heads, step, 0)
    send.wait()


def own_triangle(q, k, g, q_head, k_head):
    rows = q.shape[0]
    heads = k.shape[1] // (2 * HEAD_DIM)
    width = q.shape[1] // (2 * heads)
    lanes = width // HEAD_DIM * rows
    return pl.pallas_call(
        triangle_kernel,
        in_specs=[HBM] * 3 + [VMEM] * 2,
        out_specs=[VMEM] * 5,
        out_shape=[
            jax.ShapeDtypeStruct((heads, 8, lanes), jnp.float32),
            jax.ShapeDtypeStruct((heads, PROMPT, lanes), jnp.float32),
            jax.ShapeDtypeStruct((heads, rows, width), jnp.bfloat16),
            jax.ShapeDtypeStruct((heads, rows, HEAD_DIM), jnp.bfloat16),
            jax.ShapeDtypeStruct((rows, heads * width), jnp.bfloat16),
        ],
        scratch_shapes=[pltpu.SemaphoreType.DMA((heads, 2))],
        compiler_params=pltpu.CompilerParams(vmem_limit_bytes=16 * 1024 * 1024),
        cost_estimate=pl.CostEstimate(
            flops=2 * heads * lanes * rows * HEAD_DIM,
            bytes_accessed=6 * heads * rows * width,
            transcendentals=heads * lanes * rows,
        ),
    )(q, k, g, q_head, k_head)


def attention_kernel(*refs, turn):
    if turn:
        totals, prompts, q_own, k_own, g, far, weight, prob, g_own, turned, k_first, done = refs
    else:
        totals, prompts, q_own, k_own, g, far, prob, g_own, k_first, done = refs
    heads, rows, width = q_own.shape
    group = width // HEAD_DIM
    lanes = group * LANES
    seq = lax.axis_index("seq")
    first = seq == 0
    half = g_own.shape[1]
    load = pltpu.make_async_copy(
        g.at[:, pl.ds(pl.multiple_of(seq * half, LANES), half)], g_own, done.at[0]
    )
    load.start()

    def step(h, carry):
        at_q = pl.ds(pl.multiple_of(h * width, LANES), width)
        at_k = pl.ds(pl.multiple_of(heads * width + h * HEAD_DIM, LANES), HEAD_DIM)
        k_far = far.at[:, at_k]
        if turn:
            share = weight.shape[1] // heads
            features = pl.ds(pl.multiple_of(h * share, LANES), share)
            turned[features, :] = weight[:, features].T
        k_first[...] = jnp.where(first, k_own[h], k_far[...])
        for i, start in enumerate(range(0, rows, LANES)):
            at = slice(i * lanes, (i + 1) * lanes)
            q_block = far[start : start + LANES, at_q]
            other, far_prompt = add_scores(query_block(q_block), k_far, start + LANES, True, None)
            q_block = jnp.where(first, q_block, q_own[h, start : start + LANES, :])
            square, late_prompt = add_scores(query_block(q_block), k_first, rows, False, None)
            own, own_prompt = totals[h, :, at], prompts[h, :, at]
            early = jnp.where(first, own, other)
            late = square + jnp.where(first, other, own)
            early_prompt = jnp.where(first, own_prompt, far_prompt)
            early = early_prompt / jnp.sum(early, axis=0, keepdims=True)
            late = late_prompt / jnp.sum(late, axis=0, keepdims=True)
            for slot, scaled in enumerate((jnp.where(first, early, late), jnp.where(first, late, early))):
                scaled = scaled.astype(jnp.bfloat16)
                column = slot * rows + start
                for j in range(group):
                    prob[h, j, :, column : column + LANES] = scaled[:, j * LANES : (j + 1) * LANES]
        return carry

    lax.fori_loop(0, heads, step, 0)
    load.wait()


def value_kernel(prob, g_own, g_far, mine, theirs):
    heads, group, _, rows = prob.shape
    rows = rows // 2
    width = group * HEAD_DIM
    first = lax.axis_index("seq") == 0

    def step(h):
        at_k = slice(h * HEAD_DIM, (h + 1) * HEAD_DIM)
        at_g = slice(h * width, (h + 1) * width)
        whole = None
        for slot, g in enumerate((g_own[:, at_g], g_far[:, at_g])):
            term = jnp.dot(
                jnp.concatenate(
                    [prob[h, j, :, slot * rows : (slot + 1) * rows] for j in range(group)], axis=0
                ),
                g,
                preferred_element_type=jnp.float32,
            )
            whole = term if whole is None else whole + term
        value = None
        for j in range(group):
            part = whole[j * PROMPT : (j + 1) * PROMPT, j * HEAD_DIM : (j + 1) * HEAD_DIM]
            value = part if value is None else value + part
        value = value.astype(jnp.bfloat16)
        low, high = value[: PROMPT // 2], value[PROMPT // 2 :]
        mine[:, at_k] = jnp.where(first, low, high)
        theirs[:, at_k] = jnp.where(first, high, low)

    for h in range(heads):
        step(h)


def prompt_value_grad(totals, prompts, q_own, k_own, g, far, g_far, weight):
    heads, rows, width = q_own.shape
    group = width // HEAD_DIM
    weights = [] if weight is None else [weight]
    prob, g_own, *turned = pl.pallas_call(
        functools.partial(attention_kernel, turn=bool(weights)),
        in_specs=[VMEM] * 4 + [HBM, VMEM] + [VMEM] * len(weights),
        out_specs=[VMEM] * (2 + len(weights)),
        out_shape=[
            jax.ShapeDtypeStruct((heads, group, PROMPT, 2 * rows), jnp.bfloat16),
            jax.ShapeDtypeStruct((rows, heads * width), jnp.bfloat16),
        ]
        + [jax.ShapeDtypeStruct(w.shape[::-1], w.dtype) for w in weights],
        scratch_shapes=[
            pltpu.VMEM((rows, HEAD_DIM), jnp.bfloat16),
            pltpu.SemaphoreType.DMA((1,)),
        ],
        compiler_params=pltpu.CompilerParams(vmem_limit_bytes=16 * 1024 * 1024),
        cost_estimate=pl.CostEstimate(
            flops=heads * group * 6 * rows * rows * HEAD_DIM,
            bytes_accessed=6 * rows * heads * width,
            transcendentals=heads * group * 3 * rows * rows,
        ),
    )(totals, prompts, q_own, k_own, g, far, *weights)
    mine, theirs = pl.pallas_call(
        value_kernel,
        in_specs=[VMEM] * 3,
        out_specs=[VMEM] * 2,
        out_shape=[jax.ShapeDtypeStruct((PROMPT // 2, heads * HEAD_DIM), jnp.bfloat16)] * 2,
        compiler_params=pltpu.CompilerParams(vmem_limit_bytes=16 * 1024 * 1024),
        cost_estimate=pl.CostEstimate(
            flops=4 * heads * group * PROMPT * rows * HEAD_DIM,
            bytes_accessed=6 * rows * heads * width,
            transcendentals=0,
        ),
    )(prob, g_own, g_far)
    return mine, theirs, turned


def sibling_kernel(q, k, out, q_head, k_head, done):
    seq = lax.axis_index("seq")
    copies, to = [], 0
    for i, source in enumerate((q, k)):
        half = source.shape[1] // 2
        columns = pl.ds(pl.multiple_of((1 - seq) * half, LANES), half)
        copies.append(
            pltpu.make_async_copy(
                source.at[:, columns], out.at[:, to : to + half], done.at[i]
            )
        )
        to += half
    for i, (source, target) in enumerate(((q, q_head), (k, k_head))):
        start = pl.multiple_of(seq * (source.shape[1] // 2), LANES)
        copies.append(
            pltpu.make_async_copy(
                source.at[:, pl.ds(start, target.shape[1])], target, done.at[2 + i]
            )
        )
    for copy in copies:
        copy.start()
    for copy in copies:
        copy.wait()


def for_sibling(q, k):
    rows = q.shape[0]
    width = q.shape[1] * HEAD_DIM // k.shape[1]
    return pl.pallas_call(
        sibling_kernel,
        in_specs=[HBM] * 2,
        out_specs=[VMEM] * 3,
        out_shape=[
            jax.ShapeDtypeStruct((rows, (q.shape[1] + k.shape[1]) // 2), jnp.bfloat16),
            jax.ShapeDtypeStruct((rows, width), jnp.bfloat16),
            jax.ShapeDtypeStruct((rows, HEAD_DIM), jnp.bfloat16),
        ],
        scratch_shapes=[pltpu.SemaphoreType.DMA((4,))],
        compiler_params=pltpu.CompilerParams(vmem_limit_bytes=16 * 1024 * 1024),
    )(q, k)


def partial_kernel(*refs):
    blocks, weight, out = refs[:-2], refs[-2], refs[-1]
    rows = blocks[0].shape[0]
    total = jnp.dot(
        jnp.concatenate([block[...] for block in blocks], axis=0),
        weight[...],
        preferred_element_type=jnp.float32,
    )
    for i in range(len(blocks)):
        out[i] = total[i * rows : (i + 1) * rows].astype(out.dtype)


def combine_kernel(near, far, grad, squares, *, steps):
    example = lax.broadcasted_iota(jnp.int32, squares.shape, 0)
    by_example = jnp.zeros(squares.shape, jnp.float32)
    for i, step in enumerate(steps):
        folded = None
        for at in range(0, near.shape[2], LANES):
            part = near[i, :, at : at + LANES].astype(jnp.float32)
            part = part + far[i, :, at : at + LANES].astype(jnp.float32)
            grad[i, :, at : at + LANES] = part
            folded = part * part if folded is None else folded + part * part
        folded = jnp.sum(folded, axis=0, keepdims=True)
        by_example = jnp.where(example == (lax.axis_index("dp") ^ step), folded, by_example)
    squares[...] = by_example


def select_kernel(tenant_of, owner_of, counts, select, count, *, examples):
    dp_index = lax.axis_index("dp")
    for step in range(examples):
        owner = owner_of[tenant_of[dp_index ^ step]]
        for k in range(examples):
            hit = jnp.where(owner == (dp_index ^ k), 1.0, 0.0)
            row = k * examples + step
            select[row : row + 1, :] = jnp.full((1, LANES), hit, jnp.float32)
    total = 0
    for slot in range(examples):
        total = total + jnp.where(owner_of[slot] == dp_index, counts[slot], 0)
    count[...] = jnp.full((1, LANES), total.astype(jnp.float32), jnp.float32)


def add_kernel(left, right, out):
    out[...] = left[...] + right[...]


def share_kernel(select, norms, *refs, groups):
    examples = sum(len(steps) for steps in groups)
    grads = refs[: len(groups)]
    outs, scales = refs[len(groups) : -1], refs[-1]
    norm_sq = jnp.sum(norms[...], axis=1, keepdims=True)
    scales[...] = jnp.broadcast_to(1.0 / jnp.maximum(1.0, jnp.sqrt(norm_sq)), scales.shape)
    dp_index = lax.axis_index("dp")
    scale = [scales[pl.ds(dp_index ^ step, 1), :] for step in range(examples)]
    for k in range(examples):
        factor = [
            scale[step] * select[k * examples + step : k * examples + step + 1, :]
            for step in range(examples)
        ]
        for at in range(0, outs[k].shape[1], LANES):
            total = None
            for ref, steps in zip(grads, groups):
                for i, step in enumerate(steps):
                    term = ref[i, :, at : at + LANES] * factor[step]
                    total = term if total is None else total + term
            outs[k][:, at : at + LANES] = total.astype(jnp.bfloat16)


def update_kernel(count, share, noise, *refs, step):
    out, stage, done = refs[-3:]
    columns = share.shape[1]
    base = pl.multiple_of((lax.axis_index("dp") ^ step) * columns, LANES)
    for at in range(0, columns, LANES):
        part = share[:, at : at + LANES].astype(jnp.float32)
        added = noise[0, :, pl.ds(pl.multiple_of(base + at, LANES), LANES)]
        stage[:, at : at + LANES] = (math.sqrt(PROMPT * D) * part + added) / count[...]
    copy = pltpu.make_async_copy(stage, out.at[0, :, pl.ds(base, columns)], done.at[0])
    copy.start()
    copy.wait()


def to_dp(array, dp):
    return [array] + [lax.ppermute(array, "dp", xor_pairs(dp, step)) for step in range(1, dp)]


def tail_by_permutes(value_grad, weight, tenant_of, owner_of, counts, noise, sizes):
    dp = sizes["dp"]
    columns = weight.shape[1]
    rows = PROMPT // 2
    swap = xor_pairs(2, 1)
    small = pltpu.CompilerParams(vmem_limit_bytes=16 * 1024 * 1024)
    blocks = to_dp(value_grad, dp)
    groups = [[step] for step in [0] + arrival("blocks", dp)]
    tenant_of, blocks[-1] = lax.optimization_barrier((tenant_of, blocks[-1]))
    select, count = pl.pallas_call(
        functools.partial(select_kernel, examples=dp),
        in_specs=[SMEM] * 3,
        out_specs=[VMEM] * 2,
        out_shape=[
            jax.ShapeDtypeStruct((dp * dp, LANES), jnp.float32),
            jax.ShapeDtypeStruct((1, LANES), jnp.float32),
        ],
        compiler_params=small,
    )(tenant_of, owner_of, counts)
    grads, squares = [], None
    nears = []
    for steps in groups:
        if len(nears) > 1:
            blocks[steps[0]], _ = lax.optimization_barrier((blocks[steps[0]], nears[-1]))
        shape = (len(steps), rows, columns)
        near = pl.pallas_call(
            partial_kernel,
            in_specs=[VMEM] * (len(steps) + 1),
            out_specs=VMEM,
            out_shape=jax.ShapeDtypeStruct(shape, PARTIAL_TYPE),
            compiler_params=small,
            cost_estimate=pl.CostEstimate(
                flops=2 * len(steps) * rows * weight.size,
                bytes_accessed=2 * weight.size,
                transcendentals=0,
            ),
        )(*[blocks[step] for step in steps], weight)
        nears.append(near)
        far = lax.ppermute(near, "tensor", swap)
        grad, square = pl.pallas_call(
            functools.partial(combine_kernel, steps=steps),
            in_specs=[VMEM] * 2,
            out_specs=[VMEM] * 2,
            out_shape=[
                jax.ShapeDtypeStruct(shape, jnp.float32),
                jax.ShapeDtypeStruct((8, LANES), jnp.float32),
            ],
            compiler_params=small,
        )(near, far)
        grads.append(grad)
        squares = square if squares is None else squares + square
    norms = to_dp(squares + lax.ppermute(squares, "seq", swap), dp)
    total = norms[0]
    for step in arrival("norms", dp):
        total = pl.pallas_call(
            add_kernel,
            in_specs=[VMEM] * 2,
            out_specs=VMEM,
            out_shape=jax.ShapeDtypeStruct(total.shape, total.dtype),
            compiler_params=small,
        )(total, norms[step])
    shares = pl.pallas_call(
        functools.partial(share_kernel, groups=groups),
        in_specs=[VMEM] * (2 + len(groups)),
        out_specs=[VMEM] * dp,
        out_shape=[jax.ShapeDtypeStruct((rows, columns), jnp.bfloat16)] * dp,
        scratch_shapes=[pltpu.VMEM((8, LANES), jnp.float32)],
        compiler_params=small,
    )(select, total, *grads)
    arrived = [shares[0]] + [
        lax.ppermute(shares[step], "dp", xor_pairs(dp, step)) for step in range(1, dp)
    ]
    result = []
    for step in [0] + arrival("shares", dp):
        result = [
            pl.pallas_call(
                functools.partial(update_kernel, step=step),
                in_specs=[VMEM] * 3 + [ANY] * len(result),
                out_specs=ANY,
                out_shape=jax.ShapeDtypeStruct(noise.shape, jnp.float32),
                input_output_aliases={3: 0} if result else {},
                scratch_shapes=[
                    pltpu.VMEM((rows, columns), jnp.float32),
                    pltpu.SemaphoreType.DMA((1,)),
                ],
                compiler_params=small,
            )(count, arrived[step], noise, *result)
        ]
    return result[0]


def tail_by_collectives(value_grad, weight, tenant_of, owner_of, counts, noise):
    rows = PROMPT // 2
    dp_index = lax.axis_index("dp")
    whole = lax.all_gather(value_grad, "tensor", axis=1, tiled=True)
    whole = lax.all_gather(whole, "dp", axis=0, tiled=True)
    part = lax.all_to_all(weight, "tensor", split_axis=0, concat_axis=1, tiled=True)
    grad = lax.dot_general(whole, part, CONTRACT_LAST, preferred_element_type=jnp.float32)
    grad = grad.reshape(-1, rows, part.shape[0])
    norm_sq = lax.psum(jnp.sum(grad * grad, axis=(1, 2)), ("dp", "tensor", "seq"))
    clipped = grad / jnp.maximum(1.0, jnp.sqrt(norm_sq))[:, None, None]
    slots = jnp.arange(owner_of.shape[0])
    owner_ex = jnp.sum(
        jnp.where(tenant_of[:, None] == slots[None, :], owner_of[None, :], 0), axis=1
    )
    select = (owner_ex[None, :] == slots[:, None]).astype(jnp.float32)
    sums = jnp.einsum("oe,erc->orc", select, clipped, precision=lax.Precision.HIGHEST)
    sums = lax.all_gather(sums, "tensor", axis=2, tiled=True)
    sums = lax.all_to_all(sums, "dp", split_axis=0, concat_axis=2, tiled=True)
    my_count = jnp.sum(jnp.where(owner_of == dp_index, counts, 0)).astype(jnp.float32)
    return (math.sqrt(PROMPT * D) * sums + noise) / my_count


def body(sizes, queries, keys, out_grad, value_weight, tenant_of, owner_of, counts, noise):
    swap = xor_pairs(2, 1)
    seq_index = lax.axis_index("seq")
    q, k, g = (
        pltpu.with_memory_space_constraint(x[0], pltpu.HBM) for x in (queries, keys, out_grad)
    )

    sent, q_head, k_head = for_sibling(q, k)
    far = lax.ppermute(sent, "seq", swap)
    aligned = value_weight.shape[0] % LANES == 0 and sizes["dp"] in (1, 2, 4, 8)
    permutes = sizes["tensor"] == 2 and aligned
    *own, g_sent = own_triangle(q, k, g, q_head, k_head)
    g_far = lax.ppermute(g_sent, "seq", swap)
    mine, theirs, turned = prompt_value_grad(
        *own, g, far, g_far, value_weight if permutes else None
    )
    other = lax.ppermute(theirs, "seq", swap)
    first = seq_index == 0
    value_grad = jnp.concatenate(
        [jnp.where(first, mine, other), jnp.where(first, other, mine)], axis=1
    )
    if permutes:
        return tail_by_permutes(
            value_grad, turned[0], tenant_of, owner_of, counts, noise, sizes
        )
    return tail_by_collectives(value_grad, value_weight, tenant_of, owner_of, counts, noise)


def solution(mesh):
    return jax.shard_map(
        functools.partial(body, dict(mesh.shape)),
        mesh=mesh,
        in_specs=(
            P(("group", "dp"), "seq", "tensor"),
            P(("group", "dp"), "seq", "tensor"),
            P(("group", "dp"), "seq", "tensor"),
            P("dp", "tensor"),
            P("group"),
            P("group"),
            P("group"),
            P(("group", "dp"), "seq", None),
        ),
        out_specs=P(("group", "dp"), "seq", None),
        check_vma=False,
    )
```

```python
import functools
import math

import jax
import jax.numpy as jnp
from jax import lax
from jax.experimental import pallas as pl
from jax.experimental.pallas import tpu as pltpu
from jax.sharding import PartitionSpec as P

D = 4608
HEAD_DIM = 128
PROMPT = 64
LANES = 128

softcap = 50.0
query_scale = 144.0 ** (-0.5)
TANH_SCALE = query_scale / softcap
EXP2_SCALE = softcap * math.log2(math.e)

PARTIAL_TYPE = jnp.bfloat16


ORDER = {
    "blocks": ((3, 1, 2), (3, 1, 2)),
    "norms": ((3, 2, 1), (3, 2, 1)),
    "shares": ((1, 2, 3), (1, 2, 3)),
}


def order(what, dp):
    return ORDER[what] if dp == 4 else (tuple(range(1, dp)),) * 2


def partner(what, slot, dp):
    here = lax.axis_index("dp")
    if slot == 0:
        return here
    first, second = (steps[slot - 1] for steps in order(what, dp))
    if first == second:
        return here ^ first
    return here ^ jnp.where(lax.axis_index("seq") == 0, first, second)


def to_partner(array, what, slot, dp):
    steps = [steps[slot - 1] for steps in order(what, dp)]
    pairs = [(2 * z + s, 2 * (z ^ step) + s) for z in range(dp) for s, step in enumerate(steps)]
    return lax.ppermute(array, ("dp", "seq"), pairs)


CONTRACT_LAST = (((1,), (1,)), ((), ()))
VMEM = pl.BlockSpec(memory_space=pltpu.VMEM)
SMEM = pl.BlockSpec(memory_space=pltpu.SMEM)
HBM = pl.BlockSpec(memory_space=pltpu.HBM)
ANY = pl.BlockSpec(memory_space=pl.ANY)


def xor_pairs(size, step):
    return [(i, i ^ step) for i in range(size)]


def add_scores(query, keys, count, diagonal, total):
    block = LANES
    lanes = query.shape[0]
    raw = lax.dot_general(
        keys[:count, :], query, CONTRACT_LAST, preferred_element_type=jnp.float32
    )
    prompt = None
    for low in range(0, count, block):
        e = jnp.exp2(jnp.tanh(raw[low : low + block] * TANH_SCALE) * EXP2_SCALE)
        if diagonal and low == count - block:
            key_pos = lax.broadcasted_iota(jnp.int32, (block, block), 0)
            query_pos = lax.broadcasted_iota(jnp.int32, (block, block), 1)
            keep = jnp.concatenate([key_pos <= query_pos] * (lanes // block), axis=1)
            e = jnp.where(keep, e, 0.0)
        if prompt is None:
            prompt = e[:PROMPT]
        part = jnp.sum(e.reshape(block // 8, 8, lanes), axis=0)
        total = part if total is None else total + part
    return total, prompt


def query_block(queries):
    return jnp.concatenate(
        [
            queries[:, at : at + HEAD_DIM] for at in range(0, queries.shape[1], HEAD_DIM)
        ],
        axis=0,
    )


def triangle_kernel(q, k, g, q_head, k_head, totals, prompts, q_own, k_own, g_sent, done):
    heads, rows, width = q_own.shape
    seq = lax.axis_index("seq")
    lanes = width // HEAD_DIM * LANES

    def load(source, target, h, i):
        extent = target.shape[2]
        columns = pl.ds(pl.multiple_of((seq * heads + h) * extent, LANES), extent)
        return pltpu.make_async_copy(source.at[:, columns], target.at[h], done.at[h, i])

    for h in range(1, heads):
        load(k, k_own, h, 0).start()
        load(q, q_own, h, 1).start()
    half = g_sent.shape[1]
    sibling = pl.ds(pl.multiple_of((1 - seq) * half, LANES), half)
    send = pltpu.make_async_copy(g.at[:, sibling], g_sent, done.at[0, 0])
    send.start()

    def triangle(h, queries, keys):
        for i, start in enumerate(range(0, rows, LANES)):
            total, prompt = add_scores(
                query_block(queries[start : start + LANES, :]), keys, start + LANES, True, None
            )
            at = slice(i * lanes, (i + 1) * lanes)
            totals[h, :, at] = total
            prompts[h, :, at] = prompt

    def step(h, carry):
        load(k, k_own, h, 0).wait()
        load(q, q_own, h, 1).wait()
        triangle(h, q_own.at[h], k_own.at[h])
        return carry

    q_own[0] = q_head[...]
    k_own[0] = k_head[...]
    triangle(0, q_head, k_head)
    lax.fori_loop(1, heads, step, 0)
    send.wait()


def own_triangle(q, k, g, q_head, k_head):
    rows = q.shape[0]
    heads = k.shape[1] // (2 * HEAD_DIM)
    width = q.shape[1] // (2 * heads)
    lanes = width // HEAD_DIM * rows
    return pl.pallas_call(
        triangle_kernel,
        in_specs=[HBM] * 3 + [VMEM] * 2,
        out_specs=[VMEM] * 5,
        out_shape=[
            jax.ShapeDtypeStruct((heads, 8, lanes), jnp.float32),
            jax.ShapeDtypeStruct((heads, PROMPT, lanes), jnp.float32),
            jax.ShapeDtypeStruct((heads, rows, width), jnp.bfloat16),
            jax.ShapeDtypeStruct((heads, rows, HEAD_DIM), jnp.bfloat16),
            jax.ShapeDtypeStruct((rows, heads * width), jnp.bfloat16),
        ],
        scratch_shapes=[pltpu.SemaphoreType.DMA((heads, 2))],
        compiler_params=pltpu.CompilerParams(vmem_limit_bytes=16 * 1024 * 1024),
        cost_estimate=pl.CostEstimate(
            flops=2 * heads * lanes * rows * HEAD_DIM,
            bytes_accessed=6 * heads * rows * width,
            transcendentals=heads * lanes * rows,
        ),
    )(q, k, g, q_head, k_head)


def attention_kernel(*refs, turn):
    if turn:
        totals, prompts, q_own, k_own, g, far, weight, prob, g_own, turned, done = refs
    else:
        totals, prompts, q_own, k_own, g, far, prob, g_own, done = refs
    heads, rows, width = q_own.shape
    group = width // HEAD_DIM
    lanes = group * LANES
    seq = lax.axis_index("seq")
    first = seq == 0
    half = g_own.shape[1]
    load = pltpu.make_async_copy(
        g.at[:, pl.ds(pl.multiple_of(seq * half, LANES), half)], g_own, done.at[0]
    )
    load.start()

    def step(h, carry):
        at_q = pl.ds(pl.multiple_of(h * width, LANES), width)
        at_k = pl.ds(pl.multiple_of(heads * width + h * HEAD_DIM, LANES), HEAD_DIM)
        k_far = far.at[:, at_k]
        if turn:
            share = weight.shape[1] // heads
            features = pl.ds(pl.multiple_of(h * share, LANES), share)
            turned[features, :] = weight[:, features].T
        early_keys = jnp.where(first, k_own[h], k_far[...])
        for i, start in enumerate(range(0, rows, LANES)):
            at = slice(i * lanes, (i + 1) * lanes)
            q_block = far[start : start + LANES, at_q]
            other, far_prompt = add_scores(query_block(q_block), k_far, start + LANES, True, None)
            q_block = jnp.where(first, q_block, q_own[h, start : start + LANES, :])
            square, late_prompt = add_scores(query_block(q_block), early_keys, rows, False, None)
            own, own_prompt = totals[h, :, at], prompts[h, :, at]
            early = jnp.where(first, own, other)
            late = square + jnp.where(first, other, own)
            early_prompt = jnp.where(first, own_prompt, far_prompt)
            early = early_prompt / jnp.sum(early, axis=0, keepdims=True)
            late = late_prompt / jnp.sum(late, axis=0, keepdims=True)
            for slot, scaled in enumerate((jnp.where(first, early, late), jnp.where(first, late, early))):
                scaled = scaled.astype(jnp.bfloat16)
                column = slot * rows + start
                for j in range(group):
                    prob[h, j, :, column : column + LANES] = scaled[:, j * LANES : (j + 1) * LANES]
        return carry

    lax.fori_loop(0, heads, step, 0, unroll=2 if heads % 2 == 0 else 1)
    load.wait()


def value_kernel(prob, g_own, g_far, mine, theirs):
    heads, group, _, rows = prob.shape
    rows = rows // 2
    width = group * HEAD_DIM
    first = lax.axis_index("seq") == 0

    def step(h):
        at_k = slice(h * HEAD_DIM, (h + 1) * HEAD_DIM)
        at_g = slice(h * width, (h + 1) * width)
        whole = None
        for slot, g in enumerate((g_own[:, at_g], g_far[:, at_g])):
            term = jnp.dot(
                jnp.concatenate(
                    [prob[h, j, :, slot * rows : (slot + 1) * rows] for j in range(group)], axis=0
                ),
                g,
                preferred_element_type=jnp.float32,
            )
            whole = term if whole is None else whole + term
        value = None
        for j in range(group):
            part = whole[j * PROMPT : (j + 1) * PROMPT, j * HEAD_DIM : (j + 1) * HEAD_DIM]
            value = part if value is None else value + part
        value = value.astype(jnp.bfloat16)
        low, high = value[: PROMPT // 2], value[PROMPT // 2 :]
        mine[:, at_k] = jnp.where(first, low, high)
        theirs[:, at_k] = jnp.where(first, high, low)

    for h in range(heads):
        step(h)


def prompt_value_grad(totals, prompts, q_own, k_own, g, far, g_far, weight):
    heads, rows, width = q_own.shape
    group = width // HEAD_DIM
    weights = [] if weight is None else [weight]
    prob, g_own, *turned = pl.pallas_call(
        functools.partial(attention_kernel, turn=bool(weights)),
        in_specs=[VMEM] * 4 + [HBM, VMEM] + [VMEM] * len(weights),
        out_specs=[VMEM] * (2 + len(weights)),
        out_shape=[
            jax.ShapeDtypeStruct((heads, group, PROMPT, 2 * rows), jnp.bfloat16),
            jax.ShapeDtypeStruct((rows, heads * width), jnp.bfloat16),
        ]
        + [jax.ShapeDtypeStruct(w.shape[::-1], w.dtype) for w in weights],
        scratch_shapes=[pltpu.SemaphoreType.DMA((1,))],
        compiler_params=pltpu.CompilerParams(vmem_limit_bytes=16 * 1024 * 1024),
        cost_estimate=pl.CostEstimate(
            flops=heads * group * 6 * rows * rows * HEAD_DIM,
            bytes_accessed=6 * rows * heads * width,
            transcendentals=heads * group * 3 * rows * rows,
        ),
    )(totals, prompts, q_own, k_own, g, far, *weights)
    mine, theirs = pl.pallas_call(
        value_kernel,
        in_specs=[VMEM] * 3,
        out_specs=[VMEM] * 2,
        out_shape=[jax.ShapeDtypeStruct((PROMPT // 2, heads * HEAD_DIM), jnp.bfloat16)] * 2,
        compiler_params=pltpu.CompilerParams(vmem_limit_bytes=16 * 1024 * 1024),
        cost_estimate=pl.CostEstimate(
            flops=4 * heads * group * PROMPT * rows * HEAD_DIM,
            bytes_accessed=6 * rows * heads * width,
            transcendentals=0,
        ),
    )(prob, g_own, g_far)
    return mine, theirs, turned


def sibling_kernel(q, k, out, q_head, k_head, done):
    seq = lax.axis_index("seq")
    copies, to = [], 0
    for i, source in enumerate((q, k)):
        half = source.shape[1] // 2
        columns = pl.ds(pl.multiple_of((1 - seq) * half, LANES), half)
        copies.append(
            pltpu.make_async_copy(
                source.at[:, columns], out.at[:, to : to + half], done.at[i]
            )
        )
        to += half
    for i, (source, target) in enumerate(((q, q_head), (k, k_head))):
        start = pl.multiple_of(seq * (source.shape[1] // 2), LANES)
        copies.append(
            pltpu.make_async_copy(
                source.at[:, pl.ds(start, target.shape[1])], target, done.at[2 + i]
            )
        )
    for copy in copies:
        copy.start()
    for copy in copies:
        copy.wait()


def for_sibling(q, k):
    rows = q.shape[0]
    width = q.shape[1] * HEAD_DIM // k.shape[1]
    return pl.pallas_call(
        sibling_kernel,
        in_specs=[HBM] * 2,
        out_specs=[VMEM] * 3,
        out_shape=[
            jax.ShapeDtypeStruct((rows, (q.shape[1] + k.shape[1]) // 2), jnp.bfloat16),
            jax.ShapeDtypeStruct((rows, width), jnp.bfloat16),
            jax.ShapeDtypeStruct((rows, HEAD_DIM), jnp.bfloat16),
        ],
        scratch_shapes=[pltpu.SemaphoreType.DMA((4,))],
        compiler_params=pltpu.CompilerParams(vmem_limit_bytes=16 * 1024 * 1024),
    )(q, k)


def partial_kernel(block, weight, out):
    total = jnp.dot(block[...], weight[...], preferred_element_type=jnp.float32)
    out[...] = total.astype(out.dtype)


def combine_kernel(near, far, grad, squares, *, slot, dp):
    folded = None
    for at in range(0, near.shape[1], LANES):
        part = near[:, at : at + LANES].astype(jnp.float32)
        part = part + far[:, at : at + LANES].astype(jnp.float32)
        grad[:, at : at + LANES] = part
        folded = part * part if folded is None else folded + part * part
    folded = jnp.sum(folded, axis=0, keepdims=True)
    example = lax.broadcasted_iota(jnp.int32, squares.shape, 0)
    squares[...] = jnp.where(example == partner("blocks", slot, dp), folded, 0.0)


def select_kernel(tenant_of, owner_of, counts, select, count, *, dp):
    for j in range(dp):
        owner = owner_of[tenant_of[partner("blocks", j, dp)]]
        for i in range(dp):
            hit = jnp.where(owner == partner("shares", i, dp), 1.0, 0.0)
            row = i * dp + j
            select[row : row + 1, :] = jnp.full((1, LANES), hit, jnp.float32)
    total = 0
    for slot in range(dp):
        total = total + jnp.where(owner_of[slot] == lax.axis_index("dp"), counts[slot], 0)
    count[...] = jnp.full((1, LANES), total.astype(jnp.float32), jnp.float32)


def add_kernel(left, right, out):
    out[...] = left[...] + right[...]


def share_kernel(select, norms, *refs, dp):
    grads, outs, scales = refs[:dp], refs[dp : 2 * dp], refs[-1]
    norm_sq = jnp.sum(norms[...], axis=1, keepdims=True)
    scales[...] = jnp.broadcast_to(1.0 / jnp.maximum(1.0, jnp.sqrt(norm_sq)), scales.shape)
    scale = [scales[pl.ds(partner("blocks", j, dp), 1), :] for j in range(dp)]
    for i, out in enumerate(outs):
        factor = [scale[j] * select[i * dp + j : i * dp + j + 1, :] for j in range(dp)]
        for at in range(0, out.shape[1], LANES):
            total = None
            for grad, weight in zip(grads, factor):
                term = grad[:, at : at + LANES] * weight
                total = term if total is None else total + term
            out[:, at : at + LANES] = total.astype(jnp.bfloat16)


def update_kernel(count, share, noise, *refs, slot, dp):
    out, stage, done = refs[-3:]
    columns = share.shape[1]
    base = pl.multiple_of(partner("shares", slot, dp) * columns, LANES)
    for at in range(0, columns, LANES):
        part = share[:, at : at + LANES].astype(jnp.float32)
        added = noise[0, :, pl.ds(pl.multiple_of(base + at, LANES), LANES)]
        stage[:, at : at + LANES] = (math.sqrt(PROMPT * D) * part + added) / count[...]
    copy = pltpu.make_async_copy(stage, out.at[0, :, pl.ds(base, columns)], done.at[0])
    copy.start()
    copy.wait()


def tail_by_permutes(value_grad, weight, tenant_of, owner_of, counts, noise, sizes):
    dp = sizes["dp"]
    columns = weight.shape[1]
    rows = PROMPT // 2
    swap = xor_pairs(2, 1)
    small = pltpu.CompilerParams(vmem_limit_bytes=16 * 1024 * 1024)

    def kernel(body, operands, outs, scalar=False, **static):
        return pl.pallas_call(
            functools.partial(body, **static),
            in_specs=[SMEM if scalar else VMEM] * len(operands),
            out_specs=[VMEM] * len(outs),
            out_shape=[jax.ShapeDtypeStruct(shape, dtype) for shape, dtype in outs],
            compiler_params=small,
        )(*operands)

    blocks = [value_grad]
    blocks += [to_partner(value_grad, "blocks", slot, dp) for slot in range(1, dp)]
    tenant_of, blocks[1] = lax.optimization_barrier((tenant_of, blocks[1]))
    select, count = kernel(
        select_kernel,
        (tenant_of, owner_of, counts),
        [((dp * dp, LANES), jnp.float32), ((1, LANES), jnp.float32)],
        scalar=True,
        dp=dp,
    )
    grads, squares, near = [], None, None
    for slot, block in enumerate(blocks):
        if slot > 1:
            block, _ = lax.optimization_barrier((block, near))
        (near,) = pl.pallas_call(
            partial_kernel,
            in_specs=[VMEM] * 2,
            out_specs=[VMEM],
            out_shape=[jax.ShapeDtypeStruct((rows, columns), PARTIAL_TYPE)],
            compiler_params=small,
            cost_estimate=pl.CostEstimate(
                flops=2 * rows * weight.size, bytes_accessed=2 * weight.size, transcendentals=0
            ),
        )(block, weight)
        far = lax.ppermute(near, "tensor", swap)
        grad, square = kernel(
            combine_kernel,
            (near, far),
            [((rows, columns), jnp.float32), ((8, LANES), jnp.float32)],
            slot=slot,
            dp=dp,
        )
        grads.append(grad)
        squares = square if squares is None else squares + square
    squares = squares + lax.ppermute(squares, "seq", swap)
    total = squares
    for slot in range(1, dp):
        other = to_partner(squares, "norms", slot, dp)
        (total,) = kernel(add_kernel, (total, other), [((8, LANES), jnp.float32)])
    shares = pl.pallas_call(
        functools.partial(share_kernel, dp=dp),
        in_specs=[VMEM] * (2 + dp),
        out_specs=[VMEM] * dp,
        out_shape=[jax.ShapeDtypeStruct((rows, columns), jnp.bfloat16)] * dp,
        scratch_shapes=[pltpu.VMEM((8, LANES), jnp.float32)],
        compiler_params=small,
    )(select, total, *grads)
    result = []
    for slot, share in enumerate(shares):
        if slot:
            share = to_partner(share, "shares", slot, dp)
        result = [
            pl.pallas_call(
                functools.partial(update_kernel, slot=slot, dp=dp),
                in_specs=[VMEM] * 3 + [ANY] * len(result),
                out_specs=ANY,
                out_shape=jax.ShapeDtypeStruct(noise.shape, jnp.float32),
                input_output_aliases={3: 0} if result else {},
                scratch_shapes=[
                    pltpu.VMEM((rows, columns), jnp.float32),
                    pltpu.SemaphoreType.DMA((1,)),
                ],
                compiler_params=small,
            )(count, share, noise, *result)
        ]
    return result[0]


def tail_by_collectives(value_grad, weight, tenant_of, owner_of, counts, noise):
    rows = PROMPT // 2
    dp_index = lax.axis_index("dp")
    whole = lax.all_gather(value_grad, "tensor", axis=1, tiled=True)
    whole = lax.all_gather(whole, "dp", axis=0, tiled=True)
    part = lax.all_to_all(weight, "tensor", split_axis=0, concat_axis=1, tiled=True)
    grad = lax.dot_general(whole, part, CONTRACT_LAST, preferred_element_type=jnp.float32)
    grad = grad.reshape(-1, rows, part.shape[0])
    norm_sq = lax.psum(jnp.sum(grad * grad, axis=(1, 2)), ("dp", "tensor", "seq"))
    clipped = grad / jnp.maximum(1.0, jnp.sqrt(norm_sq))[:, None, None]
    slots = jnp.arange(owner_of.shape[0])
    owner_ex = jnp.sum(
        jnp.where(tenant_of[:, None] == slots[None, :], owner_of[None, :], 0), axis=1
    )
    select = (owner_ex[None, :] == slots[:, None]).astype(jnp.float32)
    sums = jnp.einsum("oe,erc->orc", select, clipped, precision=lax.Precision.HIGHEST)
    sums = lax.all_gather(sums, "tensor", axis=2, tiled=True)
    sums = lax.all_to_all(sums, "dp", split_axis=0, concat_axis=2, tiled=True)
    my_count = jnp.sum(jnp.where(owner_of == dp_index, counts, 0)).astype(jnp.float32)
    return (math.sqrt(PROMPT * D) * sums + noise) / my_count


def body(sizes, queries, keys, out_grad, value_weight, tenant_of, owner_of, counts, noise):
    swap = xor_pairs(2, 1)
    seq_index = lax.axis_index("seq")
    q, k, g = (
        pltpu.with_memory_space_constraint(x[0], pltpu.HBM) for x in (queries, keys, out_grad)
    )

    sent, q_head, k_head = for_sibling(q, k)
    far = lax.ppermute(sent, "seq", swap)
    aligned = value_weight.shape[0] % LANES == 0 and sizes["dp"] in (1, 2, 4, 8)
    permutes = sizes["tensor"] == 2 and aligned
    *own, g_sent = own_triangle(q, k, g, q_head, k_head)
    g_far = lax.ppermute(g_sent, "seq", swap)
    mine, theirs, turned = prompt_value_grad(
        *own, g, far, g_far, value_weight if permutes else None
    )
    other = lax.ppermute(theirs, "seq", swap)
    first = seq_index == 0
    value_grad = jnp.concatenate(
        [jnp.where(first, mine, other), jnp.where(first, other, mine)], axis=1
    )
    if permutes:
        return tail_by_permutes(
            value_grad, turned[0], tenant_of, owner_of, counts, noise, sizes
        )
    return tail_by_collectives(value_grad, value_weight, tenant_of, owner_of, counts, noise)


def solution(mesh):
    return jax.shard_map(
        functools.partial(body, dict(mesh.shape)),
        mesh=mesh,
        in_specs=(
            P(("group", "dp"), "seq", "tensor"),
            P(("group", "dp"), "seq", "tensor"),
            P(("group", "dp"), "seq", "tensor"),
            P("dp", "tensor"),
            P("group"),
            P("group"),
            P("group"),
            P(("group", "dp"), "seq", None),
        ),
        out_specs=P(("group", "dp"), "seq", None),
        check_vma=False,
    )
```

```python
import functools
import math

import jax
import jax.numpy as jnp
from jax import lax
from jax.experimental import pallas as pl
from jax.experimental.pallas import tpu as pltpu
from jax.sharding import PartitionSpec as P

D = 4608
HEAD_DIM = 128
PROMPT = 64
LANES = 128

softcap = 50.0
query_scale = 144.0 ** (-0.5)
TANH_SCALE = query_scale / softcap
EXP2_SCALE = softcap * math.log2(math.e)

PARTIAL_TYPE = jnp.bfloat16


ORDER = {
    "blocks": ((3, 1, 2), (3, 1, 2)),
    "norms": ((3, 2, 1), (3, 2, 1)),
    "shares": ((1, 2, 3), (1, 2, 3)),
}


def order(what, dp):
    return ORDER[what] if dp == 4 else (tuple(range(1, dp)),) * 2


def partner(what, slot, dp):
    here = lax.axis_index("dp")
    if slot == 0:
        return here
    first, second = (steps[slot - 1] for steps in order(what, dp))
    if first == second:
        return here ^ first
    return here ^ jnp.where(lax.axis_index("seq") == 0, first, second)


def to_partner(array, what, slot, dp):
    steps = [steps[slot - 1] for steps in order(what, dp)]
    pairs = [(2 * z + s, 2 * (z ^ step) + s) for z in range(dp) for s, step in enumerate(steps)]
    return lax.ppermute(array, ("dp", "seq"), pairs)


CONTRACT_LAST = (((1,), (1,)), ((), ()))
VMEM = pl.BlockSpec(memory_space=pltpu.VMEM)
SMEM = pl.BlockSpec(memory_space=pltpu.SMEM)
HBM = pl.BlockSpec(memory_space=pltpu.HBM)
ANY = pl.BlockSpec(memory_space=pl.ANY)


def xor_pairs(size, step):
    return [(i, i ^ step) for i in range(size)]


def add_scores(query, keys, count, diagonal, total):
    block = LANES
    lanes = query.shape[0]
    raw = lax.dot_general(
        keys[:count, :], query, CONTRACT_LAST, preferred_element_type=jnp.float32
    )
    prompt = None
    for low in range(0, count, block):
        e = jnp.exp2(jnp.tanh(raw[low : low + block] * TANH_SCALE) * EXP2_SCALE)
        if diagonal and low == count - block:
            key_pos = lax.broadcasted_iota(jnp.int32, (block, block), 0)
            query_pos = lax.broadcasted_iota(jnp.int32, (block, block), 1)
            keep = jnp.concatenate([key_pos <= query_pos] * (lanes // block), axis=1)
            e = jnp.where(keep, e, 0.0)
        if prompt is None:
            prompt = e[:PROMPT]
        part = jnp.sum(e.reshape(block // 8, 8, lanes), axis=0)
        total = part if total is None else total + part
    return total, prompt


def query_block(queries):
    return jnp.concatenate(
        [
            queries[:, at : at + HEAD_DIM] for at in range(0, queries.shape[1], HEAD_DIM)
        ],
        axis=0,
    )


def triangle_kernel(q, k, g, q_head, k_head, totals, prompts, q_own, k_own, g_sent, done):
    heads, rows, width = q_own.shape
    seq = lax.axis_index("seq")
    lanes = width // HEAD_DIM * LANES

    def load(source, target, h, i):
        extent = target.shape[2]
        columns = pl.ds(pl.multiple_of((seq * heads + h) * extent, LANES), extent)
        return pltpu.make_async_copy(source.at[:, columns], target.at[h], done.at[h, i])

    for h in range(1, heads):
        load(k, k_own, h, 0).start()
        load(q, q_own, h, 1).start()
    half = g_sent.shape[1]
    sibling = pl.ds(pl.multiple_of((1 - seq) * half, LANES), half)
    send = pltpu.make_async_copy(g.at[:, sibling], g_sent, done.at[0, 0])
    send.start()

    def triangle(h, queries, keys):
        for i, start in enumerate(range(0, rows, LANES)):
            total, prompt = add_scores(
                query_block(queries[start : start + LANES, :]), keys, start + LANES, True, None
            )
            at = slice(i * lanes, (i + 1) * lanes)
            totals[h, :, at] = total
            prompts[h, :, at] = prompt

    def step(h, carry):
        load(k, k_own, h, 0).wait()
        load(q, q_own, h, 1).wait()
        triangle(h, q_own.at[h], k_own.at[h])
        return carry

    q_own[0] = q_head[...]
    k_own[0] = k_head[...]
    triangle(0, q_head, k_head)
    lax.fori_loop(1, heads, step, 0)
    send.wait()


def own_triangle(q, k, g, q_head, k_head):
    rows = q.shape[0]
    heads = k.shape[1] // (2 * HEAD_DIM)
    width = q.shape[1] // (2 * heads)
    lanes = width // HEAD_DIM * rows
    return pl.pallas_call(
        triangle_kernel,
        in_specs=[HBM] * 3 + [VMEM] * 2,
        out_specs=[VMEM] * 5,
        out_shape=[
            jax.ShapeDtypeStruct((heads, 8, lanes), jnp.float32),
            jax.ShapeDtypeStruct((heads, PROMPT, lanes), jnp.float32),
            jax.ShapeDtypeStruct((heads, rows, width), jnp.bfloat16),
            jax.ShapeDtypeStruct((heads, rows, HEAD_DIM), jnp.bfloat16),
            jax.ShapeDtypeStruct((rows, heads * width), jnp.bfloat16),
        ],
        scratch_shapes=[pltpu.SemaphoreType.DMA((heads, 2))],
        compiler_params=pltpu.CompilerParams(vmem_limit_bytes=16 * 1024 * 1024),
        cost_estimate=pl.CostEstimate(
            flops=2 * heads * lanes * rows * HEAD_DIM,
            bytes_accessed=6 * heads * rows * width,
            transcendentals=heads * lanes * rows,
        ),
    )(q, k, g, q_head, k_head)


def attention_kernel(*refs, turn):
    if turn:
        totals, prompts, q_own, k_own, g, far, weight, prob, g_own, turned, done = refs
    else:
        totals, prompts, q_own, k_own, g, far, prob, g_own, done = refs
    heads, rows, width = q_own.shape
    group = width // HEAD_DIM
    lanes = group * LANES
    seq = lax.axis_index("seq")
    first = seq == 0
    half = g_own.shape[1]
    load = pltpu.make_async_copy(
        g.at[:, pl.ds(pl.multiple_of(seq * half, LANES), half)], g_own, done.at[0]
    )
    load.start()

    def step(h, carry):
        at_q = pl.ds(pl.multiple_of(h * width, LANES), width)
        at_k = pl.ds(pl.multiple_of(heads * width + h * HEAD_DIM, LANES), HEAD_DIM)
        k_far = far.at[:, at_k]
        if turn:
            share = weight.shape[1] // heads
            features = pl.ds(pl.multiple_of(h * share, LANES), share)
            turned[features, :] = weight[:, features].T
        early_keys = jnp.where(first, k_own[h], k_far[...])
        for i, start in enumerate(range(0, rows, LANES)):
            at = slice(i * lanes, (i + 1) * lanes)
            q_block = far[start : start + LANES, at_q]
            other, far_prompt = add_scores(query_block(q_block), k_far, start + LANES, True, None)
            q_block = jnp.where(first, q_block, q_own[h, start : start + LANES, :])
            square, late_prompt = add_scores(query_block(q_block), early_keys, rows, False, None)
            own, own_prompt = totals[h, :, at], prompts[h, :, at]
            early = jnp.where(first, own, other)
            late = square + jnp.where(first, other, own)
            early_prompt = jnp.where(first, own_prompt, far_prompt)
            early = early_prompt / jnp.sum(early, axis=0, keepdims=True)
            late = late_prompt / jnp.sum(late, axis=0, keepdims=True)
            for slot, scaled in enumerate((jnp.where(first, early, late), jnp.where(first, late, early))):
                scaled = scaled.astype(jnp.bfloat16)
                column = slot * rows + start
                for j in range(group):
                    prob[h, j, :, column : column + LANES] = scaled[:, j * LANES : (j + 1) * LANES]
        return carry

    lax.fori_loop(0, heads, step, 0, unroll=2 if heads % 2 == 0 else 1)
    load.wait()


def value_kernel(prob, g_own, g_far, mine, theirs):
    heads, group, _, rows = prob.shape
    rows = rows // 2
    width = group * HEAD_DIM
    first = lax.axis_index("seq") == 0

    def step(h):
        at_k = slice(h * HEAD_DIM, (h + 1) * HEAD_DIM)
        at_g = slice(h * width, (h + 1) * width)
        whole = None
        for slot, g in enumerate((g_own[:, at_g], g_far[:, at_g])):
            term = jnp.dot(
                jnp.concatenate(
                    [prob[h, j, :, slot * rows : (slot + 1) * rows] for j in range(group)], axis=0
                ),
                g,
                preferred_element_type=jnp.float32,
            )
            whole = term if whole is None else whole + term
        value = None
        for j in range(group):
            part = whole[j * PROMPT : (j + 1) * PROMPT, j * HEAD_DIM : (j + 1) * HEAD_DIM]
            value = part if value is None else value + part
        value = value.astype(jnp.bfloat16)
        low, high = value[: PROMPT // 2], value[PROMPT // 2 :]
        mine[:, at_k] = jnp.where(first, low, high)
        theirs[:, at_k] = jnp.where(first, high, low)

    for h in range(heads):
        step(h)


def prompt_value_grad(totals, prompts, q_own, k_own, g, far, g_far, weight):
    heads, rows, width = q_own.shape
    group = width // HEAD_DIM
    weights = [] if weight is None else [weight]
    prob, g_own, *turned = pl.pallas_call(
        functools.partial(attention_kernel, turn=bool(weights)),
        in_specs=[VMEM] * 4 + [HBM, VMEM] + [VMEM] * len(weights),
        out_specs=[VMEM] * (2 + len(weights)),
        out_shape=[
            jax.ShapeDtypeStruct((heads, group, PROMPT, 2 * rows), jnp.bfloat16),
            jax.ShapeDtypeStruct((rows, heads * width), jnp.bfloat16),
        ]
        + [jax.ShapeDtypeStruct(w.shape[::-1], w.dtype) for w in weights],
        scratch_shapes=[pltpu.SemaphoreType.DMA((1,))],
        compiler_params=pltpu.CompilerParams(vmem_limit_bytes=16 * 1024 * 1024),
        cost_estimate=pl.CostEstimate(
            flops=heads * group * 6 * rows * rows * HEAD_DIM,
            bytes_accessed=6 * rows * heads * width,
            transcendentals=heads * group * 3 * rows * rows,
        ),
    )(totals, prompts, q_own, k_own, g, far, *weights)
    mine, theirs = pl.pallas_call(
        value_kernel,
        in_specs=[VMEM] * 3,
        out_specs=[VMEM] * 2,
        out_shape=[jax.ShapeDtypeStruct((PROMPT // 2, heads * HEAD_DIM), jnp.bfloat16)] * 2,
        compiler_params=pltpu.CompilerParams(vmem_limit_bytes=16 * 1024 * 1024),
        cost_estimate=pl.CostEstimate(
            flops=4 * heads * group * PROMPT * rows * HEAD_DIM,
            bytes_accessed=6 * rows * heads * width,
            transcendentals=0,
        ),
    )(prob, g_own, g_far)
    return mine, theirs, turned


def sibling_kernel(q, k, out, q_head, k_head, done):
    seq = lax.axis_index("seq")
    copies, to = [], 0
    for i, source in enumerate((q, k)):
        half = source.shape[1] // 2
        columns = pl.ds(pl.multiple_of((1 - seq) * half, LANES), half)
        copies.append(
            pltpu.make_async_copy(
                source.at[:, columns], out.at[:, to : to + half], done.at[i]
            )
        )
        to += half
    for i, (source, target) in enumerate(((q, q_head), (k, k_head))):
        start = pl.multiple_of(seq * (source.shape[1] // 2), LANES)
        copies.append(
            pltpu.make_async_copy(
                source.at[:, pl.ds(start, target.shape[1])], target, done.at[2 + i]
            )
        )
    for copy in copies:
        copy.start()
    for copy in copies:
        copy.wait()


def for_sibling(q, k):
    rows = q.shape[0]
    width = q.shape[1] * HEAD_DIM // k.shape[1]
    return pl.pallas_call(
        sibling_kernel,
        in_specs=[HBM] * 2,
        out_specs=[VMEM] * 3,
        out_shape=[
            jax.ShapeDtypeStruct((rows, (q.shape[1] + k.shape[1]) // 2), jnp.bfloat16),
            jax.ShapeDtypeStruct((rows, width), jnp.bfloat16),
            jax.ShapeDtypeStruct((rows, HEAD_DIM), jnp.bfloat16),
        ],
        scratch_shapes=[pltpu.SemaphoreType.DMA((4,))],
        compiler_params=pltpu.CompilerParams(vmem_limit_bytes=16 * 1024 * 1024),
    )(q, k)


def partial_kernel(block, weight, out):
    total = jnp.dot(block[...], weight[...], preferred_element_type=jnp.float32)
    out[...] = total.astype(out.dtype)


def combine_kernel(near, far, grad, squares, *, slot, dp):
    folded = None
    for at in range(0, near.shape[1], LANES):
        part = near[:, at : at + LANES].astype(jnp.float32)
        part = part + far[:, at : at + LANES].astype(jnp.float32)
        grad[:, at : at + LANES] = part
        folded = part * part if folded is None else folded + part * part
    folded = jnp.sum(folded, axis=0, keepdims=True)
    example = lax.broadcasted_iota(jnp.int32, squares.shape, 0)
    squares[...] = jnp.where(example == partner("blocks", slot, dp), folded, 0.0)


def select_kernel(tenant_of, owner_of, counts, select, count, *, dp):
    for j in range(dp):
        owner = owner_of[tenant_of[partner("blocks", j, dp)]]
        for i in range(dp):
            hit = jnp.where(owner == partner("shares", i, dp), 1.0, 0.0)
            row = i * dp + j
            select[row : row + 1, :] = jnp.full((1, LANES), hit, jnp.float32)
    total = 0
    for slot in range(dp):
        total = total + jnp.where(owner_of[slot] == lax.axis_index("dp"), counts[slot], 0)
    count[...] = jnp.full((1, LANES), total.astype(jnp.float32), jnp.float32)


def add_kernel(left, right, out):
    out[...] = left[...] + right[...]


def share_kernel(select, norms, *refs, slots, dp):
    grads, outs, scales = refs[:dp], refs[dp:-1], refs[-1]
    norm_sq = jnp.sum(norms[...], axis=1, keepdims=True)
    scales[...] = jnp.broadcast_to(1.0 / jnp.maximum(1.0, jnp.sqrt(norm_sq)), scales.shape)
    scale = [scales[pl.ds(partner("blocks", j, dp), 1), :] for j in range(dp)]
    factors = [
        [scale[j] * select[i * dp + j : i * dp + j + 1, :] for j in range(dp)] for i in slots
    ]
    for at in range(0, outs[0].shape[1], LANES):
        parts = [grad[:, at : at + LANES] for grad in grads]
        for out, factor in zip(outs, factors):
            total = None
            for part, weight in zip(parts, factor):
                term = part * weight
                total = term if total is None else total + term
            out[:, at : at + LANES] = total.astype(jnp.bfloat16)


def update_kernel(count, share, noise, *refs, slot, dp):
    out, stage, done = refs[-3:]
    columns = share.shape[1]
    base = pl.multiple_of(partner("shares", slot, dp) * columns, LANES)
    for at in range(0, columns, LANES):
        part = share[:, at : at + LANES].astype(jnp.float32)
        added = noise[0, :, pl.ds(pl.multiple_of(base + at, LANES), LANES)]
        stage[:, at : at + LANES] = (math.sqrt(PROMPT * D) * part + added) / count[...]
    copy = pltpu.make_async_copy(stage, out.at[0, :, pl.ds(base, columns)], done.at[0])
    copy.start()
    copy.wait()


def tail_by_permutes(value_grad, weight, tenant_of, owner_of, counts, noise, sizes):
    dp = sizes["dp"]
    columns = weight.shape[1]
    rows = PROMPT // 2
    swap = xor_pairs(2, 1)
    small = pltpu.CompilerParams(vmem_limit_bytes=16 * 1024 * 1024)

    def kernel(body, operands, outs, scalar=False, **static):
        return pl.pallas_call(
            functools.partial(body, **static),
            in_specs=[SMEM if scalar else VMEM] * len(operands),
            out_specs=[VMEM] * len(outs),
            out_shape=[jax.ShapeDtypeStruct(shape, dtype) for shape, dtype in outs],
            compiler_params=small,
        )(*operands)

    blocks = [value_grad]
    blocks += [to_partner(value_grad, "blocks", slot, dp) for slot in range(1, dp)]
    tenant_of, blocks[1] = lax.optimization_barrier((tenant_of, blocks[1]))
    select, count = kernel(
        select_kernel,
        (tenant_of, owner_of, counts),
        [((dp * dp, LANES), jnp.float32), ((1, LANES), jnp.float32)],
        scalar=True,
        dp=dp,
    )
    grads, squares, near = [], None, None
    for slot, block in enumerate(blocks):
        if slot > 1:
            block, _ = lax.optimization_barrier((block, near))
        (near,) = pl.pallas_call(
            partial_kernel,
            in_specs=[VMEM] * 2,
            out_specs=[VMEM],
            out_shape=[jax.ShapeDtypeStruct((rows, columns), PARTIAL_TYPE)],
            compiler_params=small,
            cost_estimate=pl.CostEstimate(
                flops=2 * rows * weight.size, bytes_accessed=2 * weight.size, transcendentals=0
            ),
        )(block, weight)
        far = lax.ppermute(near, "tensor", swap)
        grad, square = kernel(
            combine_kernel,
            (near, far),
            [((rows, columns), jnp.float32), ((8, LANES), jnp.float32)],
            slot=slot,
            dp=dp,
        )
        grads.append(grad)
        squares = square if squares is None else squares + square
    squares = squares + lax.ppermute(squares, "seq", swap)
    total = squares
    for slot in range(1, dp):
        other = to_partner(squares, "norms", slot, dp)
        (total,) = kernel(add_kernel, (total, other), [((8, LANES), jnp.float32)])
    shares = {}
    for slots in (range(1, dp), range(1))[dp == 1 :]:
        parts = pl.pallas_call(
            functools.partial(share_kernel, slots=slots, dp=dp),
            in_specs=[VMEM] * (2 + dp),
            out_specs=[VMEM] * len(slots),
            out_shape=[jax.ShapeDtypeStruct((rows, columns), jnp.bfloat16)] * len(slots),
            scratch_shapes=[pltpu.VMEM((8, LANES), jnp.float32)],
            compiler_params=small,
        )(select, total, *grads)
        shares.update(zip(slots, parts))
    result = []
    for slot in range(dp):
        share = shares[slot]
        if slot:
            share = to_partner(share, "shares", slot, dp)
        result = [
            pl.pallas_call(
                functools.partial(update_kernel, slot=slot, dp=dp),
                in_specs=[VMEM] * 3 + [ANY] * len(result),
                out_specs=ANY,
                out_shape=jax.ShapeDtypeStruct(noise.shape, jnp.float32),
                input_output_aliases={3: 0} if result else {},
                scratch_shapes=[
                    pltpu.VMEM((rows, columns), jnp.float32),
                    pltpu.SemaphoreType.DMA((1,)),
                ],
                compiler_params=small,
            )(count, share, noise, *result)
        ]
    return result[0]


def tail_by_collectives(value_grad, weight, tenant_of, owner_of, counts, noise):
    rows = PROMPT // 2
    dp_index = lax.axis_index("dp")
    whole = lax.all_gather(value_grad, "tensor", axis=1, tiled=True)
    whole = lax.all_gather(whole, "dp", axis=0, tiled=True)
    part = lax.all_to_all(weight, "tensor", split_axis=0, concat_axis=1, tiled=True)
    grad = lax.dot_general(whole, part, CONTRACT_LAST, preferred_element_type=jnp.float32)
    grad = grad.reshape(-1, rows, part.shape[0])
    norm_sq = lax.psum(jnp.sum(grad * grad, axis=(1, 2)), ("dp", "tensor", "seq"))
    clipped = grad / jnp.maximum(1.0, jnp.sqrt(norm_sq))[:, None, None]
    slots = jnp.arange(owner_of.shape[0])
    owner_ex = jnp.sum(
        jnp.where(tenant_of[:, None] == slots[None, :], owner_of[None, :], 0), axis=1
    )
    select = (owner_ex[None, :] == slots[:, None]).astype(jnp.float32)
    sums = jnp.einsum("oe,erc->orc", select, clipped, precision=lax.Precision.HIGHEST)
    sums = lax.all_gather(sums, "tensor", axis=2, tiled=True)
    sums = lax.all_to_all(sums, "dp", split_axis=0, concat_axis=2, tiled=True)
    my_count = jnp.sum(jnp.where(owner_of == dp_index, counts, 0)).astype(jnp.float32)
    return (math.sqrt(PROMPT * D) * sums + noise) / my_count


def body(sizes, queries, keys, out_grad, value_weight, tenant_of, owner_of, counts, noise):
    swap = xor_pairs(2, 1)
    seq_index = lax.axis_index("seq")
    q, k, g = (
        pltpu.with_memory_space_constraint(x[0], pltpu.HBM) for x in (queries, keys, out_grad)
    )

    sent, q_head, k_head = for_sibling(q, k)
    far = lax.ppermute(sent, "seq", swap)
    aligned = value_weight.shape[0] % LANES == 0 and sizes["dp"] in (1, 2, 4, 8)
    permutes = sizes["tensor"] == 2 and aligned
    *own, g_sent = own_triangle(q, k, g, q_head, k_head)
    g_far = lax.ppermute(g_sent, "seq", swap)
    mine, theirs, turned = prompt_value_grad(
        *own, g, far, g_far, value_weight if permutes else None
    )
    other = lax.ppermute(theirs, "seq", swap)
    first = seq_index == 0
    value_grad = jnp.concatenate(
        [jnp.where(first, mine, other), jnp.where(first, other, mine)], axis=1
    )
    if permutes:
        return tail_by_permutes(
            value_grad, turned[0], tenant_of, owner_of, counts, noise, sizes
        )
    return tail_by_collectives(value_grad, value_weight, tenant_of, owner_of, counts, noise)


def solution(mesh):
    return jax.shard_map(
        functools.partial(body, dict(mesh.shape)),
        mesh=mesh,
        in_specs=(
            P(("group", "dp"), "seq", "tensor"),
            P(("group", "dp"), "seq", "tensor"),
            P(("group", "dp"), "seq", "tensor"),
            P("dp", "tensor"),
            P("group"),
            P("group"),
            P("group"),
            P(("group", "dp"), "seq", None),
        ),
        out_specs=P(("group", "dp"), "seq", None),
        check_vma=False,
    )
```

```python
import functools
import math

import jax
import jax.numpy as jnp
from jax import lax
from jax.experimental import pallas as pl
from jax.experimental.pallas import tpu as pltpu
from jax.sharding import PartitionSpec as P

D = 4608
HEAD_DIM = 128
PROMPT = 64
LANES = 128

softcap = 50.0
query_scale = 144.0 ** (-0.5)
TANH_SCALE = query_scale / softcap
EXP2_SCALE = softcap * math.log2(math.e)

PARTIAL_TYPE = jnp.bfloat16


ORDER = {
    "blocks": ((3, 1, 2), (3, 1, 2)),
    "norms": ((3, 2, 1), (3, 2, 1)),
    "shares": ((1, 2, 3), (1, 2, 3)),
}


def order(what, dp):
    return ORDER[what] if dp == 4 else (tuple(range(1, dp)),) * 2


def partner(what, slot, dp):
    here = lax.axis_index("dp")
    if slot == 0:
        return here
    first, second = (steps[slot - 1] for steps in order(what, dp))
    if first == second:
        return here ^ first
    return here ^ jnp.where(lax.axis_index("seq") == 0, first, second)


def to_partner(array, what, slot, dp):
    steps = [steps[slot - 1] for steps in order(what, dp)]
    pairs = [(2 * z + s, 2 * (z ^ step) + s) for z in range(dp) for s, step in enumerate(steps)]
    return lax.ppermute(array, ("dp", "seq"), pairs)


CONTRACT_LAST = (((1,), (1,)), ((), ()))
VMEM = pl.BlockSpec(memory_space=pltpu.VMEM)
SMEM = pl.BlockSpec(memory_space=pltpu.SMEM)
HBM = pl.BlockSpec(memory_space=pltpu.HBM)
ANY = pl.BlockSpec(memory_space=pl.ANY)


def xor_pairs(size, step):
    return [(i, i ^ step) for i in range(size)]


def add_scores(query, keys, count, diagonal, total):
    block = LANES
    lanes = query.shape[0]
    raw = lax.dot_general(
        keys[:count, :], query, CONTRACT_LAST, preferred_element_type=jnp.float32
    )
    prompt = None
    for low in range(0, count, block):
        e = jnp.exp2(jnp.tanh(raw[low : low + block] * TANH_SCALE) * EXP2_SCALE)
        if diagonal and low == count - block:
            key_pos = lax.broadcasted_iota(jnp.int32, (block, block), 0)
            query_pos = lax.broadcasted_iota(jnp.int32, (block, block), 1)
            keep = jnp.concatenate([key_pos <= query_pos] * (lanes // block), axis=1)
            e = jnp.where(keep, e, 0.0)
        if prompt is None:
            prompt = e[:PROMPT]
        part = jnp.sum(e.reshape(block // 8, 8, lanes), axis=0)
        total = part if total is None else total + part
    return total, prompt


def query_block(queries):
    return jnp.concatenate(
        [
            queries[:, at : at + HEAD_DIM] for at in range(0, queries.shape[1], HEAD_DIM)
        ],
        axis=0,
    )


def triangle_kernel(q, k, g, q_head, k_head, totals, prompts, q_own, k_own, g_sent, done):
    heads, rows, width = q_own.shape
    seq = lax.axis_index("seq")
    lanes = width // HEAD_DIM * LANES

    def load(source, target, h, i):
        extent = target.shape[2]
        columns = pl.ds(pl.multiple_of((seq * heads + h) * extent, LANES), extent)
        return pltpu.make_async_copy(source.at[:, columns], target.at[h], done.at[h, i])

    for h in range(1, heads):
        load(k, k_own, h, 0).start()
        load(q, q_own, h, 1).start()
    half = g_sent.shape[1]
    sibling = pl.ds(pl.multiple_of((1 - seq) * half, LANES), half)
    send = pltpu.make_async_copy(g.at[:, sibling], g_sent, done.at[0, 0])
    send.start()

    def triangle(h, queries, keys):
        for i, start in enumerate(range(0, rows, LANES)):
            total, prompt = add_scores(
                query_block(queries[start : start + LANES, :]), keys, start + LANES, True, None
            )
            at = slice(i * lanes, (i + 1) * lanes)
            totals[h, :, at] = total
            prompts[h, :, at] = prompt

    def step(h, carry):
        load(k, k_own, h, 0).wait()
        load(q, q_own, h, 1).wait()
        triangle(h, q_own.at[h], k_own.at[h])
        return carry

    q_own[0] = q_head[...]
    k_own[0] = k_head[...]
    triangle(0, q_head, k_head)
    lax.fori_loop(1, heads, step, 0)
    send.wait()


def own_triangle(q, k, g, q_head, k_head):
    rows = q.shape[0]
    heads = k.shape[1] // (2 * HEAD_DIM)
    width = q.shape[1] // (2 * heads)
    lanes = width // HEAD_DIM * rows
    return pl.pallas_call(
        triangle_kernel,
        in_specs=[HBM] * 3 + [VMEM] * 2,
        out_specs=[VMEM] * 5,
        out_shape=[
            jax.ShapeDtypeStruct((heads, 8, lanes), jnp.float32),
            jax.ShapeDtypeStruct((heads, PROMPT, lanes), jnp.float32),
            jax.ShapeDtypeStruct((heads, rows, width), jnp.bfloat16),
            jax.ShapeDtypeStruct((heads, rows, HEAD_DIM), jnp.bfloat16),
            jax.ShapeDtypeStruct((rows, heads * width), jnp.bfloat16),
        ],
        scratch_shapes=[pltpu.SemaphoreType.DMA((heads, 2))],
        compiler_params=pltpu.CompilerParams(vmem_limit_bytes=16 * 1024 * 1024),
        cost_estimate=pl.CostEstimate(
            flops=2 * heads * lanes * rows * HEAD_DIM,
            bytes_accessed=6 * heads * rows * width,
            transcendentals=heads * lanes * rows,
        ),
    )(q, k, g, q_head, k_head)


def attention_kernel(*refs, turn):
    if turn:
        totals, prompts, q_own, k_own, g, far, weight, prob, g_own, turned, done = refs
    else:
        totals, prompts, q_own, k_own, g, far, prob, g_own, done = refs
    heads, rows, width = q_own.shape
    group = width // HEAD_DIM
    lanes = group * LANES
    seq = lax.axis_index("seq")
    first = seq == 0
    half = g_own.shape[1]
    load = pltpu.make_async_copy(
        g.at[:, pl.ds(pl.multiple_of(seq * half, LANES), half)], g_own, done.at[0]
    )
    load.start()

    def step(h, carry):
        at_q = pl.ds(pl.multiple_of(h * width, LANES), width)
        at_k = pl.ds(pl.multiple_of(heads * width + h * HEAD_DIM, LANES), HEAD_DIM)
        k_far = far.at[:, at_k]
        if turn:
            share = weight.shape[1] // heads
            features = pl.ds(pl.multiple_of(h * share, LANES), share)
            turned[features, :] = weight[:, features].T
        early_keys = jnp.where(first, k_own[h], k_far[...])
        for i, start in enumerate(range(0, rows, LANES)):
            at = slice(i * lanes, (i + 1) * lanes)
            q_block = far[start : start + LANES, at_q]
            other, far_prompt = add_scores(query_block(q_block), k_far, start + LANES, True, None)
            q_block = jnp.where(first, q_block, q_own[h, start : start + LANES, :])
            square, late_prompt = add_scores(query_block(q_block), early_keys, rows, False, None)
            own, own_prompt = totals[h, :, at], prompts[h, :, at]
            early = jnp.where(first, own, other)
            late = square + jnp.where(first, other, own)
            early_prompt = jnp.where(first, own_prompt, far_prompt)
            early = early_prompt / jnp.sum(early, axis=0, keepdims=True)
            late = late_prompt / jnp.sum(late, axis=0, keepdims=True)
            for slot, scaled in enumerate((jnp.where(first, early, late), jnp.where(first, late, early))):
                scaled = scaled.astype(jnp.bfloat16)
                column = slot * rows + start
                for j in range(group):
                    prob[h, j, :, column : column + LANES] = scaled[:, j * LANES : (j + 1) * LANES]
        return carry

    lax.fori_loop(0, heads, step, 0, unroll=2 if heads % 2 == 0 else 1)
    load.wait()


def value_kernel(prob, g_own, g_far, mine, theirs):
    heads, group, _, rows = prob.shape
    rows = rows // 2
    width = group * HEAD_DIM
    first = lax.axis_index("seq") == 0

    def step(h):
        at_k = slice(h * HEAD_DIM, (h + 1) * HEAD_DIM)
        at_g = slice(h * width, (h + 1) * width)
        whole = None
        for slot, g in enumerate((g_own[:, at_g], g_far[:, at_g])):
            term = jnp.dot(
                jnp.concatenate(
                    [prob[h, j, :, slot * rows : (slot + 1) * rows] for j in range(group)], axis=0
                ),
                g,
                preferred_element_type=jnp.float32,
            )
            whole = term if whole is None else whole + term
        value = None
        for j in range(group):
            part = whole[j * PROMPT : (j + 1) * PROMPT, j * HEAD_DIM : (j + 1) * HEAD_DIM]
            value = part if value is None else value + part
        value = value.astype(jnp.bfloat16)
        low, high = value[: PROMPT // 2], value[PROMPT // 2 :]
        mine[:, at_k] = jnp.where(first, low, high)
        theirs[:, at_k] = jnp.where(first, high, low)

    for h in range(heads):
        step(h)


def prompt_value_grad(totals, prompts, q_own, k_own, g, far, g_far, weight):
    heads, rows, width = q_own.shape
    group = width // HEAD_DIM
    weights = [] if weight is None else [weight]
    prob, g_own, *turned = pl.pallas_call(
        functools.partial(attention_kernel, turn=bool(weights)),
        in_specs=[VMEM] * 4 + [HBM, VMEM] + [VMEM] * len(weights),
        out_specs=[VMEM] * (2 + len(weights)),
        out_shape=[
            jax.ShapeDtypeStruct((heads, group, PROMPT, 2 * rows), jnp.bfloat16),
            jax.ShapeDtypeStruct((rows, heads * width), jnp.bfloat16),
        ]
        + [jax.ShapeDtypeStruct(w.shape[::-1], w.dtype) for w in weights],
        scratch_shapes=[pltpu.SemaphoreType.DMA((1,))],
        compiler_params=pltpu.CompilerParams(vmem_limit_bytes=16 * 1024 * 1024),
        cost_estimate=pl.CostEstimate(
            flops=heads * group * 6 * rows * rows * HEAD_DIM,
            bytes_accessed=6 * rows * heads * width,
            transcendentals=heads * group * 3 * rows * rows,
        ),
    )(totals, prompts, q_own, k_own, g, far, *weights)
    mine, theirs = pl.pallas_call(
        value_kernel,
        in_specs=[VMEM] * 3,
        out_specs=[VMEM] * 2,
        out_shape=[jax.ShapeDtypeStruct((PROMPT // 2, heads * HEAD_DIM), jnp.bfloat16)] * 2,
        compiler_params=pltpu.CompilerParams(vmem_limit_bytes=16 * 1024 * 1024),
        cost_estimate=pl.CostEstimate(
            flops=4 * heads * group * PROMPT * rows * HEAD_DIM,
            bytes_accessed=6 * rows * heads * width,
            transcendentals=0,
        ),
    )(prob, g_own, g_far)
    return mine, theirs, turned


def sibling_kernel(q, k, out, q_head, k_head, done):
    seq = lax.axis_index("seq")
    copies, to = [], 0
    for i, source in enumerate((q, k)):
        half = source.shape[1] // 2
        columns = pl.ds(pl.multiple_of((1 - seq) * half, LANES), half)
        copies.append(
            pltpu.make_async_copy(
                source.at[:, columns], out.at[:, to : to + half], done.at[i]
            )
        )
        to += half
    for i, (source, target) in enumerate(((q, q_head), (k, k_head))):
        start = pl.multiple_of(seq * (source.shape[1] // 2), LANES)
        copies.append(
            pltpu.make_async_copy(
                source.at[:, pl.ds(start, target.shape[1])], target, done.at[2 + i]
            )
        )
    for copy in copies:
        copy.start()
    for copy in copies:
        copy.wait()


def for_sibling(q, k):
    rows = q.shape[0]
    width = q.shape[1] * HEAD_DIM // k.shape[1]
    return pl.pallas_call(
        sibling_kernel,
        in_specs=[HBM] * 2,
        out_specs=[VMEM] * 3,
        out_shape=[
            jax.ShapeDtypeStruct((rows, (q.shape[1] + k.shape[1]) // 2), jnp.bfloat16),
            jax.ShapeDtypeStruct((rows, width), jnp.bfloat16),
            jax.ShapeDtypeStruct((rows, HEAD_DIM), jnp.bfloat16),
        ],
        scratch_shapes=[pltpu.SemaphoreType.DMA((4,))],
        compiler_params=pltpu.CompilerParams(vmem_limit_bytes=16 * 1024 * 1024),
    )(q, k)


def partial_kernel(block, weight, out):
    total = jnp.dot(block[...], weight[...], preferred_element_type=jnp.float32)
    out[...] = total.astype(out.dtype)


def combine_kernel(near, far, grad, squares, *, slot, dp):
    folded = None
    for at in range(0, near.shape[1], LANES):
        part = near[:, at : at + LANES].astype(jnp.float32)
        part = part + far[:, at : at + LANES].astype(jnp.float32)
        grad[:, at : at + LANES] = part
        folded = part * part if folded is None else folded + part * part
    folded = jnp.sum(folded, axis=0, keepdims=True)
    example = lax.broadcasted_iota(jnp.int32, squares.shape, 0)
    squares[...] = jnp.where(example == partner("blocks", slot, dp), folded, 0.0)


def select_kernel(tenant_of, owner_of, counts, select, count, *, dp):
    for j in range(dp):
        owner = owner_of[tenant_of[partner("blocks", j, dp)]]
        for i in range(dp):
            hit = jnp.where(owner == partner("shares", i, dp), 1.0, 0.0)
            row = i * dp + j
            select[row : row + 1, :] = jnp.full((1, LANES), hit, jnp.float32)
    total = 0
    for slot in range(dp):
        total = total + jnp.where(owner_of[slot] == lax.axis_index("dp"), counts[slot], 0)
    count[...] = jnp.full((1, LANES), total.astype(jnp.float32), jnp.float32)


def add_kernel(left, right, out):
    out[...] = left[...] + right[...]


def share_kernel(select, norms, last, *refs, slots, dp):
    grads, outs, scales = refs[:dp], refs[dp:-1], refs[-1]
    norm_sq = jnp.sum(norms[...] + last[...], axis=1, keepdims=True)
    scales[...] = jnp.broadcast_to(1.0 / jnp.maximum(1.0, jnp.sqrt(norm_sq)), scales.shape)
    scale = [scales[pl.ds(partner("blocks", j, dp), 1), :] for j in range(dp)]
    factors = [
        [scale[j] * select[i * dp + j : i * dp + j + 1, :] for j in range(dp)] for i in slots
    ]
    for at in range(0, outs[0].shape[1], LANES):
        parts = [grad[:, at : at + LANES] for grad in grads]
        for out, factor in zip(outs, factors):
            total = None
            for part, weight in zip(parts, factor):
                term = part * weight
                total = term if total is None else total + term
            out[:, at : at + LANES] = total.astype(jnp.bfloat16)


def update_kernel(count, share, noise, *refs, slot, dp):
    out, stage, done = refs[-3:]
    columns = share.shape[1]
    base = pl.multiple_of(partner("shares", slot, dp) * columns, LANES)
    for at in range(0, columns, LANES):
        part = share[:, at : at + LANES].astype(jnp.float32)
        added = noise[0, :, pl.ds(pl.multiple_of(base + at, LANES), LANES)]
        stage[:, at : at + LANES] = (math.sqrt(PROMPT * D) * part + added) / count[...]
    copy = pltpu.make_async_copy(stage, out.at[0, :, pl.ds(base, columns)], done.at[0])
    copy.start()
    copy.wait()


def tail_by_permutes(value_grad, weight, tenant_of, owner_of, counts, noise, sizes):
    dp = sizes["dp"]
    columns = weight.shape[1]
    rows = PROMPT // 2
    swap = xor_pairs(2, 1)
    small = pltpu.CompilerParams(vmem_limit_bytes=16 * 1024 * 1024)

    def kernel(body, operands, outs, scalar=False, **static):
        return pl.pallas_call(
            functools.partial(body, **static),
            in_specs=[SMEM if scalar else VMEM] * len(operands),
            out_specs=[VMEM] * len(outs),
            out_shape=[jax.ShapeDtypeStruct(shape, dtype) for shape, dtype in outs],
            compiler_params=small,
        )(*operands)

    blocks = [value_grad]
    blocks += [to_partner(value_grad, "blocks", slot, dp) for slot in range(1, dp)]
    tenant_of, blocks[1] = lax.optimization_barrier((tenant_of, blocks[1]))
    select, count = kernel(
        select_kernel,
        (tenant_of, owner_of, counts),
        [((dp * dp, LANES), jnp.float32), ((1, LANES), jnp.float32)],
        scalar=True,
        dp=dp,
    )
    grads, squares, near = [], None, None
    for slot, block in enumerate(blocks):
        if slot > 1:
            block, _ = lax.optimization_barrier((block, near))
        (near,) = pl.pallas_call(
            partial_kernel,
            in_specs=[VMEM] * 2,
            out_specs=[VMEM],
            out_shape=[jax.ShapeDtypeStruct((rows, columns), PARTIAL_TYPE)],
            compiler_params=small,
            cost_estimate=pl.CostEstimate(
                flops=2 * rows * weight.size, bytes_accessed=2 * weight.size, transcendentals=0
            ),
        )(block, weight)
        far = lax.ppermute(near, "tensor", swap)
        grad, square = kernel(
            combine_kernel,
            (near, far),
            [((rows, columns), jnp.float32), ((8, LANES), jnp.float32)],
            slot=slot,
            dp=dp,
        )
        grads.append(grad)
        squares = square if squares is None else squares + square
    squares = squares + lax.ppermute(squares, "seq", swap)
    total = squares
    last = jnp.zeros_like(squares)
    for slot in range(1, dp):
        if slot > 1:
            (total,) = kernel(add_kernel, (total, last), [((8, LANES), jnp.float32)])
        last = to_partner(squares, "norms", slot, dp)
    shares = {}
    for slots in (range(1, dp), range(1))[dp == 1 :]:
        parts = pl.pallas_call(
            functools.partial(share_kernel, slots=slots, dp=dp),
            in_specs=[VMEM] * (3 + dp),
            out_specs=[VMEM] * len(slots),
            out_shape=[jax.ShapeDtypeStruct((rows, columns), jnp.bfloat16)] * len(slots),
            scratch_shapes=[pltpu.VMEM((8, LANES), jnp.float32)],
            compiler_params=small,
        )(select, total, last, *grads)
        shares.update(zip(slots, parts))
    result = []
    for slot in range(dp):
        share = shares[slot]
        if slot:
            share = to_partner(share, "shares", slot, dp)
        result = [
            pl.pallas_call(
                functools.partial(update_kernel, slot=slot, dp=dp),
                in_specs=[VMEM] * 3 + [ANY] * len(result),
                out_specs=ANY,
                out_shape=jax.ShapeDtypeStruct(noise.shape, jnp.float32),
                input_output_aliases={3: 0} if result else {},
                scratch_shapes=[
                    pltpu.VMEM((rows, columns), jnp.float32),
                    pltpu.SemaphoreType.DMA((1,)),
                ],
                compiler_params=small,
            )(count, share, noise, *result)
        ]
    return result[0]


def tail_by_collectives(value_grad, weight, tenant_of, owner_of, counts, noise):
    rows = PROMPT // 2
    dp_index = lax.axis_index("dp")
    whole = lax.all_gather(value_grad, "tensor", axis=1, tiled=True)
    whole = lax.all_gather(whole, "dp", axis=0, tiled=True)
    part = lax.all_to_all(weight, "tensor", split_axis=0, concat_axis=1, tiled=True)
    grad = lax.dot_general(whole, part, CONTRACT_LAST, preferred_element_type=jnp.float32)
    grad = grad.reshape(-1, rows, part.shape[0])
    norm_sq = lax.psum(jnp.sum(grad * grad, axis=(1, 2)), ("dp", "tensor", "seq"))
    clipped = grad / jnp.maximum(1.0, jnp.sqrt(norm_sq))[:, None, None]
    slots = jnp.arange(owner_of.shape[0])
    owner_ex = jnp.sum(
        jnp.where(tenant_of[:, None] == slots[None, :], owner_of[None, :], 0), axis=1
    )
    select = (owner_ex[None, :] == slots[:, None]).astype(jnp.float32)
    sums = jnp.einsum("oe,erc->orc", select, clipped, precision=lax.Precision.HIGHEST)
    sums = lax.all_gather(sums, "tensor", axis=2, tiled=True)
    sums = lax.all_to_all(sums, "dp", split_axis=0, concat_axis=2, tiled=True)
    my_count = jnp.sum(jnp.where(owner_of == dp_index, counts, 0)).astype(jnp.float32)
    return (math.sqrt(PROMPT * D) * sums + noise) / my_count


def body(sizes, queries, keys, out_grad, value_weight, tenant_of, owner_of, counts, noise):
    swap = xor_pairs(2, 1)
    seq_index = lax.axis_index("seq")
    q, k, g = (
        pltpu.with_memory_space_constraint(x[0], pltpu.HBM) for x in (queries, keys, out_grad)
    )

    sent, q_head, k_head = for_sibling(q, k)
    far = lax.ppermute(sent, "seq", swap)
    aligned = value_weight.shape[0] % LANES == 0 and sizes["dp"] in (1, 2, 4, 8)
    permutes = sizes["tensor"] == 2 and aligned
    *own, g_sent = own_triangle(q, k, g, q_head, k_head)
    g_far = lax.ppermute(g_sent, "seq", swap)
    mine, theirs, turned = prompt_value_grad(
        *own, g, far, g_far, value_weight if permutes else None
    )
    other = lax.ppermute(theirs, "seq", swap)
    first = seq_index == 0
    value_grad = jnp.concatenate(
        [jnp.where(first, mine, other), jnp.where(first, other, mine)], axis=1
    )
    if permutes:
        return tail_by_permutes(
            value_grad, turned[0], tenant_of, owner_of, counts, noise, sizes
        )
    return tail_by_collectives(value_grad, value_weight, tenant_of, owner_of, counts, noise)


def solution(mesh):
    return jax.shard_map(
        functools.partial(body, dict(mesh.shape)),
        mesh=mesh,
        in_specs=(
            P(("group", "dp"), "seq", "tensor"),
            P(("group", "dp"), "seq", "tensor"),
            P(("group", "dp"), "seq", "tensor"),
            P("dp", "tensor"),
            P("group"),
            P("group"),
            P("group"),
            P(("group", "dp"), "seq", None),
        ),
        out_specs=P(("group", "dp"), "seq", None),
        check_vma=False,
    )
```

```python
import functools
import math

import jax
import jax.numpy as jnp
from jax import lax
from jax.experimental import pallas as pl
from jax.experimental.pallas import tpu as pltpu
from jax.sharding import PartitionSpec as P

D = 4608
HEAD_DIM = 128
PROMPT = 64
LANES = 128

softcap = 50.0
query_scale = 144.0 ** (-0.5)
TANH_SCALE = query_scale / softcap
EXP2_SCALE = softcap * math.log2(math.e)

PARTIAL_TYPE = jnp.bfloat16


ORDER = {
    "blocks": ((3, 1, 2), (3, 1, 2)),
    "norms": ((3, 2, 1), (3, 2, 1)),
    "shares": ((1, 2, 3), (1, 3, 2)),
}


def order(what, dp):
    return ORDER[what] if dp == 4 else (tuple(range(1, dp)),) * 2


def partner(what, slot, dp):
    here = lax.axis_index("dp")
    if slot == 0:
        return here
    first, second = (steps[slot - 1] for steps in order(what, dp))
    if first == second:
        return here ^ first
    return here ^ jnp.where(lax.axis_index("seq") == 0, first, second)


def to_partner(array, what, slot, dp):
    steps = [steps[slot - 1] for steps in order(what, dp)]
    pairs = [(2 * z + s, 2 * (z ^ step) + s) for z in range(dp) for s, step in enumerate(steps)]
    return lax.ppermute(array, ("dp", "seq"), pairs)


CONTRACT_LAST = (((1,), (1,)), ((), ()))
VMEM = pl.BlockSpec(memory_space=pltpu.VMEM)
SMEM = pl.BlockSpec(memory_space=pltpu.SMEM)
HBM = pl.BlockSpec(memory_space=pltpu.HBM)
ANY = pl.BlockSpec(memory_space=pl.ANY)


def xor_pairs(size, step):
    return [(i, i ^ step) for i in range(size)]


def add_scores(query, keys, count, diagonal, total):
    block = LANES
    lanes = query.shape[0]
    raw = lax.dot_general(
        keys[:count, :], query, CONTRACT_LAST, preferred_element_type=jnp.float32
    )
    prompt = None
    for low in range(0, count, block):
        e = jnp.exp2(jnp.tanh(raw[low : low + block] * TANH_SCALE) * EXP2_SCALE)
        if diagonal and low == count - block:
            key_pos = lax.broadcasted_iota(jnp.int32, (block, block), 0)
            query_pos = lax.broadcasted_iota(jnp.int32, (block, block), 1)
            keep = jnp.concatenate([key_pos <= query_pos] * (lanes // block), axis=1)
            e = jnp.where(keep, e, 0.0)
        if prompt is None:
            prompt = e[:PROMPT]
        part = jnp.sum(e.reshape(block // 8, 8, lanes), axis=0)
        total = part if total is None else total + part
    return total, prompt


def query_block(queries):
    return jnp.concatenate(
        [
            queries[:, at : at + HEAD_DIM] for at in range(0, queries.shape[1], HEAD_DIM)
        ],
        axis=0,
    )


def triangle_kernel(q, k, g, q_head, k_head, totals, prompts, q_own, k_own, g_sent, done):
    heads, rows, width = q_own.shape
    seq = lax.axis_index("seq")
    lanes = width // HEAD_DIM * LANES

    def load(source, target, h, i):
        extent = target.shape[2]
        columns = pl.ds(pl.multiple_of((seq * heads + h) * extent, LANES), extent)
        return pltpu.make_async_copy(source.at[:, columns], target.at[h], done.at[h, i])

    for h in range(1, heads):
        load(k, k_own, h, 0).start()
        load(q, q_own, h, 1).start()
    half = g_sent.shape[1]
    sibling = pl.ds(pl.multiple_of((1 - seq) * half, LANES), half)
    send = pltpu.make_async_copy(g.at[:, sibling], g_sent, done.at[0, 0])
    send.start()

    def triangle(h, queries, keys):
        for i, start in enumerate(range(0, rows, LANES)):
            total, prompt = add_scores(
                query_block(queries[start : start + LANES, :]), keys, start + LANES, True, None
            )
            at = slice(i * lanes, (i + 1) * lanes)
            totals[h, :, at] = total
            prompts[h, :, at] = prompt

    def step(h, carry):
        load(k, k_own, h, 0).wait()
        load(q, q_own, h, 1).wait()
        triangle(h, q_own.at[h], k_own.at[h])
        return carry

    q_own[0] = q_head[...]
    k_own[0] = k_head[...]
    triangle(0, q_head, k_head)
    lax.fori_loop(1, heads, step, 0)
    send.wait()


def own_triangle(q, k, g, q_head, k_head):
    rows = q.shape[0]
    heads = k.shape[1] // (2 * HEAD_DIM)
    width = q.shape[1] // (2 * heads)
    lanes = width // HEAD_DIM * rows
    return pl.pallas_call(
        triangle_kernel,
        in_specs=[HBM] * 3 + [VMEM] * 2,
        out_specs=[VMEM] * 5,
        out_shape=[
            jax.ShapeDtypeStruct((heads, 8, lanes), jnp.float32),
            jax.ShapeDtypeStruct((heads, PROMPT, lanes), jnp.float32),
            jax.ShapeDtypeStruct((heads, rows, width), jnp.bfloat16),
            jax.ShapeDtypeStruct((heads, rows, HEAD_DIM), jnp.bfloat16),
            jax.ShapeDtypeStruct((rows, heads * width), jnp.bfloat16),
        ],
        scratch_shapes=[pltpu.SemaphoreType.DMA((heads, 2))],
        compiler_params=pltpu.CompilerParams(vmem_limit_bytes=16 * 1024 * 1024),
        cost_estimate=pl.CostEstimate(
            flops=2 * heads * lanes * rows * HEAD_DIM,
            bytes_accessed=6 * heads * rows * width,
            transcendentals=heads * lanes * rows,
        ),
    )(q, k, g, q_head, k_head)


def attention_kernel(*refs, turn):
    if turn:
        totals, prompts, q_own, k_own, g, far, weight, prob, g_own, turned, done = refs
    else:
        totals, prompts, q_own, k_own, g, far, prob, g_own, done = refs
    heads, rows, width = q_own.shape
    group = width // HEAD_DIM
    lanes = group * LANES
    seq = lax.axis_index("seq")
    first = seq == 0
    half = g_own.shape[1]
    load = pltpu.make_async_copy(
        g.at[:, pl.ds(pl.multiple_of(seq * half, LANES), half)], g_own, done.at[0]
    )
    load.start()

    def step(h, carry):
        at_q = pl.ds(pl.multiple_of(h * width, LANES), width)
        at_k = pl.ds(pl.multiple_of(heads * width + h * HEAD_DIM, LANES), HEAD_DIM)
        k_far = far.at[:, at_k]
        if turn:
            share = weight.shape[1] // heads
            features = pl.ds(pl.multiple_of(h * share, LANES), share)
            turned[features, :] = weight[:, features].T
        early_keys = jnp.where(first, k_own[h], k_far[...])
        for i, start in enumerate(range(0, rows, LANES)):
            at = slice(i * lanes, (i + 1) * lanes)
            q_block = far[start : start + LANES, at_q]
            other, far_prompt = add_scores(query_block(q_block), k_far, start + LANES, True, None)
            q_block = jnp.where(first, q_block, q_own[h, start : start + LANES, :])
            square, late_prompt = add_scores(query_block(q_block), early_keys, rows, False, None)
            own, own_prompt = totals[h, :, at], prompts[h, :, at]
            early = jnp.where(first, own, other)
            late = square + jnp.where(first, other, own)
            early_prompt = jnp.where(first, own_prompt, far_prompt)
            early = early_prompt / jnp.sum(early, axis=0, keepdims=True)
            late = late_prompt / jnp.sum(late, axis=0, keepdims=True)
            for slot, scaled in enumerate((jnp.where(first, early, late), jnp.where(first, late, early))):
                scaled = scaled.astype(jnp.bfloat16)
                column = slot * rows + start
                for j in range(group):
                    prob[h, j, :, column : column + LANES] = scaled[:, j * LANES : (j + 1) * LANES]
        return carry

    lax.fori_loop(0, heads, step, 0, unroll=2 if heads % 2 == 0 else 1)
    load.wait()


def value_kernel(prob, g_own, g_far, mine, theirs):
    heads, group, _, rows = prob.shape
    rows = rows // 2
    width = group * HEAD_DIM
    first = lax.axis_index("seq") == 0

    def step(h):
        at_k = slice(h * HEAD_DIM, (h + 1) * HEAD_DIM)
        at_g = slice(h * width, (h + 1) * width)
        whole = None
        for slot, g in enumerate((g_own[:, at_g], g_far[:, at_g])):
            term = jnp.dot(
                jnp.concatenate(
                    [prob[h, j, :, slot * rows : (slot + 1) * rows] for j in range(group)], axis=0
                ),
                g,
                preferred_element_type=jnp.float32,
            )
            whole = term if whole is None else whole + term
        value = None
        for j in range(group):
            part = whole[j * PROMPT : (j + 1) * PROMPT, j * HEAD_DIM : (j + 1) * HEAD_DIM]
            value = part if value is None else value + part
        value = value.astype(jnp.bfloat16)
        low, high = value[: PROMPT // 2], value[PROMPT // 2 :]
        mine[:, at_k] = jnp.where(first, low, high)
        theirs[:, at_k] = jnp.where(first, high, low)

    for h in range(heads):
        step(h)


def prompt_value_grad(totals, prompts, q_own, k_own, g, far, g_far, weight):
    heads, rows, width = q_own.shape
    group = width // HEAD_DIM
    weights = [] if weight is None else [weight]
    prob, g_own, *turned = pl.pallas_call(
        functools.partial(attention_kernel, turn=bool(weights)),
        in_specs=[VMEM] * 4 + [HBM, VMEM] + [VMEM] * len(weights),
        out_specs=[VMEM] * (2 + len(weights)),
        out_shape=[
            jax.ShapeDtypeStruct((heads, group, PROMPT, 2 * rows), jnp.bfloat16),
            jax.ShapeDtypeStruct((rows, heads * width), jnp.bfloat16),
        ]
        + [jax.ShapeDtypeStruct(w.shape[::-1], w.dtype) for w in weights],
        scratch_shapes=[pltpu.SemaphoreType.DMA((1,))],
        compiler_params=pltpu.CompilerParams(vmem_limit_bytes=16 * 1024 * 1024),
        cost_estimate=pl.CostEstimate(
            flops=heads * group * 6 * rows * rows * HEAD_DIM,
            bytes_accessed=6 * rows * heads * width,
            transcendentals=heads * group * 3 * rows * rows,
        ),
    )(totals, prompts, q_own, k_own, g, far, *weights)
    mine, theirs = pl.pallas_call(
        value_kernel,
        in_specs=[VMEM] * 3,
        out_specs=[VMEM] * 2,
        out_shape=[jax.ShapeDtypeStruct((PROMPT // 2, heads * HEAD_DIM), jnp.bfloat16)] * 2,
        compiler_params=pltpu.CompilerParams(vmem_limit_bytes=16 * 1024 * 1024),
        cost_estimate=pl.CostEstimate(
            flops=4 * heads * group * PROMPT * rows * HEAD_DIM,
            bytes_accessed=6 * rows * heads * width,
            transcendentals=0,
        ),
    )(prob, g_own, g_far)
    return mine, theirs, turned


def sibling_kernel(q, k, out, q_head, k_head, done):
    seq = lax.axis_index("seq")
    copies, to = [], 0
    for i, source in enumerate((q, k)):
        half = source.shape[1] // 2
        columns = pl.ds(pl.multiple_of((1 - seq) * half, LANES), half)
        copies.append(
            pltpu.make_async_copy(
                source.at[:, columns], out.at[:, to : to + half], done.at[i]
            )
        )
        to += half
    for i, (source, target) in enumerate(((q, q_head), (k, k_head))):
        start = pl.multiple_of(seq * (source.shape[1] // 2), LANES)
        copies.append(
            pltpu.make_async_copy(
                source.at[:, pl.ds(start, target.shape[1])], target, done.at[2 + i]
            )
        )
    for copy in copies:
        copy.start()
    for copy in copies:
        copy.wait()


def for_sibling(q, k):
    rows = q.shape[0]
    width = q.shape[1] * HEAD_DIM // k.shape[1]
    return pl.pallas_call(
        sibling_kernel,
        in_specs=[HBM] * 2,
        out_specs=[VMEM] * 3,
        out_shape=[
            jax.ShapeDtypeStruct((rows, (q.shape[1] + k.shape[1]) // 2), jnp.bfloat16),
            jax.ShapeDtypeStruct((rows, width), jnp.bfloat16),
            jax.ShapeDtypeStruct((rows, HEAD_DIM), jnp.bfloat16),
        ],
        scratch_shapes=[pltpu.SemaphoreType.DMA((4,))],
        compiler_params=pltpu.CompilerParams(vmem_limit_bytes=16 * 1024 * 1024),
    )(q, k)


def partial_kernel(block, weight, out):
    total = jnp.dot(block[...], weight[...], preferred_element_type=jnp.float32)
    out[...] = total.astype(out.dtype)


def combine_kernel(near, far, grad, squares, *, slot, dp):
    folded = None
    for at in range(0, near.shape[1], LANES):
        part = near[:, at : at + LANES].astype(jnp.float32)
        part = part + far[:, at : at + LANES].astype(jnp.float32)
        grad[:, at : at + LANES] = part
        folded = part * part if folded is None else folded + part * part
    folded = jnp.sum(folded, axis=0, keepdims=True)
    example = lax.broadcasted_iota(jnp.int32, squares.shape, 0)
    squares[...] = jnp.where(example == partner("blocks", slot, dp), folded, 0.0)


def select_kernel(tenant_of, owner_of, counts, select, count, *, dp):
    for j in range(dp):
        owner = owner_of[tenant_of[partner("blocks", j, dp)]]
        for i in range(dp):
            hit = jnp.where(owner == partner("shares", i, dp), 1.0, 0.0)
            row = i * dp + j
            select[row : row + 1, :] = jnp.full((1, LANES), hit, jnp.float32)
    total = 0
    for slot in range(dp):
        total = total + jnp.where(owner_of[slot] == lax.axis_index("dp"), counts[slot], 0)
    count[...] = jnp.full((1, LANES), total.astype(jnp.float32), jnp.float32)


def add_kernel(left, right, out):
    out[...] = left[...] + right[...]


def share_kernel(select, norms, *refs, slots, dp):
    grads, outs, scales = refs[:dp], refs[dp:-1], refs[-1]
    norm_sq = jnp.sum(norms[...], axis=1, keepdims=True)
    scales[...] = jnp.broadcast_to(1.0 / jnp.maximum(1.0, jnp.sqrt(norm_sq)), scales.shape)
    scale = [scales[pl.ds(partner("blocks", j, dp), 1), :] for j in range(dp)]
    factors = [
        [scale[j] * select[i * dp + j : i * dp + j + 1, :] for j in range(dp)] for i in slots
    ]
    for at in range(0, outs[0].shape[1], LANES):
        parts = [grad[:, at : at + LANES] for grad in grads]
        for out, factor in zip(outs, factors):
            total = None
            for part, weight in zip(parts, factor):
                term = part * weight
                total = term if total is None else total + term
            out[:, at : at + LANES] = total.astype(jnp.bfloat16)


def update_kernel(count, share, noise, *refs, slot, dp):
    out, stage, done = refs[-3:]
    columns = share.shape[1]
    base = pl.multiple_of(partner("shares", slot, dp) * columns, LANES)
    for at in range(0, columns, LANES):
        part = share[:, at : at + LANES].astype(jnp.float32)
        added = noise[0, :, pl.ds(pl.multiple_of(base + at, LANES), LANES)]
        stage[:, at : at + LANES] = (math.sqrt(PROMPT * D) * part + added) / count[...]
    copy = pltpu.make_async_copy(stage, out.at[0, :, pl.ds(base, columns)], done.at[0])
    copy.start()
    copy.wait()


def tail_by_permutes(value_grad, weight, tenant_of, owner_of, counts, noise, sizes):
    dp = sizes["dp"]
    columns = weight.shape[1]
    rows = PROMPT // 2
    swap = xor_pairs(2, 1)
    small = pltpu.CompilerParams(vmem_limit_bytes=16 * 1024 * 1024)

    def kernel(body, operands, outs, scalar=False, **static):
        return pl.pallas_call(
            functools.partial(body, **static),
            in_specs=[SMEM if scalar else VMEM] * len(operands),
            out_specs=[VMEM] * len(outs),
            out_shape=[jax.ShapeDtypeStruct(shape, dtype) for shape, dtype in outs],
            compiler_params=small,
        )(*operands)

    blocks = [value_grad]
    blocks += [to_partner(value_grad, "blocks", slot, dp) for slot in range(1, dp)]
    tenant_of, blocks[1] = lax.optimization_barrier((tenant_of, blocks[1]))
    select, count = kernel(
        select_kernel,
        (tenant_of, owner_of, counts),
        [((dp * dp, LANES), jnp.float32), ((1, LANES), jnp.float32)],
        scalar=True,
        dp=dp,
    )
    grads, squares, near = [], None, None
    for slot, block in enumerate(blocks):
        if slot > 1:
            block, _ = lax.optimization_barrier((block, near))
        (near,) = pl.pallas_call(
            partial_kernel,
            in_specs=[VMEM] * 2,
            out_specs=[VMEM],
            out_shape=[jax.ShapeDtypeStruct((rows, columns), PARTIAL_TYPE)],
            compiler_params=small,
            cost_estimate=pl.CostEstimate(
                flops=2 * rows * weight.size, bytes_accessed=2 * weight.size, transcendentals=0
            ),
        )(block, weight)
        far = lax.ppermute(near, "tensor", swap)
        grad, square = kernel(
            combine_kernel,
            (near, far),
            [((rows, columns), jnp.float32), ((8, LANES), jnp.float32)],
            slot=slot,
            dp=dp,
        )
        grads.append(grad)
        squares = square if squares is None else squares + square
    squares = squares + lax.ppermute(squares, "seq", swap)
    total = squares
    for slot in range(1, dp):
        other = to_partner(squares, "norms", slot, dp)
        (total,) = kernel(add_kernel, (total, other), [((8, LANES), jnp.float32)])
    shares = {}
    for slots in (range(1, dp), range(1))[dp == 1 :]:
        parts = pl.pallas_call(
            functools.partial(share_kernel, slots=slots, dp=dp),
            in_specs=[VMEM] * (2 + dp),
            out_specs=[VMEM] * len(slots),
            out_shape=[jax.ShapeDtypeStruct((rows, columns), jnp.bfloat16)] * len(slots),
            scratch_shapes=[pltpu.VMEM((8, LANES), jnp.float32)],
            compiler_params=small,
        )(select, total, *grads)
        shares.update(zip(slots, parts))
    result = []
    for slot in range(dp):
        share = shares[slot]
        if slot:
            share = to_partner(share, "shares", slot, dp)
        result = [
            pl.pallas_call(
                functools.partial(update_kernel, slot=slot, dp=dp),
                in_specs=[VMEM] * 3 + [ANY] * len(result),
                out_specs=ANY,
                out_shape=jax.ShapeDtypeStruct(noise.shape, jnp.float32),
                input_output_aliases={3: 0} if result else {},
                scratch_shapes=[
                    pltpu.VMEM((rows, columns), jnp.float32),
                    pltpu.SemaphoreType.DMA((1,)),
                ],
                compiler_params=small,
            )(count, share, noise, *result)
        ]
    return result[0]


def tail_by_collectives(value_grad, weight, tenant_of, owner_of, counts, noise):
    rows = PROMPT // 2
    dp_index = lax.axis_index("dp")
    whole = lax.all_gather(value_grad, "tensor", axis=1, tiled=True)
    whole = lax.all_gather(whole, "dp", axis=0, tiled=True)
    part = lax.all_to_all(weight, "tensor", split_axis=0, concat_axis=1, tiled=True)
    grad = lax.dot_general(whole, part, CONTRACT_LAST, preferred_element_type=jnp.float32)
    grad = grad.reshape(-1, rows, part.shape[0])
    norm_sq = lax.psum(jnp.sum(grad * grad, axis=(1, 2)), ("dp", "tensor", "seq"))
    clipped = grad / jnp.maximum(1.0, jnp.sqrt(norm_sq))[:, None, None]
    slots = jnp.arange(owner_of.shape[0])
    owner_ex = jnp.sum(
        jnp.where(tenant_of[:, None] == slots[None, :], owner_of[None, :], 0), axis=1
    )
    select = (owner_ex[None, :] == slots[:, None]).astype(jnp.float32)
    sums = jnp.einsum("oe,erc->orc", select, clipped, precision=lax.Precision.HIGHEST)
    sums = lax.all_gather(sums, "tensor", axis=2, tiled=True)
    sums = lax.all_to_all(sums, "dp", split_axis=0, concat_axis=2, tiled=True)
    my_count = jnp.sum(jnp.where(owner_of == dp_index, counts, 0)).astype(jnp.float32)
    return (math.sqrt(PROMPT * D) * sums + noise) / my_count


def body(sizes, queries, keys, out_grad, value_weight, tenant_of, owner_of, counts, noise):
    swap = xor_pairs(2, 1)
    seq_index = lax.axis_index("seq")
    q, k, g = (
        pltpu.with_memory_space_constraint(x[0], pltpu.HBM) for x in (queries, keys, out_grad)
    )

    sent, q_head, k_head = for_sibling(q, k)
    far = lax.ppermute(sent, "seq", swap)
    aligned = value_weight.shape[0] % LANES == 0 and sizes["dp"] in (1, 2, 4, 8)
    permutes = sizes["tensor"] == 2 and aligned
    *own, g_sent = own_triangle(q, k, g, q_head, k_head)
    g_far = lax.ppermute(g_sent, "seq", swap)
    mine, theirs, turned = prompt_value_grad(
        *own, g, far, g_far, value_weight if permutes else None
    )
    other = lax.ppermute(theirs, "seq", swap)
    first = seq_index == 0
    value_grad = jnp.concatenate(
        [jnp.where(first, mine, other), jnp.where(first, other, mine)], axis=1
    )
    if permutes:
        return tail_by_permutes(
            value_grad, turned[0], tenant_of, owner_of, counts, noise, sizes
        )
    return tail_by_collectives(value_grad, value_weight, tenant_of, owner_of, counts, noise)


def solution(mesh):
    return jax.shard_map(
        functools.partial(body, dict(mesh.shape)),
        mesh=mesh,
        in_specs=(
            P(("group", "dp"), "seq", "tensor"),
            P(("group", "dp"), "seq", "tensor"),
            P(("group", "dp"), "seq", "tensor"),
            P("dp", "tensor"),
            P("group"),
            P("group"),
            P("group"),
            P(("group", "dp"), "seq", None),
        ),
        out_specs=P(("group", "dp"), "seq", None),
        check_vma=False,
    )
```
